32 devices in a mesh: dp: 4 (over y, x), ctx: 2 (over core), tensor: 4 (over z).
Axes of the slice: x: 2, y: 2, z: 4, core: 2. Of those that a mesh axis runs over, the one named last changes fastest.
Arguments:
- tokens: bfloat16 [2, 4, 1024, 2048], P(None, 'dp', 'ctx'), may hold values from -6 to 6
- out_grad: bfloat16 [2, 4, 1024, 2048], P(None, 'dp', 'ctx'), may hold values from -6 to 6
- norm_gain: float32 [2048], P(('dp', 'ctx')), may hold values from 0.5 to 1.5
- in_weight: float32 [2048, 2, 4096], P(('dp', 'ctx'), None, 'tensor'), may hold values from -0.125 to 0.125
- xproj_weight: float32 [160, 4096], P(('dp', 'ctx'), 'tensor'), may hold values from -0.375 to 0.375
- step_weight: float32 [128, 4096], P(('dp', 'ctx'), 'tensor'), may hold values from -0.5 to 0.5
- outproj_weight: float32 [2048, 4096], P(('dp', 'ctx'), 'tensor'), may hold values from -0.09375 to 0.09375
- channel_table: float32 [23, 4096], P(None, 'tensor'), may hold values from -20 to 3
- gain_second: float32 [2048], P(('dp', 'ctx')), may hold values from 8192 to 67108864
- in_rows: float32 [2048], P(('dp', 'ctx')), may hold values from 8192 to 67108864
- in_cols: float32 [2, 4096], P(None, 'tensor'), may hold values from 8192 to 67108864
- xproj_rows: float32 [160], P(('dp', 'ctx')), may hold values from 8192 to 67108864
- xproj_cols: float32 [4096], P('tensor'), may hold values from 8192 to 67108864
- step_rows: float32 [128], P(('dp', 'ctx')), may hold values from 8192 to 67108864
- step_cols: float32 [4096], P('tensor'), may hold values from 8192 to 67108864
- out_rows: float32 [2048], P(('dp', 'ctx')), may hold values from 8192 to 67108864
- out_cols: float32 [4096], P('tensor'), may hold values from 8192 to 67108864
- table_second: float32 [23, 4096], P(None, 'tensor'), may hold values from 8192 to 67108864
Outputs:
- mixed: bfloat16 [2, 4, 1024, 2048], P(None, 'dp', 'ctx')
- token_grad: bfloat16 [2, 4, 1024, 2048], P(None, 'dp', 'ctx')
- gain_grad: float32 [2048], P(('dp', 'ctx'))
- in_grad: float32 [2048, 2, 4096], P(('dp', 'ctx'), None, 'tensor')
- xproj_grad: float32 [160, 4096], P(('dp', 'ctx'), 'tensor')
- step_grad: float32 [128, 4096], P(('dp', 'ctx'), 'tensor')
- outproj_grad: float32 [2048, 4096], P(('dp', 'ctx'), 'tensor')
- table_grad: float32 [23, 4096], P(None, 'tensor')
- new_gain: float32 [2048], P(('dp', 'ctx'))
- new_in: float32 [2048, 2, 4096], P(('dp', 'ctx'), None, 'tensor')
- new_xproj: float32 [160, 4096], P(('dp', 'ctx'), 'tensor')
- new_step: float32 [128, 4096], P(('dp', 'ctx'), 'tensor')
- new_outproj: float32 [2048, 4096], P(('dp', 'ctx'), 'tensor')
- new_table: float32 [23, 4096], P(None, 'tensor')
- new_gain_second: float32 [2048], P(('dp', 'ctx'))
- new_in_rows: float32 [2048], P(('dp', 'ctx'))
- new_in_cols: float32 [2, 4096], P(None, 'tensor')
- new_xproj_rows: float32 [160], P(('dp', 'ctx'))
- new_xproj_cols: float32 [4096], P('tensor')
- new_step_rows: float32 [128], P(('dp', 'ctx'))
- new_step_cols: float32 [4096], P('tensor')
- new_out_rows: float32 [2048], P(('dp', 'ctx'))
- new_out_cols: float32 [4096], P('tensor')
- new_table_second: float32 [23, 4096], P(None, 'tensor')
- update_rms: float32 [6], replicated
The draws below stay inside these ranges and needn't reach their ends.
All inputs are finite; a program needn't handle non-finite values.
Results may differ from the reference program's by a relative error of at most 0.018.
The reference program's roundings to bfloat16 on the way count: a program that leaves them out, or rounds other values in their place, can miss the bound.
Values may be sent and summed in bfloat16 or wider, within the bound.
No kernel may reach another device: no remote copies, remote signals or barrier semaphores. Data moves between devices by JAX's collectives and lax.ppermute only.
A program may use at most 768 MiB of HBM per device.

```python
import math
import jax
import jax.numpy as jnp
from jax import lax

D = 2048
E = 4096
N = 16
R = 128
K = 4
MICRO = 2
SEQS = 4
SEQLEN = 1024


def draw_channel_table(key, part):
    keys = jax.random.split(key, 5)
    taps = 0.5 * jax.random.truncated_normal(keys[0], -4.0, 4.0, (K, E), jnp.float32)
    conv_bias = 0.5 * jax.random.truncated_normal(keys[1], -4.0, 4.0, (1, E), jnp.float32)
    low_end = math.log(0.05 / SEQLEN)
    high_end = math.log(0.1)
    base_size = jnp.exp(jax.random.uniform(keys[2], (1, E), jnp.float32, low_end, high_end))
    step_bias = base_size + jnp.log(-jnp.expm1(-base_size))
    skip = jax.random.uniform(keys[3], (1, E), jnp.float32, 0.5, 1.5)
    a_log = jax.random.uniform(keys[4], (N, E), jnp.float32, 0.0, math.log(16.0))
    return jnp.concatenate([taps, conv_bias, step_bias, skip, a_log], axis=0)


def block_scale(stream_key, shape, shards, least, largest):
    loudness = 1.0
    for axis_at, blocks in shards:
        draws = jax.random.uniform(jax.random.fold_in(jax.random.fold_in(stream_key, 6), axis_at), (blocks,), jnp.float32, least / len(shards), largest / len(shards))
        loudness = loudness * jnp.repeat(jnp.exp(draws), shape[axis_at] // blocks).reshape((-1,) + (1,) * (len(shape) - 1 - axis_at))
    return loudness


def scatter_about(key, extent, spread, most, cuts=(), kind=jnp.bfloat16):
    entries = spread * jax.random.normal(key, extent, jnp.float32)
    if cuts:
        entries = entries * block_scale(key, extent, cuts, -0.22, 0.18)
    return jnp.clip(entries, -most, most).astype(kind)


def setup_inputs(seed: int = 0) -> dict:
    arg_keys = jax.random.split(jax.random.key(seed), 19)
    return {
        "tokens": scatter_about(arg_keys[0], (MICRO, SEQS, SEQLEN, D), 1.0, 6.0, ((1, 4), (2, 2))),
        "out_grad": scatter_about(arg_keys[1], (MICRO, SEQS, SEQLEN, D), 1.0, 6.0, ((1, 4), (2, 2))),
        "norm_gain": jnp.clip(1.0 + 0.1 * jax.random.normal(arg_keys[2], (D,), jnp.float32), 0.5, 1.5),
        "in_weight": scatter_about(arg_keys[3], (D, 2, E), D ** -0.5, 0.125, ((0, 8), (2, 4)), jnp.float32),
        "xproj_weight": scatter_about(arg_keys[4], (R + 2 * N, E), (E // 16) ** -0.5, 0.375, ((0, 8), (1, 4)), jnp.float32),
        "step_weight": scatter_about(arg_keys[5], (R, E), R ** -0.5, 0.5, ((0, 8), (1, 4)), jnp.float32),
        "outproj_weight": scatter_about(arg_keys[6], (D, E), E ** -0.5, 0.09375, ((0, 8), (1, 4)), jnp.float32),
        "channel_table": draw_channel_table(jax.random.fold_in(arg_keys[18], 71), 0),
        "gain_second": jnp.clip(jnp.exp(math.log(67108864) - 9.010913 * jax.random.uniform(arg_keys[8], (D,), jnp.float32) ** block_scale(arg_keys[8], (D,), ((0, 8),), -0.2, 0.2)), 8192.0, 67108864),
        "in_rows": jnp.clip(jnp.exp(math.log(67108864) - 9.010913 * jax.random.uniform(arg_keys[9], (D,), jnp.float32) ** block_scale(arg_keys[9], (D,), ((0, 8),), -0.2, 0.2)), 8192.0, 67108864),
        "in_cols": jnp.clip(jnp.exp(math.log(67108864) - 9.010913 * jax.random.uniform(arg_keys[10], (2, E), jnp.float32) ** block_scale(arg_keys[10], (2, E), ((1, 4),), -0.2, 0.2)), 8192.0, 67108864),
        "xproj_rows": jnp.clip(jnp.exp(math.log(67108864) - 9.010913 * jax.random.uniform(arg_keys[11], (R + 2 * N,), jnp.float32) ** block_scale(arg_keys[11], (R + 2 * N,), ((0, 8),), -0.2, 0.2)), 8192.0, 67108864),
        "xproj_cols": jnp.clip(jnp.exp(math.log(67108864) - 9.010913 * jax.random.uniform(arg_keys[12], (E,), jnp.float32) ** block_scale(arg_keys[12], (E,), ((0, 4),), -0.2, 0.2)), 8192.0, 67108864),
        "step_rows": jnp.clip(jnp.exp(math.log(67108864) - 9.010913 * jax.random.uniform(arg_keys[13], (R,), jnp.float32) ** block_scale(arg_keys[13], (R,), ((0, 8),), -0.2, 0.2)), 8192.0, 67108864),
        "step_cols": jnp.clip(jnp.exp(math.log(67108864) - 9.010913 * jax.random.uniform(arg_keys[14], (E,), jnp.float32) ** block_scale(arg_keys[14], (E,), ((0, 4),), -0.2, 0.2)), 8192.0, 67108864),
        "out_rows": jnp.clip(jnp.exp(math.log(67108864) - 9.010913 * jax.random.uniform(arg_keys[15], (D,), jnp.float32) ** block_scale(arg_keys[15], (D,), ((0, 8),), -0.2, 0.2)), 8192.0, 67108864),
        "out_cols": jnp.clip(jnp.exp(math.log(67108864) - 9.010913 * jax.random.uniform(arg_keys[16], (E,), jnp.float32) ** block_scale(arg_keys[16], (E,), ((0, 4),), -0.2, 0.2)), 8192.0, 67108864),
        "table_second": jnp.clip(jnp.exp(math.log(67108864) - 9.010913 * jax.random.uniform(arg_keys[17], (K + 3 + N, E), jnp.float32) ** block_scale(arg_keys[17], (K + 3 + N, E), ((1, 4),), -0.2, 0.2)), 8192.0, 67108864),
    }


norm_epsilon = 1e-05
square_floor = 1e-30
decay_rate = 0.5
clip_limit = 0.5
step_rate = 1.0
precision_highest_mode = lax.Precision.HIGHEST

@jax.custom_vjp
def low_precision(v):
    return lax.optimization_barrier(v.astype(jnp.bfloat16)).astype(jnp.float32)

@jax.custom_vjp
def low_precision_back(v):
    return v

def low_keep(v):
    return (low_precision(v), None)

def low_pass(kept, grad):
    return (grad,)

def back_keep(v):
    return (v, None)

def back_low(kept, grad):
    return (low_precision(grad),)
low_precision.defvjp(low_keep, low_pass)
low_precision_back.defvjp(back_keep, back_low)

def selective_scan(step_size, values, b_coef, c_coef, a_neg):
    seqs, length, inner = step_size.shape
    rows = math.gcd(length, 64)
    count = length // rows

    def arrange(value):
        return jnp.transpose(value.reshape(seqs, count, rows, value.shape[-1]), (1, 2, 0, 3))

    def token_step(state, item):
        size_t, value_t, b_t, c_t = item
        state = jnp.exp(size_t[:, None, :] * a_neg[None]) * state + (size_t * value_t)[:, None, :] * b_t[:, :, None]
        return (state, lax.optimization_barrier(jnp.sum(c_t[:, :, None] * state, axis=1)))

    def block_plain(state, item):
        return lax.scan(token_step, state, item)
    block_step = jax.checkpoint(block_plain)
    start = jnp.zeros((seqs,) + a_neg.shape, jnp.float32)
    final, outs = lax.scan(block_step, start, (arrange(step_size), arrange(values), arrange(b_coef), arrange(c_coef)))
    return jnp.transpose(outs, (2, 0, 1, 3)).reshape(seqs, length, inner)

def forward(input_value, gain, input_weight, w_x, w_dt, output_weight, table):
    inverse = lax.rsqrt(lax.optimization_barrier(jnp.mean(input_value * input_value, axis=-1, keepdims=True)) + norm_epsilon)
    normalized_rows = low_precision(input_value * inverse * low_precision(gain))
    mixer_input = low_precision(low_precision_back(jnp.einsum('xub,bzt->xuzt', normalized_rows, low_precision(input_weight), precision=precision_highest_mode)))
    conv_in = mixer_input[:, :, 0]
    gate_in = mixer_input[:, :, 1]
    padded = jnp.pad(conv_in, ((0, 0), (K - 1, 0), (0, 0)))
    conv = table[K] + table[0] * padded[:, 0:SEQLEN]
    for k in range(1, K):
        conv = conv + table[k] * padded[:, k:k + SEQLEN]
    values = low_precision(jax.nn.silu(conv))
    proj = low_precision_back(jnp.einsum('sle,pe->slp', values, low_precision(w_x), precision=precision_highest_mode))
    rank_in = low_precision(proj[..., :R])
    b_coef = proj[..., R:R + N]
    c_coef = proj[..., R + N:]
    pre = low_precision_back(jnp.einsum('slr,re->sle', rank_in, low_precision(w_dt), precision=precision_highest_mode)) + table[K + 1]
    step_size = jax.nn.softplus(pre)
    a_neg = -jnp.exp(table[K + 3:])
    scan_out = selective_scan(step_size, values, b_coef, c_coef, a_neg) + table[K + 2] * values
    gated_output = low_precision(scan_out * jax.nn.silu(gate_in))
    return input_value + jnp.einsum('ikr,or->iko', gated_output, low_precision(output_weight), precision=precision_highest_mode)

def factored(grad, rows, cols):
    square = grad * grad + square_floor
    row_new = decay_rate * rows + (1.0 - decay_rate) * lax.optimization_barrier(jnp.mean(square.reshape(square.shape[0], -1), axis=1))
    col_new = decay_rate * cols + (1.0 - decay_rate) * lax.optimization_barrier(jnp.mean(square, axis=0))
    shape = (-1,) + (1,) * (grad.ndim - 1)
    second = row_new.reshape(shape) * col_new[None] / jnp.mean(row_new)
    return (grad * lax.rsqrt(second), row_new, col_new)

def unfactored(grad, second):
    second_new = decay_rate * second + (1.0 - decay_rate) * (grad * grad + square_floor)
    return (grad * lax.rsqrt(second_new), second_new)

def apply_update(weight_matrix, update):
    rms_value = jnp.sqrt(jnp.mean(update * update))
    factor = jnp.maximum(1.0, rms_value / clip_limit)
    scale = jnp.sqrt(jnp.mean(weight_matrix * weight_matrix))
    return (weight_matrix - step_rate * scale / factor * update, rms_value)

def reference(tokens, out_grad, norm_gain, in_weight, xproj_weight, step_weight, outproj_weight, channel_table, gain_second, in_rows, in_cols, xproj_rows, xproj_cols, step_rows, step_cols, out_rows, out_cols, table_second):
    weights = (norm_gain, in_weight, xproj_weight, step_weight, outproj_weight, channel_table)
    totals = [jnp.zeros(w.shape, jnp.float32) for w in weights]
    mixed_list = []
    grad_list = []
    for m in range(MICRO):
        input_value = tokens[m].astype(jnp.float32)
        result, pull = jax.vjp(forward, input_value, norm_gain, in_weight, xproj_weight, step_weight, outproj_weight, channel_table)
        grads = pull(out_grad[m].astype(jnp.float32))
        mixed_list.append(result.astype(jnp.bfloat16))
        grad_list.append(grads[0].astype(jnp.bfloat16))
        totals = [totals[i] + grads[i + 1] for i in range(6)]
    gain_grad, in_grad, xproj_grad, step_grad, outproj_grad, table_grad = totals
    gain_update, new_gain_second = unfactored(gain_grad, gain_second)
    in_update, new_in_rows, new_in_cols = factored(in_grad, in_rows, in_cols)
    xproj_update, new_xproj_rows, new_xproj_cols = factored(xproj_grad, xproj_rows, xproj_cols)
    step_update, new_step_rows, new_step_cols = factored(step_grad, step_rows, step_cols)
    out_update, new_out_rows, new_out_cols = factored(outproj_grad, out_rows, out_cols)
    table_update, new_table_second = unfactored(table_grad, table_second)
    updates = (gain_update, in_update, xproj_update, step_update, out_update, table_update)
    news = [apply_update(weights[i], updates[i]) for i in range(6)]
    update_rms = jnp.stack([item[1] for item in news])
    return (jnp.stack(mixed_list), jnp.stack(grad_list), gain_grad, in_grad, xproj_grad, step_grad, outproj_grad, table_grad, news[0][0], news[1][0], news[2][0], news[3][0], news[4][0], news[5][0], new_gain_second, new_in_rows, new_in_cols, new_xproj_rows, new_xproj_cols, new_step_rows, new_step_cols, new_out_rows, new_out_cols, new_table_second, update_rms)
```

```python
import functools
import math

import jax
import jax.numpy as jnp
from jax import lax
from jax.experimental import pallas as pl
from jax.experimental.pallas import tpu as pltpu
from jax.sharding import PartitionSpec as P

D = 2048
E = 4096
N = 16
R = 128
K = 4
LANES = 128
LOG_2 = math.log(2.0)
LOW = jnp.bfloat16
FULL = jnp.float32

norm_epsilon = 1e-05
square_floor = 1e-30
decay_rate = 0.5
clip_limit = 0.5
step_rate = 1.0


def bits(axis):
    size = lax.axis_size(axis)
    return [1 << b for b in range(size.bit_length() - 1)]


def swap(block, axis, bit):
    return lax.ppermute(block, axis, [(i, i ^ bit) for i in range(lax.axis_size(axis))])


def shifted(block, axis, distance):
    devices = range(lax.axis_size(axis))
    route = [(i - distance, i) for i in devices if i - distance in devices]
    return lax.ppermute(block, axis, route)


def butterfly(value, axes):
    for axis in axes:
        for bit in bits(axis):
            value = value + swap(value, axis, bit)
    return value


def relative_blocks():
    n_dp, n_ctx = lax.axis_size("dp"), lax.axis_size("ctx")
    dp, ctx = lax.axis_index("dp"), lax.axis_index("ctx")
    return [
        (dp ^ (q % n_dp)) * n_ctx + (ctx ^ (q // n_dp)) for q in range(n_dp * n_ctx)
    ], [
        (ctx ^ (j % n_ctx)) * n_dp + (dp ^ (j // n_ctx)) for j in range(n_dp * n_ctx)
    ]


def pick(blocks, order):
    return jnp.stack([lax.dynamic_index_in_dim(blocks, q, 0, False) for q in order])


def pick_columns(rows, order):
    width = rows.shape[1] // len(order)
    return jnp.concatenate(
        [lax.dynamic_slice_in_dim(rows, q * width, width, 1) for q in order], axis=1
    )


def gather(own):
    if lax.axis_size("dp") == 4:
        half = own.shape[0] // 2
        one = swap(own, "dp", 1)
        two = swap(own, "dp", 2)
        three = [swap(two[:half], "dp", 1), swap(one[half:], "dp", 2)]
        whole = jnp.concatenate([own, one, two] + three, axis=0)
    else:
        whole = own
        for bit in bits("dp"):
            whole = jnp.concatenate([whole, swap(whole, "dp", bit)], axis=0)
    for bit in bits("ctx"):
        whole = jnp.concatenate([whole, swap(whole, "ctx", bit)], axis=0)
    return whole


def scatter(parts):
    for bit in reversed(bits("ctx")):
        half = parts.shape[0] // 2
        parts = (
            parts[:half].astype(FULL) + swap(parts[half:], "ctx", bit).astype(FULL)
        ).astype(LOW)
    if lax.axis_size("dp") == 4:
        half = parts.shape[2] // 2
        left, right = parts[:, :, :half], parts[:, :, half:]
        got_left = swap(jnp.stack([left[1], left[3]]), "dp", 1).astype(FULL)
        got_right = swap(right[2:], "dp", 2).astype(FULL)
        far_left = (left[2].astype(FULL) + got_left[1]).astype(LOW)
        far_right = (right[1].astype(FULL) + got_right[1]).astype(LOW)
        end_left = swap(far_left, "dp", 2).astype(FULL)
        end_right = swap(far_right, "dp", 1).astype(FULL)
        return jnp.concatenate(
            [
                left[0].astype(FULL) + got_left[0] + end_left,
                right[0].astype(FULL) + got_right[0] + end_right,
            ],
            axis=1,
        )
    for bit in reversed(bits("dp")):
        half = parts.shape[0] // 2
        parts = parts[:half].astype(FULL) + swap(parts[half:].astype(LOW), "dp", bit).astype(FULL)
    return parts[0].astype(FULL)


def line_scatter(parts):
    n = lax.axis_size("tensor")
    me = lax.axis_index("tensor")

    def part(index):
        return lax.dynamic_index_in_dim(parts, jnp.clip(index, 0, n - 1), 0, False)

    total = part(me).astype(FULL)
    up = down = None
    for s in range(1, n):
        send_up, send_down = part(n - s + me), part(s - n + me)
        if up is not None:
            send_up = (send_up.astype(FULL) + up.astype(FULL)).astype(LOW)
            send_down = (send_down.astype(FULL) + down.astype(FULL)).astype(LOW)
        up = lax.ppermute(send_up, "tensor", [(i, i + 1) for i in range(s)])
        down = lax.ppermute(send_down, "tensor", [(i, i - 1) for i in range(n - s, n)])
    if up is not None:
        total = total + up.astype(FULL) + down.astype(FULL)
    return total


def line_gather(own):
    n = lax.axis_size("tensor")
    me = lax.axis_index("tensor")
    ups, downs = [own], [own]
    for s in range(1, n):
        ups.append(lax.ppermute(ups[-1], "tensor", [(i, i + 1) for i in range(s - 1, n - 1)]))
        downs.append(lax.ppermute(downs[-1], "tensor", [(i, i - 1) for i in range(1, n - s + 1)]))
    whole = jnp.zeros((n,) + own.shape, own.dtype)
    whole = lax.dynamic_update_index_in_dim(whole, own, me, 0)
    for s in range(1, n):
        value = jnp.where(me >= s, ups[s], downs[n - s])
        whole = lax.dynamic_update_index_in_dim(whole, value, lax.rem(me - s + n, n), 0)
    return whole


def tensor_total(term):
    for bit in bits("tensor"):
        low = term.astype(LOW)
        term = low.astype(FULL) + swap(low, "tensor", bit).astype(FULL)
    return term


def spread(target, columns, place, rows, tile):
    target[pl.ds(place, rows, stride=tile), :] = columns


def splat(target, table, first, rows):
    for n in range(N):
        target[pl.ds(n, rows, stride=N), :] = jnp.broadcast_to(
            table[:, first + n : first + n + 1], (rows, LANES)
        )


def columns_of(j):
    return slice(j * LANES, (j + 1) * LANES)


def edge_kernel(
    rows, groups, tile, unroll, flag, size_ref, value_ref, grad_ref, gate_ref, coef_ref, rate_ref,
    edge_ref, size_s, term_s, coef_s,
):
    backward = flag[0] == 1

    @pl.when(pl.program_id(1) == 0)
    def _():
        edge_ref[...] = jnp.zeros_like(edge_ref)

    for j in range(tile):
        if j < groups:
            spread(size_s, size_ref[:, columns_of(j)], j, rows, tile)
        else:
            spread(size_s, jnp.zeros((rows, LANES), FULL), j, rows, tile)
            spread(term_s, jnp.zeros((rows, LANES), FULL), j, rows, tile)

    def loop(body):
        first = tuple(edge_ref[n] for n in range(N))
        last = lax.fori_loop(0, rows, body, first, unroll=unroll)
        for n in range(N):
            edge_ref[n] = last[n]

    @pl.when(jnp.logical_not(backward))
    def _():
        for j in range(groups):
            cut = columns_of(j)
            spread(term_s, size_ref[:, cut] * value_ref[:, cut].astype(FULL), j, rows, tile)
        splat(coef_s, coef_ref, 0, rows)

        def body(t, state):
            place = pl.ds(pl.multiple_of(t * tile, tile), tile)
            size, term = size_s[place, :], term_s[place, :]
            return tuple(
                jnp.exp2(size * rate_ref[n]) * state[n] + term * coef_s[pl.ds(t * N + n, 1), :]
                for n in range(N)
            )

        loop(body)

    @pl.when(backward)
    def _():
        for j in range(groups):
            cut = columns_of(j)
            gate = gate_ref[:, cut].astype(FULL)
            spread(term_s, grad_ref[:, cut] * gate * jax.nn.sigmoid(gate), j, rows, tile)
        splat(coef_s, coef_ref, N, rows)

        def body(step, state):
            t = rows - 1 - step
            place = pl.ds(pl.multiple_of(t * tile, tile), tile)
            size, term = size_s[place, :], term_s[place, :]
            return tuple(
                jnp.exp2(size * rate_ref[n])
                * (state[n] + term * coef_s[pl.ds(t * N + n, 1), :])
                for n in range(N)
            )

        loop(body)


def forward_kernel(
    rows, groups, tile, part, unroll,
    size_ref, value_ref, grad_ref, gate_ref, coef_ref, rate_ref, start_ref, skip_ref, pick_ref,
    gated_ref, gate_grad_ref, before_ref, grad_c_ref, grad_skip_ref,
    size_s, input_s, grad_s, out_s, b_s, c_s, product_s, state_s,
):
    @pl.when(pl.program_id(1) == 0)
    def _():
        state_s[...] = start_ref[...]
        grad_skip_ref[...] = jnp.zeros_like(grad_skip_ref)

    blank = jnp.zeros((rows, LANES), FULL)
    for j in range(tile):
        if j < groups:
            cut = columns_of(j)
            size = size_ref[:, cut]
            value = value_ref[:, cut].astype(FULL)
            gate = gate_ref[:, cut].astype(FULL)
            scan_grad = grad_ref[:, cut] * gate * jax.nn.sigmoid(gate)
            spread(size_s, size, j, rows, tile)
            spread(input_s, size * value, j, rows, tile)
            spread(grad_s, scan_grad, j, rows, tile)
            grad_skip_ref[:, cut] += jnp.sum(scan_grad * value, axis=0, keepdims=True)
        else:
            for target in (size_s, input_s, grad_s):
                spread(target, blank, j, rows, tile)
    splat(b_s, coef_ref, 0, rows)
    splat(c_s, coef_ref, N, rows)
    for low in range(0, N, part):
        rate = [rate_ref[n] for n in range(low, low + part)]

        def body(t, state):
            state = list(state)
            place = pl.ds(pl.multiple_of(t * tile, tile), tile)
            size, term, grad = size_s[place, :], input_s[place, :], grad_s[place, :]
            out = None
            for k in range(part):
                n = low + k
                before_ref[t, n] = state[k]
                state[k] = (
                    jnp.exp2(size * rate[k]) * state[k] + term * b_s[pl.ds(t * N + n, 1), :]
                )
                read = c_s[pl.ds(t * N + n, 1), :] * state[k]
                out = read if out is None else out + read
                product_s[place, columns_of(n)] = state[k] * grad
            if low == 0:
                out_s[place, :] = out
            else:
                out_s[place, :] = out_s[place, :] + out
            return tuple(state)

        first = tuple(state_s[n] for n in range(low, low + part))
        last = lax.fori_loop(0, rows, body, first, unroll=unroll)
        for k in range(part):
            state_s[low + k] = last[k]
    for j in range(groups):
        cut = columns_of(j)
        scan_out = out_s[pl.ds(j, rows, stride=tile), :] + skip_ref[:, cut] * value_ref[
            :, cut
        ].astype(FULL)
        gate = gate_ref[:, cut].astype(FULL)
        sigma = jax.nn.sigmoid(gate)
        gated_ref[:, cut] = (scan_out * (gate * sigma)).astype(LOW)
        slope = sigma * (1.0 + gate * (1.0 - sigma))
        gate_grad_ref[:, cut] = (grad_ref[:, cut] * scan_out * slope).astype(LOW)
    sums = jnp.dot(product_s[...].astype(LOW), pick_ref[...], preferred_element_type=FULL)
    grad_c_ref[...] = jnp.sum(sums.reshape(rows, tile, LANES), axis=1)


def backward_kernel(
    rows, groups, tile, part, unroll,
    size_ref, value_ref, grad_ref, gate_ref, coef_ref, rate_ref, tail_ref, skip_ref, pick_ref,
    before_ref,
    pre_low_ref, grad_value_ref, grad_b_ref, grad_rate_ref, grad_bias_ref,
    size_s, input_s, grad_s, along_s, rated_s, b_s, c_s, product_s, state_s,
):
    @pl.when(pl.program_id(1) == 0)
    def _():
        state_s[...] = tail_ref[...]
        grad_rate_ref[...] = jnp.zeros_like(grad_rate_ref)
        grad_bias_ref[...] = jnp.zeros_like(grad_bias_ref)

    blank = jnp.zeros((rows, LANES), FULL)
    for j in range(tile):
        if j < groups:
            cut = columns_of(j)
            size = size_ref[:, cut]
            gate = gate_ref[:, cut].astype(FULL)
            spread(size_s, size, j, rows, tile)
            spread(input_s, size * value_ref[:, cut].astype(FULL), j, rows, tile)
            spread(grad_s, grad_ref[:, cut] * gate * jax.nn.sigmoid(gate), j, rows, tile)
        else:
            for target in (size_s, input_s, grad_s):
                spread(target, blank, j, rows, tile)
    splat(b_s, coef_ref, 0, rows)
    splat(c_s, coef_ref, N, rows)
    for low in range(0, N, part):
        rate = [rate_ref[n] for n in range(low, low + part)]

        def body(step, carry):
            state, total = list(carry[0]), list(carry[1])
            t = rows - 1 - step
            place = pl.ds(pl.multiple_of(t * tile, tile), tile)
            size, term, grad = size_s[place, :], input_s[place, :], grad_s[place, :]
            along = rated = None
            for k in range(part):
                n = low + k
                adjoint = c_s[pl.ds(t * N + n, 1), :] * grad + state[k]
                state[k] = jnp.exp2(size * rate[k]) * adjoint
                through = state[k] * before_ref[t, n]
                first = adjoint * b_s[pl.ds(t * N + n, 1), :]
                second = through * rate[k]
                along = first if along is None else along + first
                rated = second if rated is None else rated + second
                total[k] = total[k] + through * size
                product_s[place, columns_of(n)] = adjoint * term
            if low == 0:
                along_s[place, :] = along
                rated_s[place, :] = rated
            else:
                along_s[place, :] = along_s[place, :] + along
                rated_s[place, :] = rated_s[place, :] + rated
            return tuple(state), tuple(total)

        place = range(low, low + part)
        first = (tuple(state_s[n] for n in place), tuple(grad_rate_ref[n] for n in place))
        state, total = lax.fori_loop(0, rows, body, first, unroll=unroll)
        for k in range(part):
            state_s[low + k] = state[k]
            grad_rate_ref[low + k] = total[k]
    for j in range(groups):
        cut = columns_of(j)
        size = size_ref[:, cut]
        along = along_s[pl.ds(j, rows, stride=tile), :]
        rated = rated_s[pl.ds(j, rows, stride=tile), :]
        grad_size = along * value_ref[:, cut].astype(FULL) + LOG_2 * rated
        grad_pre = grad_size * (jnp.tanh(0.5 * size) * (1.0 + jnp.exp(-size)))
        pre_low_ref[:, cut] = grad_pre.astype(LOW)
        grad_bias_ref[:, cut] += jnp.sum(grad_pre, axis=0, keepdims=True)
        scan_grad = grad_s[pl.ds(j, rows, stride=tile), :]
        grad_value_ref[:, cut] = along * size + skip_ref[:, cut] * scan_grad
    sums = jnp.dot(product_s[...].astype(LOW), pick_ref[...], preferred_element_type=FULL)
    grad_b_ref[...] = jnp.sum(sums.reshape(rows, tile, LANES), axis=1)


def picker():
    shape = (N * LANES, LANES)
    state = lax.broadcasted_iota(jnp.int32, shape, 0) // LANES
    return (state == lax.broadcasted_iota(jnp.int32, shape, 1)).astype(LOW)


def tiles(channels):
    groups = channels // LANES
    return groups, 8 * pl.cdiv(groups, 8)


def tiled(table):
    groups, tile = tiles(table.shape[-1])
    table = table.reshape(table.shape[:-1] + (groups, LANES))
    pads = [(0, 0)] * (table.ndim - 2) + [(0, tile - groups), (0, 0)]
    return jnp.pad(table, pads)


def flat(table, channels):
    groups, _ = tiles(channels)
    return table[..., :groups, :].reshape(table.shape[:-2] + (channels,))


def cost(micro, length, ops, size):
    work = micro * length * N * 1024 * ops * 100
    return pl.CostEstimate(flops=work, bytes_accessed=size, transcendentals=0)


def limits():
    return pltpu.CompilerParams(vmem_limit_bytes=56 * 1024 * 1024)


def scan_edge(flag, size, value, grad, gate, coef, rate):
    micro, length, channels = size.shape
    groups, tile = tiles(channels)
    rows = min(64, length)
    count = length // rows

    def place(m, i, f):
        return (m, jnp.where(f[0] == 0, i, count - 1 - i), 0)

    wide = pl.BlockSpec((None, rows, channels), place)
    return pl.pallas_call(
        functools.partial(edge_kernel, rows, groups, tile, 4),
        grid_spec=pltpu.PrefetchScalarGridSpec(
            num_scalar_prefetch=1,
            grid=(micro, count),
            in_specs=[wide] * 4
            + [
                pl.BlockSpec((None, rows, 2 * N), place),
                pl.BlockSpec((N, tile, LANES), lambda m, i, f: (0, 0, 0)),
            ],
            out_specs=pl.BlockSpec((None, N, tile, LANES), lambda m, i, f: (m, 0, 0, 0)),
            scratch_shapes=[pltpu.VMEM((rows * tile, LANES), FULL)] * 2
            + [pltpu.VMEM((rows * N, LANES), FULL)],
        ),
        out_shape=jax.ShapeDtypeStruct((micro, N, tile, LANES), FULL),
        compiler_params=limits(),
        cost_estimate=cost(micro, length, 8, size.size * 12),
        name="scan_edge",
    )(flag, size, value, grad, gate, coef, rate)


def scan_forward(size, value, grad, gate, coef, rate, start, skip):
    micro, length, channels = size.shape
    groups, tile = tiles(channels)
    rows = min(64, length)
    wide = pl.BlockSpec((None, rows, channels), lambda m, i: (m, i, 0))
    row = pl.BlockSpec((1, channels), lambda m, i: (0, 0))
    return pl.pallas_call(
        functools.partial(forward_kernel, rows, groups, tile, 8, 4),
        grid=(micro, length // rows),
        in_specs=[wide] * 4
        + [
            pl.BlockSpec((None, rows, 2 * N), lambda m, i: (m, i, 0)),
            pl.BlockSpec((N, tile, LANES), lambda m, i: (0, 0, 0)),
            pl.BlockSpec((None, N, tile, LANES), lambda m, i: (m, 0, 0, 0)),
            row,
            pl.BlockSpec((N * LANES, LANES), lambda m, i: (0, 0)),
        ],
        out_specs=[
            wide,
            wide,
            pl.BlockSpec((None, rows, N, tile, LANES), lambda m, i: (m, i, 0, 0, 0)),
            pl.BlockSpec((None, rows, LANES), lambda m, i: (m, i, 0)),
            pl.BlockSpec((None, 1, channels), lambda m, i: (m, 0, 0)),
        ],
        out_shape=[
            jax.ShapeDtypeStruct(size.shape, LOW),
            jax.ShapeDtypeStruct(size.shape, LOW),
            jax.ShapeDtypeStruct((micro, length, N, tile, LANES), FULL),
            jax.ShapeDtypeStruct((micro, length, LANES), FULL),
            jax.ShapeDtypeStruct((micro, 1, channels), FULL),
        ],
        scratch_shapes=[pltpu.VMEM((rows * tile, LANES), FULL)] * 4
        + [pltpu.VMEM((rows * N, LANES), FULL)] * 2
        + [pltpu.VMEM((rows * tile, N * LANES), FULL), pltpu.VMEM((N, tile, LANES), FULL)],
        compiler_params=limits(),
        cost_estimate=cost(micro, length, 15, size.size * 80),
        name="scan_forward",
    )(size, value, grad, gate, coef, rate, start, skip, picker())


def scan_backward(size, value, grad, gate, coef, rate, tail, skip, before):
    micro, length, channels = size.shape
    groups, tile = tiles(channels)
    rows = min(64, length)
    last = length // rows - 1
    wide = pl.BlockSpec((None, rows, channels), lambda m, i: (m, last - i, 0))
    row = pl.BlockSpec((1, channels), lambda m, i: (0, 0))
    return pl.pallas_call(
        functools.partial(backward_kernel, rows, groups, tile, 8, 4),
        grid=(micro, length // rows),
        in_specs=[wide] * 4
        + [
            pl.BlockSpec((None, rows, 2 * N), lambda m, i: (m, last - i, 0)),
            pl.BlockSpec((N, tile, LANES), lambda m, i: (0, 0, 0)),
            pl.BlockSpec((None, N, tile, LANES), lambda m, i: (m, 0, 0, 0)),
            row,
            pl.BlockSpec((N * LANES, LANES), lambda m, i: (0, 0)),
            pl.BlockSpec((None, rows, N, tile, LANES), lambda m, i: (m, last - i, 0, 0, 0)),
        ],
        out_specs=[
            wide,
            wide,
            pl.BlockSpec((None, rows, LANES), lambda m, i: (m, last - i, 0)),
            pl.BlockSpec((None, N, tile, LANES), lambda m, i: (m, 0, 0, 0)),
            pl.BlockSpec((None, 1, channels), lambda m, i: (m, 0, 0)),
        ],
        out_shape=[
            jax.ShapeDtypeStruct(size.shape, LOW),
            jax.ShapeDtypeStruct(size.shape, FULL),
            jax.ShapeDtypeStruct((micro, length, LANES), FULL),
            jax.ShapeDtypeStruct((micro, N, tile, LANES), FULL),
            jax.ShapeDtypeStruct((micro, 1, channels), FULL),
        ],
        scratch_shapes=[pltpu.VMEM((rows * tile, LANES), FULL)] * 5
        + [pltpu.VMEM((rows * N, LANES), FULL)] * 2
        + [pltpu.VMEM((rows * tile, N * LANES), FULL), pltpu.VMEM((N, tile, LANES), FULL)],
        compiler_params=limits(),
        cost_estimate=cost(micro, length, 20, size.size * 80),
        name="scan_backward",
    )(size, value, grad, gate, coef, rate, tail, skip, picker(), before)


def edges(size, value, grad, gate, coef, rate):
    count, place = lax.axis_size("ctx"), lax.axis_index("ctx")
    args = (size, value, grad, gate, coef, rate)
    if count == 2:
        edge = scan_edge(place.astype(jnp.int32)[None], *args)
        other = swap(edge, "ctx", 1)
        return jnp.where(place == 1, other, 0.0), jnp.where(place == 0, other, 0.0)
    last = scan_edge(jnp.zeros((1,), jnp.int32), *args)
    head = scan_edge(jnp.ones((1,), jnp.int32), *args)
    through = jnp.exp2(rate[None] * tiled(jnp.sum(size, axis=1))[:, None])
    lasts, heads, throughs = (lax.all_gather(a, "ctx") for a in (last, head, through))
    start = tail = jnp.zeros(last.shape, FULL)
    for i in range(count):
        start = jnp.where(i < place, throughs[i] * start + lasts[i], start)
        j = count - 1 - i
        tail = jnp.where(j > place, throughs[j] * tail + heads[j], tail)
    return start, tail


def silu_slope(value):
    sigma = jax.nn.sigmoid(value)
    return sigma * (1.0 + value * (1.0 - sigma))


def dot(a, b, dims, kind=FULL):
    return lax.dot_general(a, b, (dims, ((), ())), preferred_element_type=FULL).astype(kind)


def per_device(
    tokens,
    out_grad,
    norm_gain,
    in_weight,
    xproj_weight,
    step_weight,
    outproj_weight,
    channel_table,
    gain_second,
    in_rows,
    in_cols,
    xproj_rows,
    xproj_cols,
    step_rows,
    step_cols,
    out_rows,
    out_cols,
    table_second,
):
    micro = tokens.shape[0]
    length = tokens.shape[2]
    inner = in_weight.shape[2]
    n_tensor = lax.axis_size("tensor")
    n_owner = lax.axis_size("dp") * lax.axis_size("ctx")
    owned = in_weight.shape[0]
    order, inverse_order = relative_blocks()
    share = length // n_tensor
    first_row = lax.axis_index("tensor") * share
    own_axes = ("ctx", "dp")

    pad_gain = jnp.pad(norm_gain.astype(LOW), (0, inner - owned))[None]
    n_x, n_s = xproj_weight.shape[0], step_weight.shape[0]
    small = jnp.concatenate([xproj_weight.astype(LOW), step_weight.astype(LOW), pad_gain], axis=0)
    pad_rows = -small.shape[0] % 32
    small = gather(jnp.pad(small, ((0, pad_rows), (0, 0)))).reshape(n_owner, -1, inner)
    conv_low = gather(in_weight[:, 0].astype(LOW))
    gate_low = gather(in_weight[:, 1].astype(LOW))
    out_low = gather(outproj_weight.astype(LOW))
    gain_low = small[:, n_x + n_s, :owned].reshape(D).astype(FULL)
    small = pick(small, inverse_order)
    xproj_low = small[:, :n_x].reshape(n_owner * n_x, inner)
    step_low = small[:, n_x : n_x + n_s].reshape(n_owner * n_s, inner)
    gain_value = pick(gain_low.reshape(n_owner, owned), inverse_order).reshape(D)

    taps = channel_table[:K]
    conv_bias = channel_table[K]
    step_bias = channel_table[K + 1]
    skip = channel_table[K + 2][None]
    a_neg = -jnp.exp(channel_table[K + 3 :])
    rate = tiled(a_neg / LOG_2)

    x_low = tokens[:, 0]
    x = x_low.astype(FULL)
    inverse = lax.rsqrt(jnp.mean(x * x, axis=2, keepdims=True) + norm_epsilon)
    flat_rows = micro * length
    x_rel = pick_columns(x_low.reshape(flat_rows, D), order).astype(FULL)
    normed = (x_rel * inverse.reshape(flat_rows, 1) * gain_low).astype(LOW)
    out_grad_low = out_grad[:, 0]
    grad_rel = pick_columns(out_grad_low.reshape(flat_rows, D), order)
    shape = (micro, length, inner)
    conv_in = dot(normed, conv_low, ((1,), (0,)), LOW).reshape(shape)
    earlier = shifted(conv_in[:, length - (K - 1) :], "ctx", 1)
    padded = jnp.concatenate([earlier, conv_in], axis=1).astype(FULL)
    conv = conv_bias + taps[0] * padded[:, 0:length]
    for k in range(1, K):
        conv = conv + taps[k] * padded[:, k : k + length]
    values = jax.nn.silu(conv).astype(LOW)
    values_flat = values.reshape(flat_rows, inner)
    proj = tensor_total(dot(values_flat, xproj_low, ((1,), (1,))))
    rank_low = proj[:, :R].astype(LOW)
    coef = proj[:, R:].reshape(micro, length, 2 * N)
    pre = dot(rank_low, step_low, ((1,), (0,))) + step_bias
    size = jax.nn.softplus(pre).reshape(shape)
    gate_in = dot(normed, gate_low, ((1,), (0,)), LOW).reshape(shape)
    grad_gated = dot(grad_rel, out_low, ((1,), (0,))).reshape(shape)
    start, tail = edges(size, values, grad_gated, gate_in, coef, rate)
    gated, gate_grad, before, grad_c, grad_skip = scan_forward(
        size, values, grad_gated, gate_in, coef, rate, start, skip
    )
    gated_flat = gated.reshape(flat_rows, inner)
    gate_grad_flat = gate_grad.reshape(flat_rows, inner)

    part_out = dot(grad_rel, gated_flat, ((0,), (0,)), LOW)
    part_gate = dot(normed, gate_grad_flat, ((0,), (0,)), LOW)
    mixed_list, token_list = [], []
    for m in range(micro):
        branch = dot(gated[m], out_low, ((1,), (1,)), LOW)
        own = line_scatter(branch.reshape(n_tensor, share, D))
        x_rows = lax.dynamic_slice_in_dim(x[m], first_row, share, 0)
        own = (x_rows + pick_columns(own, inverse_order)).astype(LOW)
        mixed_list.append(line_gather(own).reshape(length, D))
    shard_out = scatter(part_out.reshape(n_owner, owned, inner))
    shard_gate = scatter(part_gate.reshape(n_owner, owned, inner))

    conv_grads, rank_rows, proj_grads, gain_parts, tables = [], [], [], [], []
    pre_lows = []
    for m in range(micro):
        one = slice(m, m + 1)
        pre_low, grad_value, grad_b, grad_rate, grad_bias = scan_backward(
            size[one], values[one], grad_gated[one], gate_in[one], coef[one], rate, tail[one],
            skip, before[one],
        )
        pre_lows.append(pre_low[0])
        grad_rank = dot(pre_low[0], step_low, ((1,), (1,)))
        proj_grad = tensor_total(
            jnp.concatenate([grad_rank, grad_b[0, :, :N], grad_c[m, :, :N]], axis=1)
        ).astype(LOW)
        proj_grads.append(proj_grad)
        grad_values = grad_value[0] + dot(proj_grad, xproj_low, ((1,), (0,)))
        grad_conv = grad_values * silu_slope(conv[m])
        grad_taps = [
            jnp.sum(grad_conv * padded[m, k : k + length], axis=0) for k in range(K)
        ]
        head_rows = []
        for p in range(K - 1):
            total = taps[0] * grad_conv[p]
            for k in range(1, p + 1):
                total = total + taps[k] * grad_conv[p - k]
            head_rows.append(total)
        returned = shifted(jnp.stack(head_rows), "ctx", -1)
        extended = jnp.concatenate([grad_conv, jnp.zeros((K - 1, inner), FULL)], axis=0)
        grad_conv_in = taps[K - 1] * extended[0:length]
        for k in range(K - 1):
            grad_conv_in = grad_conv_in + taps[k] * extended[K - 1 - k : K - 1 - k + length]
        grad_conv_in = jnp.concatenate(
            [grad_conv_in[: length - (K - 1)], grad_conv_in[length - (K - 1) :] + returned], axis=0
        ).astype(LOW)
        conv_grads.append(grad_conv_in)
        grad_normed = (
            dot(gate_grad[m], gate_low, ((1,), (1,))) + dot(grad_conv_in, conv_low, ((1,), (1,)))
        ).astype(LOW)
        own = pick_columns(line_scatter(grad_normed.reshape(n_tensor, share, D)), inverse_order)
        x_rows = lax.dynamic_slice_in_dim(x[m], first_row, share, 0)
        inverse_rows = lax.dynamic_slice_in_dim(inverse[m], first_row, share, 0)
        grad_rows = lax.dynamic_slice_in_dim(out_grad_low[m], first_row, share, 0).astype(FULL)
        gain_parts.append(jnp.sum(own * x_rows * inverse_rows, axis=0))
        scaled = gain_value * own
        grad_x = inverse_rows * scaled - x_rows * inverse_rows * inverse_rows * inverse_rows * (
            jnp.mean(x_rows * scaled, axis=1, keepdims=True)
        )
        token_list.append(line_gather((grad_rows + grad_x).astype(LOW)).reshape(length, D))
        tables.append(
            jnp.concatenate(
                [
                    jnp.stack(grad_taps + [jnp.sum(grad_conv, axis=0)]),
                    grad_bias[0],
                    grad_skip[m],
                    flat(grad_rate[0], inner) * a_neg,
                ],
                axis=0,
            )
        )
    part_conv = dot(normed, jnp.concatenate(conv_grads, axis=0), ((0,), (0,)), LOW)
    shard_conv = scatter(part_conv.reshape(n_owner, owned, inner))
    part_step = dot(rank_low, jnp.concatenate(pre_lows, axis=0), ((0,), (0,)))
    part_xproj = dot(jnp.concatenate(proj_grads, axis=0), values_flat, ((0,), (0,)))
    part_gain = sum(gain_parts[1:], gain_parts[0]).reshape(n_owner, 1, owned)
    part_small = jnp.concatenate(
        [
            part_xproj.reshape(n_owner, n_x, inner),
            part_step.reshape(n_owner, n_s, inner),
            jnp.pad(part_gain, ((0, 0), (0, 0), (0, inner - owned))),
            jnp.zeros((n_owner, pad_rows, inner), FULL),
        ],
        axis=1,
    ).astype(LOW)
    shard_small = scatter(pick(part_small, order))
    shard_xproj = shard_small[:n_x]
    shard_step = shard_small[n_x : n_x + n_s]
    gain_partial = shard_small[n_x + n_s, :owned]
    grad_table = sum(tables[1:], tables[0])

    shard_in = jnp.stack([shard_conv, shard_gate], axis=1)
    matrices = (shard_in, shard_xproj, shard_step, shard_out)
    weights = (in_weight, xproj_weight, step_weight, outproj_weight)
    all_weights = [norm_gain] + list(weights) + [channel_table]
    shares = jnp.array([1.0 / n_tensor, 1.0, 1.0, 1.0, 1.0, 1.0 / n_owner], FULL)
    weight_sq = jnp.stack([jnp.sum(w * w) for w in all_weights]) * shares
    old_rows = (in_rows, xproj_rows, step_rows, out_rows)
    old_cols = (in_cols, xproj_cols, step_cols, out_cols)
    width_cols = (2 * E, E, E, E)
    width_rows = (D, R + 2 * N, R, D)
    squares = [matrix * matrix + square_floor for matrix in matrices]
    row_parts = [jnp.sum(square.reshape(square.shape[0], -1), axis=1) for square in squares]
    col_parts = [jnp.sum(square, axis=0).reshape(-1, inner) for square in squares]
    row_sums = butterfly(jnp.concatenate(row_parts + [gain_partial, weight_sq]), ("tensor",))
    ends = [0]
    for part in row_parts + [gain_partial, weight_sq]:
        ends.append(ends[-1] + part.shape[0])
    row_sums = [row_sums[ends[i] : ends[i + 1]] for i in range(6)]
    row_news = [
        decay_rate * old_rows[i] + (1.0 - decay_rate) * row_sums[i] / width_cols[i]
        for i in range(4)
    ]
    shard_gain = row_sums[4]
    totals = jnp.stack([jnp.sum(row_new) for row_new in row_news])
    scalars = butterfly(jnp.concatenate([totals, row_sums[5]]), own_axes)
    row_totals, total_weight = scalars[:4], scalars[4:]
    summed = butterfly(jnp.concatenate(col_parts + [grad_table], axis=0), own_axes)
    col_sums = [summed[0:2], summed[2], summed[3], summed[4]]
    table_grad = summed[5:]
    col_news = [
        decay_rate * old_cols[i] + (1.0 - decay_rate) * col_sums[i] / width_rows[i]
        for i in range(4)
    ]
    updates = []
    for i in range(4):
        row_mean = row_totals[i] / width_rows[i]
        shape = (-1,) + (1,) * (matrices[i].ndim - 1)
        second = row_news[i].reshape(shape) * col_news[i][None] / row_mean
        updates.append(matrices[i] * lax.rsqrt(second))
    new_gain_second = decay_rate * gain_second + (1.0 - decay_rate) * (
        shard_gain * shard_gain + square_floor
    )
    gain_update = shard_gain * lax.rsqrt(new_gain_second)
    new_table_second = decay_rate * table_second + (1.0 - decay_rate) * (
        table_grad * table_grad + square_floor
    )
    table_update = table_grad * lax.rsqrt(new_table_second)
    all_updates = [gain_update] + updates + [table_update]
    update_sq = jnp.stack([jnp.sum(u * u) for u in all_updates]) * shares
    total_update = butterfly(update_sq, own_axes + ("tensor",))
    counts = jnp.array([D, 2 * D * E, (R + 2 * N) * E, R * E, D * E, (K + 3 + N) * E], FULL)
    update_rms = jnp.sqrt(total_update / counts)
    factor = jnp.maximum(1.0, update_rms / clip_limit)
    scale = jnp.sqrt(total_weight / counts)
    stride = step_rate * scale / factor
    new_weights = [all_weights[i] - stride[i] * all_updates[i] for i in range(6)]
    mixed = jnp.stack(mixed_list)[:, None]
    token_grad = jnp.stack(token_list)[:, None]
    return (
        mixed,
        token_grad,
        shard_gain,
        shard_in,
        shard_xproj,
        shard_step,
        shard_out,
        table_grad,
        new_weights[0],
        new_weights[1],
        new_weights[2],
        new_weights[3],
        new_weights[4],
        new_weights[5],
        new_gain_second,
        row_news[0],
        col_news[0],
        row_news[1],
        col_news[1],
        row_news[2],
        col_news[2],
        row_news[3],
        col_news[3],
        new_table_second,
        update_rms,
    )


def solution(mesh):
    rows = P(("dp", "ctx"))
    matrix = P(("dp", "ctx"), "tensor")
    cube = P(("dp", "ctx"), None, "tensor")
    table = P(None, "tensor")
    block = P(None, "dp", "ctx", None)
    cols = P("tensor")
    return jax.shard_map(
        per_device,
        mesh=mesh,
        in_specs=(block, block, rows, cube, matrix, matrix, matrix, table, rows)
        + (rows, table, rows, cols, rows, cols, rows, cols, table),
        out_specs=(block, block, rows, cube, matrix, matrix, matrix, table)
        + (rows, cube, matrix, matrix, matrix, table, rows)
        + (rows, table, rows, cols, rows, cols, rows, cols, table, P()),
        check_vma=False,
    )
```

```python
import functools
import math

import jax
import jax.numpy as jnp
from jax import lax
from jax.experimental import pallas as pl
from jax.experimental.pallas import tpu as pltpu
from jax.sharding import PartitionSpec as P

D = 2048
E = 4096
N = 16
R = 128
K = 4
LANES = 128
LOG_2 = math.log(2.0)
LOW = jnp.bfloat16
FULL = jnp.float32

norm_epsilon = 1e-05
square_floor = 1e-30
decay_rate = 0.5
clip_limit = 0.5
step_rate = 1.0


def after(value, *others):
    return lax.optimization_barrier((value,) + others)[0]


def bits(axis):
    size = lax.axis_size(axis)
    return [1 << b for b in range(size.bit_length() - 1)]


def swap(block, axis, bit):
    return lax.ppermute(block, axis, [(i, i ^ bit) for i in range(lax.axis_size(axis))])


def shifted(block, axis, distance):
    devices = range(lax.axis_size(axis))
    route = [(i - distance, i) for i in devices if i - distance in devices]
    return lax.ppermute(block, axis, route)


def butterfly(value, axes):
    for axis in axes:
        for bit in bits(axis):
            value = value + swap(value, axis, bit)
    return value


def relative_blocks():
    n_dp, n_ctx = lax.axis_size("dp"), lax.axis_size("ctx")
    dp, ctx = lax.axis_index("dp"), lax.axis_index("ctx")
    return [
        (dp ^ (q % n_dp)) * n_ctx + (ctx ^ (q // n_dp)) for q in range(n_dp * n_ctx)
    ], [
        (ctx ^ (j % n_ctx)) * n_dp + (dp ^ (j // n_ctx)) for j in range(n_dp * n_ctx)
    ]


def pick(blocks, order):
    return jnp.stack([lax.dynamic_index_in_dim(blocks, q, 0, False) for q in order])


def fetch(own):
    if lax.axis_size("dp") != 4:
        blocks = [own]
        for bit in bits("dp"):
            blocks = blocks + [swap(block, "dp", bit) for block in blocks]
        return blocks, blocks[1:]
    half = own.shape[0] // 2
    one, two = swap(own, "dp", 1), swap(own, "dp", 2)
    three = jnp.concatenate([swap(two[:half], "dp", 1), swap(one[half:], "dp", 2)], axis=0)
    return [own, one, two, three], [one, two]


def fetch_two(left, right, release_far, release_all):
    if lax.axis_size("dp") != 4:
        return fetch(left)[0], fetch(right)[0]
    left_one, left_two = swap(left, "dp", 1), swap(left, "dp", 2)
    right_one, right_two = swap(right, "dp", 1), swap(right, "dp", 2)
    left_far = swap(after(left_two, release_far), "dp", 1)
    right_far = swap(after(right_one, release_far), "dp", 2)
    left_far, right_far = after(left_far, *release_all), after(right_far, *release_all)
    return [left, left_one, left_two, left_far], [right, right_one, right_two, right_far]


def join(blocks):
    chunks = [jnp.concatenate(blocks, axis=0)]
    for bit in bits("ctx"):
        chunks = chunks + [swap(chunk, "ctx", bit) for chunk in chunks]
    return chunks


def scatter(chunks):
    for bit in reversed(bits("ctx")):
        half = len(chunks) // 2
        chunks = [
            (keep.astype(FULL) + swap(send, "ctx", bit).astype(FULL)).astype(LOW)
            for keep, send in zip(chunks[:half], chunks[half:])
        ]
    n_dp = lax.axis_size("dp")
    parts = chunks[0].reshape(n_dp, -1, chunks[0].shape[-1])
    if n_dp == 4:
        half = parts.shape[2] // 2
        left, right = parts[:, :, :half], parts[:, :, half:]
        got_left = swap(jnp.stack([left[1], left[3]]), "dp", 1).astype(FULL)
        got_right = swap(right[2:], "dp", 2).astype(FULL)
        far_left = (left[2].astype(FULL) + got_left[1]).astype(LOW)
        far_right = (right[1].astype(FULL) + got_right[1]).astype(LOW)
        end_left = swap(far_left, "dp", 2).astype(FULL)
        end_right = swap(far_right, "dp", 1).astype(FULL)
        return jnp.concatenate(
            [
                left[0].astype(FULL) + got_left[0] + end_left,
                right[0].astype(FULL) + got_right[0] + end_right,
            ],
            axis=1,
        )
    for bit in reversed(bits("dp")):
        half = parts.shape[0] // 2
        parts = parts[:half].astype(FULL) + swap(parts[half:].astype(LOW), "dp", bit).astype(FULL)
    return parts[0].astype(FULL)


def line_scatter(part):
    return lax.psum_scatter(part, "tensor", scatter_dimension=0, tiled=True)


def line_gather(own):
    return lax.all_gather(own, "tensor", axis=0, tiled=True)


def tensor_total(term):
    for bit in bits("tensor"):
        low = term.astype(LOW)
        term = low.astype(FULL) + swap(low, "tensor", bit).astype(FULL)
    return term


def gather_few(row):
    for axis in ("dp", "ctx"):
        for bit in bits(axis):
            row = jnp.concatenate([row, swap(row, axis, bit)], axis=0)
    return pick(row, relative_blocks()[1])


def in_order(parts):
    total = parts[0]
    for part in parts[1:]:
        total = total + part
    return total


def few_total(value, axes):
    for axis in axes:
        n, me = lax.axis_size(axis), lax.axis_index(axis)
        if n == 2:
            value = value + swap(value, axis, 1)
            continue
        parts = jnp.stack([value] + [
            lax.ppermute(value, axis, [(i, i ^ k) for i in range(n)]) for k in range(1, n)
        ])
        value = in_order([lax.dynamic_index_in_dim(parts, me ^ k, 0, False) for k in range(n)])
    return value


def spread(target, columns, place, rows, tile):
    target[pl.ds(place, rows, stride=tile), :] = columns


def splat(target, table, first, rows):
    for n in range(N):
        target[pl.ds(n, rows, stride=N), :] = jnp.broadcast_to(
            table[:, first + n : first + n + 1], (rows, LANES)
        )


def columns_of(j):
    return slice(j * LANES, (j + 1) * LANES)


def edge_kernel(
    rows, groups, tile, unroll, flag, size_ref, value_ref, grad_ref, gate_ref, coef_ref, rate_ref,
    edge_ref, size_s, term_s, coef_s,
):
    backward = flag[0] == 1

    @pl.when(pl.program_id(0) == 0)
    def _():
        edge_ref[...] = jnp.zeros_like(edge_ref)

    for j in range(tile):
        if j < groups:
            spread(size_s, size_ref[:, columns_of(j)], j, rows, tile)
        else:
            spread(size_s, jnp.zeros((rows, LANES), FULL), j, rows, tile)
            spread(term_s, jnp.zeros((rows, LANES), FULL), j, rows, tile)

    def loop(body):
        first = tuple(edge_ref[n] for n in range(N))
        last = lax.fori_loop(0, rows, body, first, unroll=unroll)
        for n in range(N):
            edge_ref[n] = last[n]

    @pl.when(jnp.logical_not(backward))
    def _():
        for j in range(groups):
            cut = columns_of(j)
            spread(term_s, size_ref[:, cut] * value_ref[:, cut].astype(FULL), j, rows, tile)
        splat(coef_s, coef_ref, 0, rows)

        def body(t, state):
            place = pl.ds(pl.multiple_of(t * tile, tile), tile)
            size, term = size_s[place, :], term_s[place, :]
            return tuple(
                jnp.exp2(size * rate_ref[n]) * state[n] + term * coef_s[pl.ds(t * N + n, 1), :]
                for n in range(N)
            )

        loop(body)

    @pl.when(backward)
    def _():
        for j in range(groups):
            cut = columns_of(j)
            gate = gate_ref[:, cut].astype(FULL)
            spread(term_s, grad_ref[:, cut] * gate * jax.nn.sigmoid(gate), j, rows, tile)
        splat(coef_s, coef_ref, N, rows)

        def body(step, state):
            t = rows - 1 - step
            place = pl.ds(pl.multiple_of(t * tile, tile), tile)
            size, term = size_s[place, :], term_s[place, :]
            return tuple(
                jnp.exp2(size * rate_ref[n])
                * (state[n] + term * coef_s[pl.ds(t * N + n, 1), :])
                for n in range(N)
            )

        loop(body)


def forward_kernel(
    rows, groups, tile, part, unroll,
    size_ref, value_ref, grad_ref, gate_ref, coef_ref, rate_ref, start_ref, skip_ref, pick_ref,
    gated_ref, gate_grad_ref, before_ref, grad_c_ref, grad_skip_ref,
    size_s, input_s, grad_s, out_s, b_s, c_s, product_s, state_s,
):
    @pl.when(pl.program_id(0) == 0)
    def _():
        state_s[...] = start_ref[...]
        grad_skip_ref[...] = jnp.zeros_like(grad_skip_ref)

    blank = jnp.zeros((rows, LANES), FULL)
    for j in range(tile):
        if j < groups:
            cut = columns_of(j)
            size = size_ref[:, cut]
            value = value_ref[:, cut].astype(FULL)
            gate = gate_ref[:, cut].astype(FULL)
            scan_grad = grad_ref[:, cut] * gate * jax.nn.sigmoid(gate)
            spread(size_s, size, j, rows, tile)
            spread(input_s, size * value, j, rows, tile)
            spread(grad_s, scan_grad, j, rows, tile)
            grad_skip_ref[:, cut] += jnp.sum(scan_grad * value, axis=0, keepdims=True)
        else:
            for target in (size_s, input_s, grad_s):
                spread(target, blank, j, rows, tile)
    splat(b_s, coef_ref, 0, rows)
    splat(c_s, coef_ref, N, rows)
    for low in range(0, N, part):
        rate = [rate_ref[n] for n in range(low, low + part)]

        def body(t, state):
            state = list(state)
            place = pl.ds(pl.multiple_of(t * tile, tile), tile)
            size, term, grad = size_s[place, :], input_s[place, :], grad_s[place, :]
            out = None
            for k in range(part):
                n = low + k
                before_ref[t, n] = state[k]
                state[k] = (
                    jnp.exp2(size * rate[k]) * state[k] + term * b_s[pl.ds(t * N + n, 1), :]
                )
                read = c_s[pl.ds(t * N + n, 1), :] * state[k]
                out = read if out is None else out + read
                product_s[place, columns_of(n)] = state[k] * grad
            if low == 0:
                out_s[place, :] = out
            else:
                out_s[place, :] = out_s[place, :] + out
            return tuple(state)

        first = tuple(state_s[n] for n in range(low, low + part))
        last = lax.fori_loop(0, rows, body, first, unroll=unroll)
        for k in range(part):
            state_s[low + k] = last[k]
    for j in range(groups):
        cut = columns_of(j)
        scan_out = out_s[pl.ds(j, rows, stride=tile), :] + skip_ref[:, cut] * value_ref[
            :, cut
        ].astype(FULL)
        gate = gate_ref[:, cut].astype(FULL)
        sigma = jax.nn.sigmoid(gate)
        gated_ref[:, cut] = (scan_out * (gate * sigma)).astype(LOW)
        slope = sigma * (1.0 + gate * (1.0 - sigma))
        gate_grad_ref[:, cut] = (grad_ref[:, cut] * scan_out * slope).astype(LOW)
    sums = jnp.dot(product_s[...].astype(LOW), pick_ref[...], preferred_element_type=FULL)
    grad_c_ref[...] = jnp.sum(sums.reshape(rows, tile, LANES), axis=1)


def backward_kernel(
    rows, groups, tile, part, unroll,
    size_ref, value_ref, grad_ref, gate_ref, coef_ref, rate_ref, tail_ref, skip_ref, pick_ref,
    before_ref,
    pre_low_ref, grad_value_ref, grad_b_ref, grad_rate_ref, grad_bias_ref,
    size_s, input_s, grad_s, along_s, rated_s, b_s, c_s, product_s, state_s,
):
    @pl.when(pl.program_id(0) == 0)
    def _():
        state_s[...] = tail_ref[...]
        grad_rate_ref[...] = jnp.zeros_like(grad_rate_ref)
        grad_bias_ref[...] = jnp.zeros_like(grad_bias_ref)

    blank = jnp.zeros((rows, LANES), FULL)
    for j in range(tile):
        if j < groups:
            cut = columns_of(j)
            size = size_ref[:, cut]
            gate = gate_ref[:, cut].astype(FULL)
            spread(size_s, size, j, rows, tile)
            spread(input_s, size * value_ref[:, cut].astype(FULL), j, rows, tile)
            spread(grad_s, grad_ref[:, cut] * gate * jax.nn.sigmoid(gate), j, rows, tile)
        else:
            for target in (size_s, input_s, grad_s):
                spread(target, blank, j, rows, tile)
    splat(b_s, coef_ref, 0, rows)
    splat(c_s, coef_ref, N, rows)
    for low in range(0, N, part):
        rate = [rate_ref[n] for n in range(low, low + part)]

        def body(step, carry):
            state, total = list(carry[0]), list(carry[1])
            t = rows - 1 - step
            place = pl.ds(pl.multiple_of(t * tile, tile), tile)
            size, term, grad = size_s[place, :], input_s[place, :], grad_s[place, :]
            along = rated = None
            for k in range(part):
                n = low + k
                adjoint = c_s[pl.ds(t * N + n, 1), :] * grad + state[k]
                state[k] = jnp.exp2(size * rate[k]) * adjoint
                through = state[k] * before_ref[t, n]
                first = adjoint * b_s[pl.ds(t * N + n, 1), :]
                second = through * rate[k]
                along = first if along is None else along + first
                rated = second if rated is None else rated + second
                total[k] = total[k] + through * size
                product_s[place, columns_of(n)] = adjoint * term
            if low == 0:
                along_s[place, :] = along
                rated_s[place, :] = rated
            else:
                along_s[place, :] = along_s[place, :] + along
                rated_s[place, :] = rated_s[place, :] + rated
            return tuple(state), tuple(total)

        place = range(low, low + part)
        first = (tuple(state_s[n] for n in place), tuple(grad_rate_ref[n] for n in place))
        state, total = lax.fori_loop(0, rows, body, first, unroll=unroll)
        for k in range(part):
            state_s[low + k] = state[k]
            grad_rate_ref[low + k] = total[k]
    for j in range(groups):
        cut = columns_of(j)
        size = size_ref[:, cut]
        along = along_s[pl.ds(j, rows, stride=tile), :]
        rated = rated_s[pl.ds(j, rows, stride=tile), :]
        grad_size = along * value_ref[:, cut].astype(FULL) + LOG_2 * rated
        grad_pre = grad_size * (jnp.tanh(0.5 * size) * (1.0 + jnp.exp(-size)))
        pre_low_ref[:, cut] = grad_pre.astype(LOW)
        grad_bias_ref[:, cut] += jnp.sum(grad_pre, axis=0, keepdims=True)
        scan_grad = grad_s[pl.ds(j, rows, stride=tile), :]
        grad_value_ref[:, cut] = along * size + skip_ref[:, cut] * scan_grad
    sums = jnp.dot(product_s[...].astype(LOW), pick_ref[...], preferred_element_type=FULL)
    grad_b_ref[...] = jnp.sum(sums.reshape(rows, tile, LANES), axis=1)


def picker():
    shape = (N * LANES, LANES)
    state = lax.broadcasted_iota(jnp.int32, shape, 0) // LANES
    return (state == lax.broadcasted_iota(jnp.int32, shape, 1)).astype(LOW)


def tiles(channels):
    groups = channels // LANES
    return groups, 8 * pl.cdiv(groups, 8)


def tiled(table):
    groups, tile = tiles(table.shape[-1])
    table = table.reshape(table.shape[:-1] + (groups, LANES))
    pads = [(0, 0)] * (table.ndim - 2) + [(0, tile - groups), (0, 0)]
    return jnp.pad(table, pads)


def flat(table, channels):
    groups, _ = tiles(channels)
    return table[..., :groups, :].reshape(table.shape[:-2] + (channels,))


def cost(micro, length, ops, size):
    work = micro * length * N * 1024 * ops * 100
    return pl.CostEstimate(flops=work, bytes_accessed=size, transcendentals=0)


def limits():
    return pltpu.CompilerParams(vmem_limit_bytes=56 * 1024 * 1024)


def scan_edge(flag, size, value, grad, gate, coef, rate):
    length, channels = size.shape
    groups, tile = tiles(channels)
    rows = min(64, length)
    count = length // rows

    def place(i, f):
        return (jnp.where(f[0] == 0, i, count - 1 - i), 0)

    wide = pl.BlockSpec((rows, channels), place)
    cube = pl.BlockSpec((N, tile, LANES), lambda i, f: (0, 0, 0))
    return pl.pallas_call(
        functools.partial(edge_kernel, rows, groups, tile, 4),
        grid_spec=pltpu.PrefetchScalarGridSpec(
            num_scalar_prefetch=1,
            grid=(count,),
            in_specs=[wide] * 4 + [pl.BlockSpec((rows, 2 * N), place), cube],
            out_specs=cube,
            scratch_shapes=[pltpu.VMEM((rows * tile, LANES), FULL)] * 2
            + [pltpu.VMEM((rows * N, LANES), FULL)],
        ),
        out_shape=jax.ShapeDtypeStruct((N, tile, LANES), FULL),
        compiler_params=limits(),
        cost_estimate=cost(1, length, 8, size.size * 12),
        name="scan_edge",
    )(flag, size, value, grad, gate, coef, rate)


def scan_forward(size, value, grad, gate, coef, rate, start, skip):
    length, channels = size.shape
    groups, tile = tiles(channels)
    rows = min(64, length)
    wide = pl.BlockSpec((rows, channels), lambda i: (i, 0))
    row = pl.BlockSpec((1, channels), lambda i: (0, 0))
    cube = pl.BlockSpec((N, tile, LANES), lambda i: (0, 0, 0))
    return pl.pallas_call(
        functools.partial(forward_kernel, rows, groups, tile, 8, 4),
        grid=(length // rows,),
        in_specs=[wide] * 4
        + [
            pl.BlockSpec((rows, 2 * N), lambda i: (i, 0)),
            cube,
            cube,
            row,
            pl.BlockSpec((N * LANES, LANES), lambda i: (0, 0)),
        ],
        out_specs=[
            wide,
            wide,
            pl.BlockSpec((rows, N, tile, LANES), lambda i: (i, 0, 0, 0)),
            pl.BlockSpec((rows, LANES), lambda i: (i, 0)),
            row,
        ],
        out_shape=[
            jax.ShapeDtypeStruct(size.shape, LOW),
            jax.ShapeDtypeStruct(size.shape, LOW),
            jax.ShapeDtypeStruct((length, N, tile, LANES), FULL),
            jax.ShapeDtypeStruct((length, LANES), FULL),
            jax.ShapeDtypeStruct((1, channels), FULL),
        ],
        scratch_shapes=[pltpu.VMEM((rows * tile, LANES), FULL)] * 4
        + [pltpu.VMEM((rows * N, LANES), FULL)] * 2
        + [pltpu.VMEM((rows * tile, N * LANES), FULL), pltpu.VMEM((N, tile, LANES), FULL)],
        compiler_params=limits(),
        cost_estimate=cost(1, length, 15, size.size * 80),
        name="scan_forward",
    )(size, value, grad, gate, coef, rate, start, skip, picker())


def scan_backward(size, value, grad, gate, coef, rate, tail, skip, before):
    length, channels = size.shape
    groups, tile = tiles(channels)
    rows = min(64, length)
    last = length // rows - 1
    wide = pl.BlockSpec((rows, channels), lambda i: (last - i, 0))
    row = pl.BlockSpec((1, channels), lambda i: (0, 0))
    cube = pl.BlockSpec((N, tile, LANES), lambda i: (0, 0, 0))
    return pl.pallas_call(
        functools.partial(backward_kernel, rows, groups, tile, 8, 4),
        grid=(length // rows,),
        in_specs=[wide] * 4
        + [
            pl.BlockSpec((rows, 2 * N), lambda i: (last - i, 0)),
            cube,
            cube,
            row,
            pl.BlockSpec((N * LANES, LANES), lambda i: (0, 0)),
            pl.BlockSpec((rows, N, tile, LANES), lambda i: (last - i, 0, 0, 0)),
        ],
        out_specs=[wide, wide, pl.BlockSpec((rows, LANES), lambda i: (last - i, 0)), cube, row],
        out_shape=[
            jax.ShapeDtypeStruct(size.shape, LOW),
            jax.ShapeDtypeStruct(size.shape, FULL),
            jax.ShapeDtypeStruct((length, LANES), FULL),
            jax.ShapeDtypeStruct((N, tile, LANES), FULL),
            jax.ShapeDtypeStruct((1, channels), FULL),
        ],
        scratch_shapes=[pltpu.VMEM((rows * tile, LANES), FULL)] * 5
        + [pltpu.VMEM((rows * N, LANES), FULL)] * 2
        + [pltpu.VMEM((rows * tile, N * LANES), FULL), pltpu.VMEM((N, tile, LANES), FULL)],
        compiler_params=limits(),
        cost_estimate=cost(1, length, 20, size.size * 80),
        name="scan_backward",
    )(size, value, grad, gate, coef, rate, tail, skip, picker(), before)


def edges(size, value, grad, gate, coef, rate):
    count, place = lax.axis_size("ctx"), lax.axis_index("ctx")
    args = (size, value, grad, gate, coef, rate)
    if count == 2:
        edge = scan_edge(place.astype(jnp.int32)[None], *args)
        other = swap(edge, "ctx", 1)
        return jnp.where(place == 1, other, 0.0), jnp.where(place == 0, other, 0.0)
    last = scan_edge(jnp.zeros((1,), jnp.int32), *args)
    head = scan_edge(jnp.ones((1,), jnp.int32), *args)
    through = jnp.exp2(rate * tiled(jnp.sum(size, axis=0, keepdims=True)))
    lasts, heads, throughs = (lax.all_gather(a, "ctx") for a in (last, head, through))
    start = tail = jnp.zeros(last.shape, FULL)
    for i in range(count):
        start = jnp.where(i < place, throughs[i] * start + lasts[i], start)
        j = count - 1 - i
        tail = jnp.where(j > place, throughs[j] * tail + heads[j], tail)
    return start, tail


def block_of(index, width):
    return pl.ds(pl.multiple_of(index * width, width), width)


def normalize_kernel(width, chunks, order, x_ref, grad_ref, gain_ref, *outs):
    x = x_ref[...].astype(FULL)
    inverse = lax.rsqrt(jnp.mean(x * x, axis=1, keepdims=True) + norm_epsilon)
    columns = D // chunks
    for chunk in range(chunks):
        for low in range(0, columns, width):
            q = (chunk * columns + low) // width
            source = block_of(order[q], width)
            place = slice(low, low + width)
            value = x_ref[:, source].astype(FULL) * inverse * gain_ref[q : q + 1, :]
            outs[chunk][:, place] = value.astype(LOW)
            outs[chunks + chunk][:, place] = grad_ref[:, source]


def normalize(order, m, length, x, grad, gain, n_ctx):
    height, width = length, D // len(order)
    if width % LANES:
        x, grad = x[m * length : (m + 1) * length], grad[m * length : (m + 1) * length]
        full = x.astype(FULL)
        inverse = lax.rsqrt(jnp.mean(full * full, axis=1, keepdims=True) + norm_epsilon)

        def arrange(array):
            blocks = jnp.swapaxes(array.reshape(height, len(order), width), 0, 1)
            blocks = pick(blocks, order).reshape(n_ctx, -1, height, width)
            return list(jnp.swapaxes(blocks, 1, 2).reshape(n_ctx, height, D // n_ctx))

        gain = pick(gain, inverse_of(order))
        return arrange((full * inverse * gain.reshape(1, D)).astype(LOW)), arrange(grad)
    rows = min(128, height)
    wide = pl.BlockSpec((rows, D), lambda i, o: (m * (length // rows) + i, 0))
    out = pl.BlockSpec((rows, D // n_ctx), lambda i, o: (i, 0))
    shape = jax.ShapeDtypeStruct((height, D // n_ctx), LOW)
    outs = pl.pallas_call(
        functools.partial(normalize_kernel, width, n_ctx),
        grid_spec=pltpu.PrefetchScalarGridSpec(
            num_scalar_prefetch=1,
            grid=(height // rows,),
            in_specs=[wide, wide, pl.BlockSpec((len(order), width), lambda i, o: (0, 0))],
            out_specs=[out] * (2 * n_ctx),
        ),
        out_shape=[shape] * (2 * n_ctx),
        compiler_params=limits(),
        name="normalize",
    )(jnp.stack(order).astype(jnp.int32), x, grad, gain)
    return outs[:n_ctx], outs[n_ctx:]


def inverse_of(order):
    return relative_blocks()[1]


def unpermuted(chunks, inverse_order):
    rows, width = jnp.concatenate(chunks, axis=1), D // len(inverse_order)
    return jnp.concatenate(
        [lax.dynamic_slice_in_dim(rows, q * width, width, 1) for q in inverse_order], axis=1
    )


def own_block(block, share):
    return pl.BlockSpec((share, D), lambda i, o: (o[block], 0))


def whole_of(array):
    return pl.BlockSpec(array.shape, lambda i, o: (0,) * array.ndim)


def mix_kernel(width, per_chunk, order, x_ref, branch_ref, out_ref):
    for q in range(D // width):
        place = block_of(order[q], width)
        value = branch_ref[:, q * width : (q + 1) * width].astype(FULL)
        out_ref[:, place] = (x_ref[:, place].astype(FULL) + value).astype(LOW)


def mix(order, block, x, branch):
    width, share = D // len(order), branch.shape[0]
    if width % LANES:
        x = lax.dynamic_slice_in_dim(x, block * share, share, 0)
        return (x.astype(FULL) + unpermuted([branch.astype(FULL)], inverse_of(order))).astype(LOW)
    return pl.pallas_call(
        functools.partial(mix_kernel, width, 0),
        grid_spec=pltpu.PrefetchScalarGridSpec(
            num_scalar_prefetch=1,
            grid=(1,),
            in_specs=[own_block(len(order), share), whole_of(branch)],
            out_specs=whole_of(branch),
        ),
        out_shape=jax.ShapeDtypeStruct((share, D), LOW),
        compiler_params=limits(),
        name="mix",
    )(jnp.stack(order + [block]).astype(jnp.int32), x, branch)


def token_kernel(width, order, x_ref, grad_ref, gain_ref, normed_ref, out_ref, gain_out_ref, scaled_s):
    x = x_ref[...].astype(FULL)
    inverse = lax.rsqrt(jnp.mean(x * x, axis=1, keepdims=True) + norm_epsilon)
    total = jnp.zeros_like(inverse)
    for q in range(D // width):
        place = block_of(order[q], width)
        value = normed_ref[:, q * width : (q + 1) * width].astype(FULL)
        part = x_ref[:, place].astype(FULL)
        gain_out_ref[pl.ds(order[q], 1), :] = jnp.sum(
            value * part * inverse, axis=0, keepdims=True
        )
        scaled = value * gain_ref[q : q + 1, :]
        total = total + jnp.sum(part * scaled, axis=1, keepdims=True)
        scaled_s[:, place] = scaled
    slope = inverse * inverse * inverse * (total / D)
    out_ref[...] = (
        grad_ref[...].astype(FULL) + inverse * scaled_s[...] - x * slope
    ).astype(LOW)


def token_rows(order, block, x, grad, gain, normed):
    width, share = D // len(order), normed.shape[0]
    if width % LANES:
        x = lax.dynamic_slice_in_dim(x, block * share, share, 0).astype(FULL)
        grad = lax.dynamic_slice_in_dim(grad, block * share, share, 0).astype(FULL)
        value = unpermuted([normed.astype(FULL)], inverse_of(order))
        inverse = lax.rsqrt(jnp.mean(x * x, axis=1, keepdims=True) + norm_epsilon)
        part = jnp.sum(value * x * inverse, axis=0).reshape(len(order), width)
        scaled = value * pick(gain, inverse_of(order)).reshape(1, D)
        slope = inverse * inverse * inverse * jnp.mean(x * scaled, axis=1, keepdims=True)
        return (grad + inverse * scaled - x * slope).astype(LOW), part
    wide = own_block(len(order), share)
    return pl.pallas_call(
        functools.partial(token_kernel, width),
        grid_spec=pltpu.PrefetchScalarGridSpec(
            num_scalar_prefetch=1,
            grid=(1,),
            in_specs=[wide, wide, whole_of(gain), whole_of(normed)],
            out_specs=[whole_of(normed), whole_of(gain)],
            scratch_shapes=[pltpu.VMEM((share, D), FULL)],
        ),
        out_shape=[
            jax.ShapeDtypeStruct((share, D), LOW),
            jax.ShapeDtypeStruct((len(order), width), FULL),
        ],
        compiler_params=limits(),
        name="token_rows",
    )(jnp.stack(order + [block]).astype(jnp.int32), x, grad, gain, normed)


def conv_kernel(
    value_grad_ref, proj_ref, xproj_ref, conv_in_ref, earlier_ref, table_ref,
    out_ref, last_ref, head_ref, sums_ref, padded_s, grad_s,
):
    length = conv_in_ref.shape[0]
    taps = [table_ref[k : k + 1, :] for k in range(K)]
    padded_s[pl.ds(0, 8), :] = earlier_ref[...].astype(FULL)
    padded_s[pl.ds(8, length), :] = conv_in_ref[...].astype(FULL)
    conv = table_ref[K : K + 1, :] + taps[0] * padded_s[pl.ds(9 - K, length), :]
    for k in range(1, K):
        conv = conv + taps[k] * padded_s[pl.ds(9 - K + k, length), :]
    sigma = jax.nn.sigmoid(conv)
    slope = sigma * (1.0 + conv * (1.0 - sigma))
    grad_values = value_grad_ref[...] + jnp.dot(
        proj_ref[...], xproj_ref[...], preferred_element_type=FULL
    )
    grad_conv = grad_values * slope
    grad_s[pl.ds(0, length), :] = grad_conv
    grad_s[pl.ds(length, 8), :] = jnp.zeros((8, grad_conv.shape[1]), FULL)
    for k in range(K):
        sums_ref[k : k + 1, :] = jnp.sum(
            grad_conv * padded_s[pl.ds(9 - K + k, length), :], axis=0, keepdims=True
        )
    sums_ref[K : K + 1, :] = jnp.sum(grad_conv, axis=0, keepdims=True)
    sums_ref[K + 1 :, :] = jnp.zeros((7 - K, grad_conv.shape[1]), FULL)
    total = taps[K - 1] * grad_conv
    for k in range(K - 1):
        total = total + taps[k] * grad_s[pl.ds(K - 1 - k, length), :]
    out_ref[...] = total.astype(LOW)
    last_ref[...] = total[length - 8 :]
    head_ref[...] = jnp.zeros_like(head_ref)
    for p in range(K - 1):
        row = taps[0] * grad_s[pl.ds(p, 1), :]
        for k in range(1, p + 1):
            row = row + taps[k] * grad_s[pl.ds(p - k, 1), :]
        head_ref[9 - K + p : 10 - K + p, :] = row


def conv_backward(value_grad, proj_grad, xproj_low, conv_in, earlier, table):
    length, channels = value_grad.shape
    width = min(256, channels)
    tall = pl.BlockSpec((length, width), lambda j: (0, j))
    short = pl.BlockSpec((8, width), lambda j: (0, j))
    few = jax.ShapeDtypeStruct((8, channels), FULL)
    return pl.pallas_call(
        conv_kernel,
        grid=(channels // width,),
        in_specs=[
            tall,
            pl.BlockSpec(proj_grad.shape, lambda j: (0, 0)),
            pl.BlockSpec((proj_grad.shape[1], width), lambda j: (0, j)),
            tall,
            short,
            pl.BlockSpec((8, width), lambda j: (0, j)),
        ],
        out_specs=[tall, short, short, short],
        out_shape=[jax.ShapeDtypeStruct((length, channels), LOW), few, few, few],
        scratch_shapes=[pltpu.VMEM((length + 8, width), FULL)] * 2,
        compiler_params=limits(),
        name="conv_backward",
    )(value_grad, proj_grad, xproj_low, conv_in, earlier, table)


def dot(a, b, dims, kind=FULL):
    return lax.dot_general(a, b, (dims, ((), ())), preferred_element_type=FULL).astype(kind)


def per_device(
    tokens,
    out_grad,
    norm_gain,
    in_weight,
    xproj_weight,
    step_weight,
    outproj_weight,
    channel_table,
    gain_second,
    in_rows,
    in_cols,
    xproj_rows,
    xproj_cols,
    step_rows,
    step_cols,
    out_rows,
    out_cols,
    table_second,
):
    micro = tokens.shape[0]
    length = tokens.shape[2]
    inner = in_weight.shape[2]
    n_tensor = lax.axis_size("tensor")
    n_owner = lax.axis_size("dp") * lax.axis_size("ctx")
    owned = in_weight.shape[0]
    order, inverse_order = relative_blocks()
    n_ctx = lax.axis_size("ctx")
    own_axes = ("ctx", "dp")
    me = lax.axis_index("tensor")

    n_x, n_s = xproj_weight.shape[0], step_weight.shape[0]
    gain_row = jnp.pad(norm_gain.astype(LOW), (0, inner - owned))[None]
    in_own = in_weight.reshape(owned, 2 * inner).astype(LOW)
    first_own = [in_own[:, :inner], xproj_weight.astype(LOW), step_weight.astype(LOW), gain_row]
    pad_rows = -(owned + n_x + n_s + 1) % 64
    if pad_rows:
        first_own.append(jnp.zeros((pad_rows, inner), LOW))
    blocks, arrived = fetch(jnp.concatenate(first_own, axis=0))
    small = jnp.concatenate(join([block[owned:] for block in blocks]), axis=0)
    small = small.reshape(n_owner, -1, inner)
    conv_low = join([block[:owned] for block in blocks])
    gain_low = small[:, n_x + n_s, :owned].astype(FULL)
    small = pick(small, inverse_order)
    xproj_low = small[:, :n_x].reshape(n_owner * n_x, inner)
    step_low = small[:, n_x : n_x + n_s].reshape(n_owner * n_s, inner)
    gate_own = after(in_own[:, inner:], *arrived)
    out_own = after(outproj_weight.astype(LOW), *arrived)

    taps = channel_table[:K]
    conv_bias = channel_table[K]
    step_bias = channel_table[K + 1]
    skip = channel_table[K + 2][None]
    a_neg = -jnp.exp(channel_table[K + 3 :])
    rate = tiled(a_neg / LOG_2)

    def contract(parts, weights):
        total = dot(parts[0], weights[0], ((1,), (0,)))
        for part, weight in zip(parts[1:], weights[1:]):
            total = total + dot(part, weight, ((1,), (0,)))
        return total

    every = range(micro)
    tokens_flat = tokens.reshape(micro * length, D)
    grad_flat = out_grad.reshape(micro * length, D)
    normed, grad_rel = zip(
        *(normalize(order, m, length, tokens_flat, grad_flat, gain_low, n_ctx) for m in every)
    )
    conv_in = [contract(normed[m], conv_low).astype(LOW) for m in every]
    earlier, values, part_proj = [], [], []
    for m in every:
        earlier.append(shifted(conv_in[m][length - 8 :], "ctx", 1))
        padded = jnp.concatenate([earlier[m], conv_in[m]], axis=0).astype(FULL)
        conv = conv_bias + taps[0] * padded[9 - K : 9 - K + length]
        for k in range(1, K):
            conv = conv + taps[k] * padded[9 - K + k : 9 - K + k + length]
        values.append(jax.nn.silu(conv).astype(LOW))
        part_proj.append(dot(values[m], xproj_low, ((1,), (1,))))
    gate_blocks, out_blocks = fetch_two(gate_own, out_own, conv_in[0], part_proj)
    gate_low, out_low = join(gate_blocks), join(out_blocks)
    gate_in = [contract(normed[m], gate_low).astype(LOW) for m in every]
    grad_gated, size, coef, rank_low = [], [], [], []
    for m in every:
        proj = tensor_total(part_proj[m])
        rank_low.append(proj[:, :R].astype(LOW))
        coef.append(proj[:, R:])
        pre = dot(rank_low[m], step_low, ((1,), (0,))) + step_bias
        size.append(jax.nn.softplus(pre))
    gated, gate_grad, before, grad_c, grad_skip, tail, branch = [], [], [], [], [], [], []
    for m in every:
        weights_now = out_low if m == 0 else [after(w, branch[-1]) for w in out_low]
        grad_gated.append(contract(grad_rel[m], weights_now))
        args = (size[m], values[m], grad_gated[m], gate_in[m], coef[m], rate)
        entering, leaving = edges(*args)
        tail.append(leaving)
        outs = scan_forward(*args, entering, skip)
        for held, out in zip((gated, gate_grad, before, grad_c, grad_skip), outs):
            held.append(out)
        branch.append(
            jnp.concatenate([dot(gated[m], w, ((1,), (1,)), LOW) for w in out_low], axis=1)
        )
    own_mixed = [
        mix(order, m * n_tensor + me, tokens_flat, line_scatter(branch[m])) for m in every
    ]

    mixed_list = [line_gather(own) for own in own_mixed]

    def stacked(parts):
        ends = ((0, micro - 1, 0), (0, 0, 0), (0, 0, 0))
        whole = lax.pad(parts[0][None], jnp.zeros((), LOW), ends)
        for m in range(1, micro):
            whole = lax.dynamic_update_slice(whole, parts[m][None], (m, 0, 0))
        return whole

    def over_micros(left, right):
        total = dot(left[0], right[0], ((0,), (0,)))
        for a, b in zip(left[1:], right[1:]):
            total = total + dot(a, b, ((0,), (0,)))
        return total

    def chunks_of(parts):
        return list(zip(*parts))

    conv_grads, proj_grads, gain_parts, tables, partial, pre_lows = [], [], [], [], [], []
    part_out = part_gate = ()
    tokens_out, before_next = [], []
    mixed_ready = [own_mixed[0]]
    for m in every:
        leaving = after(tail[m], branch[-1], *mixed_ready, *before_next)
        pre_low, value_grad, grad_b, grad_rate, grad_bias = scan_backward(
            size[m], values[m], grad_gated[m], gate_in[m], coef[m], rate, leaving, skip, before[m]
        )
        if m > 0:
            pre_low = after(pre_low, mixed_list[-1])
        pre_lows.append(pre_low)
        grad_rank = dot(pre_low, step_low, ((1,), (1,)))
        part = jnp.concatenate([grad_rank, grad_b[:, :N], grad_c[m][:, :N]], axis=1)
        proj_grad = tensor_total(part).astype(LOW)
        proj_grads.append(proj_grad)
        if m == 0:
            gated_then = [after(gated[0], part)] + gated[1:]
            part_out = [over_micros(g, gated_then).astype(LOW) for g in chunks_of(grad_rel)]
            filler = part_out
        else:
            normed_then = [[after(n, part) for n in parts] for parts in normed]
            if m == micro - 1:
                part_gate = [
                    over_micros(g, gate_grad).astype(LOW) for g in chunks_of(normed_then)
                ]
            filler = list(part_gate)
        gate_grad_then = after(gate_grad[m], part)
        gate_part = [dot(gate_grad_then, g, ((1,), (1,))) for g in gate_low]
        conv_grad, last, head, sums = conv_backward(
            after(value_grad, *filler, *gate_part, *tokens_out, mixed_list[0]),
            proj_grad, xproj_low, conv_in[m], earlier[m], channel_table[:8],
        )
        last = last + shifted(head, "ctx", -1)
        conv_grad = lax.dynamic_update_slice(conv_grad, last.astype(LOW), (length - 8, 0))
        conv_grads.append(conv_grad)
        partial.append(
            jnp.concatenate(
                [
                    (g + dot(conv_grad, c, ((1,), (1,)))).astype(LOW)
                    for g, c in zip(gate_part, conv_low)
                ],
                axis=1,
            )
        )
        mixed_ready, before_next = own_mixed, [partial[m]]
        partial[m] = after(partial[m], mixed_list[-1])
        token, gain_part = token_rows(
            order, m * n_tensor + me, tokens_flat, grad_flat, gain_low, line_scatter(partial[m])
        )
        gain_parts.append(gain_part)
        tokens_out.append(token)
        tables.append(
            jnp.concatenate(
                [sums[: K + 1], grad_bias, grad_skip[m], flat(grad_rate, inner) * a_neg], axis=0
            )
        )
    normed_then = [[after(n, partial[-1]) for n in parts] for parts in normed]
    part_conv = [over_micros(g, conv_grads).astype(LOW) for g in chunks_of(normed_then)]
    shard_out = scatter(part_out)
    shard_gate = scatter(part_gate)
    shard_conv = scatter(part_conv)
    token_grad = stacked([line_gather(token) for token in tokens_out])
    token_grad = token_grad.reshape(tokens.shape)
    mixed = stacked(mixed_list).reshape(tokens.shape)
    part_step = over_micros(rank_low, pre_lows)
    part_xproj = over_micros(proj_grads, values)
    part_small = jnp.concatenate(
        [part_xproj.reshape(n_owner, n_x, inner), part_step.reshape(n_owner, n_s, inner)], axis=1
    )
    pad_rows = -(n_x + n_s) % 16
    part_small = jnp.pad(part_small, ((0, 0), (0, pad_rows), (0, 0))).astype(LOW)
    shard_small = scatter(list(pick(part_small, order).reshape(n_ctx, -1, inner)))
    shard_xproj = shard_small[:n_x]
    shard_step = shard_small[n_x : n_x + n_s]
    gain_grad = butterfly(in_order(gain_parts), ("tensor",) + own_axes)
    owner = lax.axis_index("dp") * n_ctx + lax.axis_index("ctx")
    shard_gain = lax.dynamic_index_in_dim(gain_grad, owner, 0, False)
    grad_table = in_order(tables)

    shard_in = jnp.stack([shard_conv, shard_gate], axis=1)
    matrices = (shard_in, shard_xproj, shard_step, shard_out)
    weights = (in_weight, xproj_weight, step_weight, outproj_weight)
    all_weights = [norm_gain] + list(weights) + [channel_table]
    shares = jnp.array([1.0 / n_tensor, 1.0, 1.0, 1.0, 1.0, 1.0 / n_owner], FULL)
    weight_sq = jnp.stack([jnp.sum(jnp.square(after(w, pre_lows[0]))) for w in all_weights]) * shares
    old_rows = (in_rows, xproj_rows, step_rows, out_rows)
    old_cols = (in_cols, xproj_cols, step_cols, out_cols)
    width_cols = (2 * E, E, E, E)
    width_rows = (D, R + 2 * N, R, D)
    squares = [matrix * matrix + square_floor for matrix in matrices]
    row_parts = [jnp.sum(square.reshape(square.shape[0], -1), axis=1) for square in squares]
    col_parts = [jnp.sum(square, axis=0).reshape(-1, inner) for square in squares]
    row_sums = few_total(jnp.concatenate(row_parts + [weight_sq]), ("tensor",))
    ends = [0]
    for part in row_parts + [weight_sq]:
        ends.append(ends[-1] + part.shape[0])
    row_sums = [row_sums[ends[i] : ends[i + 1]] for i in range(5)]
    row_news = [
        decay_rate * old_rows[i] + (1.0 - decay_rate) * row_sums[i] / width_cols[i]
        for i in range(4)
    ]
    totals = jnp.stack([jnp.sum(row_new) for row_new in row_news])
    scalars = few_total(jnp.concatenate([totals, row_sums[4]]), own_axes)
    row_totals, total_weight = scalars[:4], scalars[4:]
    summed = butterfly(jnp.concatenate(col_parts + [grad_table], axis=0), own_axes)
    col_sums = [summed[0:2], summed[2], summed[3], summed[4]]
    table_grad = summed[5:]
    col_news = [
        decay_rate * old_cols[i] + (1.0 - decay_rate) * col_sums[i] / width_rows[i]
        for i in range(4)
    ]
    updates = []
    for i in range(4):
        row_mean = row_totals[i] / width_rows[i]
        shape = (-1,) + (1,) * (matrices[i].ndim - 1)
        second = row_news[i].reshape(shape) * col_news[i][None] / row_mean
        updates.append(matrices[i] * lax.rsqrt(second))
    every_second = decay_rate * gather_few(after(gain_second[None], pre_lows[0])) + (
        1.0 - decay_rate
    ) * (gain_grad * gain_grad + square_floor)
    every_update = gain_grad * lax.rsqrt(every_second)
    new_gain_second = lax.dynamic_index_in_dim(every_second, owner, 0, False)
    gain_update = lax.dynamic_index_in_dim(every_update, owner, 0, False)
    new_table_second = decay_rate * table_second + (1.0 - decay_rate) * (
        table_grad * table_grad + square_floor
    )
    table_update = table_grad * lax.rsqrt(new_table_second)
    all_updates = [gain_update] + updates + [table_update]
    update_sq = jnp.stack([jnp.sum(u * u) for u in all_updates[1:]]) * shares[1:]
    total_update = few_total(update_sq, own_axes + ("tensor",))
    gain_sq = jnp.sum(every_update * every_update)[None]
    total_update = jnp.concatenate([gain_sq, total_update])
    counts = jnp.array([D, 2 * D * E, (R + 2 * N) * E, R * E, D * E, (K + 3 + N) * E], FULL)
    update_rms = jnp.sqrt(total_update / counts)
    factor = jnp.maximum(1.0, update_rms / clip_limit)
    scale = jnp.sqrt(total_weight / counts)
    stride = step_rate * scale / factor
    new_weights = [all_weights[i] - stride[i] * all_updates[i] for i in range(6)]
    return (
        mixed,
        token_grad,
        shard_gain,
        shard_in,
        shard_xproj,
        shard_step,
        shard_out,
        table_grad,
        new_weights[0],
        new_weights[1],
        new_weights[2],
        new_weights[3],
        new_weights[4],
        new_weights[5],
        new_gain_second,
        row_news[0],
        col_news[0],
        row_news[1],
        col_news[1],
        row_news[2],
        col_news[2],
        row_news[3],
        col_news[3],
        new_table_second,
        update_rms,
    )


def solution(mesh):
    rows = P(("dp", "ctx"))
    matrix = P(("dp", "ctx"), "tensor")
    cube = P(("dp", "ctx"), None, "tensor")
    table = P(None, "tensor")
    block = P(None, "dp", "ctx", None)
    cols = P("tensor")
    return jax.shard_map(
        per_device,
        mesh=mesh,
        in_specs=(block, block, rows, cube, matrix, matrix, matrix, table, rows)
        + (rows, table, rows, cols, rows, cols, rows, cols, table),
        out_specs=(block, block, rows, cube, matrix, matrix, matrix, table)
        + (rows, cube, matrix, matrix, matrix, table, rows)
        + (rows, table, rows, cols, rows, cols, rows, cols, table, P()),
        check_vma=False,
    )
```

```python
import functools
import math

import jax
import jax.numpy as jnp
import numpy as np
from jax import lax
from jax.experimental import pallas as pl
from jax.experimental.pallas import tpu as pltpu
from jax.sharding import PartitionSpec as P

D = 2048
E = 4096
N = 16
R = 128
K = 4
LANES = 128
LOG_2 = math.log(2.0)
LOW = jnp.bfloat16
FULL = jnp.float32

norm_epsilon = 1e-05
square_floor = 1e-30
decay_rate = 0.5
clip_limit = 0.5
step_rate = 1.0


def after(value, *others):
    return lax.optimization_barrier((value,) + others)[0]


def after_all(values, *others):
    return list(lax.optimization_barrier(tuple(values) + others)[: len(values)])


def vector(scalars):
    place = lax.iota(jnp.int32, len(scalars))
    return in_order([jnp.where(place == i, s, 0.0) for i, s in enumerate(scalars)])


def bits(axis):
    size = lax.axis_size(axis)
    return [1 << b for b in range(size.bit_length() - 1)]


def swap(block, axis, bit):
    return lax.ppermute(block, axis, [(i, i ^ bit) for i in range(lax.axis_size(axis))])


def shifted(block, axis, distance):
    devices = range(lax.axis_size(axis))
    route = [(i - distance, i) for i in devices if i - distance in devices]
    return lax.ppermute(block, axis, route)


def butterfly(value, axes):
    for axis in axes:
        for bit in bits(axis):
            value = value + swap(value, axis, bit)
    return value


def relative_blocks():
    n_dp, n_ctx = lax.axis_size("dp"), lax.axis_size("ctx")
    dp, ctx = lax.axis_index("dp"), lax.axis_index("ctx")
    return [
        (dp ^ (q % n_dp)) * n_ctx + (ctx ^ (q // n_dp)) for q in range(n_dp * n_ctx)
    ], [
        (ctx ^ (j % n_ctx)) * n_dp + (dp ^ (j // n_ctx)) for j in range(n_dp * n_ctx)
    ]


def pick(blocks, order):
    return jnp.stack([lax.dynamic_index_in_dim(blocks, q, 0, False) for q in order])


def fetch(own, release_far=()):
    if lax.axis_size("dp") != 4:
        blocks = [own]
        for bit in bits("dp"):
            blocks = blocks + [swap(block, "dp", bit) for block in blocks]
        return blocks
    half = own.shape[0] // 2
    one, two = after_all([swap(own, "dp", 1), swap(own, "dp", 2)], *release_far)
    far = [swap(two[:half], "dp", 1), swap(one[half:], "dp", 2)]
    return [own, one, two, jnp.concatenate(far, axis=0)]


def fetch_two(left, right, release_far, release_all):
    if lax.axis_size("dp") != 4:
        return fetch(left), fetch(right)
    left_one, left_two = swap(left, "dp", 1), swap(left, "dp", 2)
    right_one, right_two = swap(right, "dp", 1), swap(right, "dp", 2)
    left_far = swap(after(left_two, release_far), "dp", 1)
    right_far = swap(after(right_one, release_far), "dp", 2)
    left_far, right_far = after(left_far, *release_all), after(right_far, *release_all)
    return [left, left_one, left_two, left_far], [right, right_one, right_two, right_far]


def join(blocks):
    chunks = [jnp.concatenate(blocks, axis=0)]
    for bit in bits("ctx"):
        chunks = chunks + [swap(chunk, "ctx", bit) for chunk in chunks]
    return chunks


def scatter(chunks, release=()):
    for bit in reversed(bits("ctx")):
        half = len(chunks) // 2
        chunks = [
            (keep.astype(FULL) + swap(send, "ctx", bit).astype(FULL)).astype(LOW)
            for keep, send in zip(chunks[:half], chunks[half:])
        ]
    return scatter_dp(chunks[0], release), chunks[0]


def scatter_dp(chunk, release):
    n_dp = lax.axis_size("dp")
    parts = chunk.reshape(n_dp, -1, chunk.shape[-1])
    if n_dp == 4:
        half = parts.shape[2] // 2
        left, right = parts[:, :, :half], parts[:, :, half:]
        got = [swap(jnp.stack([left[1], left[3]]), "dp", 1), swap(right[2:], "dp", 2)]
        got_left, got_right = (g.astype(FULL) for g in after_all(got, *release))
        far_left = (left[2].astype(FULL) + got_left[1]).astype(LOW)
        far_right = (right[1].astype(FULL) + got_right[1]).astype(LOW)
        end_left = swap(far_left, "dp", 2).astype(FULL)
        end_right = swap(far_right, "dp", 1).astype(FULL)
        return jnp.concatenate(
            [
                left[0].astype(FULL) + got_left[0] + end_left,
                right[0].astype(FULL) + got_right[0] + end_right,
            ],
            axis=1,
        )
    for bit in reversed(bits("dp")):
        half = parts.shape[0] // 2
        parts = parts[:half].astype(FULL) + swap(parts[half:].astype(LOW), "dp", bit).astype(FULL)
    return parts[0].astype(FULL)


def line_scatter(part):
    return lax.psum_scatter(part, "tensor", scatter_dimension=0, tiled=True)


def line_gather(own):
    return lax.all_gather(own, "tensor", axis=0, tiled=True)


def tensor_total(term):
    return tensor_steps(term)[-2]


def tensor_steps(term):
    steps, sent = [], []
    for bit in bits("tensor"):
        low = term.astype(LOW)
        term = low.astype(FULL) + swap(low, "tensor", bit).astype(FULL)
        steps.append(term)
        sent.append(low)
    return steps + sent[:1]


def gather_few(row):
    return pick(gather_relative(row), relative_blocks()[1])


def gather_relative(row):
    for axis in ("dp", "ctx"):
        for bit in bits(axis):
            row = jnp.concatenate([row, swap(row, axis, bit)], axis=0)
    return row


def in_order(parts):
    total = parts[0]
    for part in parts[1:]:
        total = total + part
    return total


def spread(target, columns, place, rows, tile):
    target[pl.ds(place, rows, stride=tile), :] = columns


def splat(target, table, first, rows):
    for n in range(N):
        target[pl.ds(n, rows, stride=N), :] = jnp.broadcast_to(
            table[:, first + n : first + n + 1], (rows, LANES)
        )


def columns_of(j):
    return slice(j * LANES, (j + 1) * LANES)


def edge_kernel(
    rows, groups, tile, unroll, flag, size_ref, value_ref, grad_ref, gate_ref, coef_ref, rate_ref,
    edge_ref, size_s, term_s, coef_s,
):
    backward = flag[0] == 1

    @pl.when(pl.program_id(0) == 0)
    def _():
        edge_ref[...] = jnp.zeros_like(edge_ref)

    for j in range(tile):
        if j < groups:
            spread(size_s, size_ref[:, columns_of(j)], j, rows, tile)
        else:
            spread(size_s, jnp.zeros((rows, LANES), FULL), j, rows, tile)
            spread(term_s, jnp.zeros((rows, LANES), FULL), j, rows, tile)

    def loop(body):
        first = tuple(edge_ref[n] for n in range(N))
        last = lax.fori_loop(0, rows, body, first, unroll=unroll)
        for n in range(N):
            edge_ref[n] = last[n]

    @pl.when(jnp.logical_not(backward))
    def _():
        for j in range(groups):
            cut = columns_of(j)
            spread(term_s, size_ref[:, cut] * value_ref[:, cut].astype(FULL), j, rows, tile)
        splat(coef_s, coef_ref, 0, rows)

        def body(t, state):
            place = pl.ds(pl.multiple_of(t * tile, tile), tile)
            size, term = size_s[place, :], term_s[place, :]
            return tuple(
                jnp.exp2(size * rate_ref[n]) * state[n] + term * coef_s[pl.ds(t * N + n, 1), :]
                for n in range(N)
            )

        loop(body)

    @pl.when(backward)
    def _():
        for j in range(groups):
            cut = columns_of(j)
            gate = gate_ref[:, cut].astype(FULL)
            spread(term_s, grad_ref[:, cut] * gate * jax.nn.sigmoid(gate), j, rows, tile)
        splat(coef_s, coef_ref, N, rows)

        def body(step, state):
            t = rows - 1 - step
            place = pl.ds(pl.multiple_of(t * tile, tile), tile)
            size, term = size_s[place, :], term_s[place, :]
            return tuple(
                jnp.exp2(size * rate_ref[n])
                * (state[n] + term * coef_s[pl.ds(t * N + n, 1), :])
                for n in range(N)
            )

        loop(body)


def forward_kernel(
    rows, groups, tile, part, unroll,
    size_ref, value_ref, grad_ref, gate_ref, coef_ref, rate_ref, start_ref, skip_ref,
    gated_ref, gate_grad_ref, before_ref, grad_c_ref, grad_skip_ref,
    size_s, input_s, grad_s, out_s, b_s, c_s, product_s, state_s, pick_s,
):
    @pl.when(pl.program_id(0) == 0)
    def _():
        state_s[...] = start_ref[...]
        set_picker(pick_s)
        grad_skip_ref[...] = jnp.zeros_like(grad_skip_ref)

    blank = jnp.zeros((rows, LANES), FULL)
    for j in range(tile):
        if j < groups:
            cut = columns_of(j)
            size = size_ref[:, cut]
            value = value_ref[:, cut].astype(FULL)
            gate = gate_ref[:, cut].astype(FULL)
            scan_grad = grad_ref[:, cut] * gate * jax.nn.sigmoid(gate)
            spread(size_s, size, j, rows, tile)
            spread(input_s, size * value, j, rows, tile)
            spread(grad_s, scan_grad, j, rows, tile)
            grad_skip_ref[:, cut] += jnp.sum(scan_grad * value, axis=0, keepdims=True)
        else:
            for target in (size_s, input_s, grad_s):
                spread(target, blank, j, rows, tile)
    splat(b_s, coef_ref, 0, rows)
    splat(c_s, coef_ref, N, rows)
    for low in range(0, N, part):
        rate = [rate_ref[n] for n in range(low, low + part)]

        def body(t, state):
            state = list(state)
            place = pl.ds(pl.multiple_of(t * tile, tile), tile)
            size, term, grad = size_s[place, :], input_s[place, :], grad_s[place, :]
            out = None
            for k in range(part):
                n = low + k
                before_ref[t, n] = state[k]
                state[k] = (
                    jnp.exp2(size * rate[k]) * state[k] + term * b_s[pl.ds(t * N + n, 1), :]
                )
                read = c_s[pl.ds(t * N + n, 1), :] * state[k]
                out = read if out is None else out + read
                product_s[place, columns_of(n)] = state[k] * grad
            if low == 0:
                out_s[place, :] = out
            else:
                out_s[place, :] = out_s[place, :] + out
            return tuple(state)

        first = tuple(state_s[n] for n in range(low, low + part))
        last = lax.fori_loop(0, rows, body, first, unroll=unroll)
        for k in range(part):
            state_s[low + k] = last[k]
    for j in range(groups):
        cut = columns_of(j)
        scan_out = out_s[pl.ds(j, rows, stride=tile), :] + skip_ref[:, cut] * value_ref[
            :, cut
        ].astype(FULL)
        gate = gate_ref[:, cut].astype(FULL)
        sigma = jax.nn.sigmoid(gate)
        gated_ref[:, cut] = (scan_out * (gate * sigma)).astype(LOW)
        slope = sigma * (1.0 + gate * (1.0 - sigma))
        gate_grad_ref[:, cut] = (grad_ref[:, cut] * scan_out * slope).astype(LOW)
    sums = jnp.dot(product_s[...].astype(LOW), pick_s[...], preferred_element_type=FULL)
    grad_c_ref[...] = jnp.sum(sums.reshape(rows, tile, LANES), axis=1)


def backward_kernel(
    rows, groups, tile, part, unroll,
    size_ref, value_ref, grad_ref, gate_ref, coef_ref, rate_ref, tail_ref, skip_ref,
    before_ref,
    pre_low_ref, grad_value_ref, grad_b_ref, grad_rate_ref, grad_bias_ref,
    size_s, input_s, grad_s, along_s, rated_s, b_s, c_s, product_s, state_s, pick_s,
):
    @pl.when(pl.program_id(0) == 0)
    def _():
        state_s[...] = tail_ref[...]
        set_picker(pick_s)
        grad_rate_ref[...] = jnp.zeros_like(grad_rate_ref)
        grad_bias_ref[...] = jnp.zeros_like(grad_bias_ref)

    blank = jnp.zeros((rows, LANES), FULL)
    for j in range(tile):
        if j < groups:
            cut = columns_of(j)
            size = size_ref[:, cut]
            gate = gate_ref[:, cut].astype(FULL)
            spread(size_s, size, j, rows, tile)
            spread(input_s, size * value_ref[:, cut].astype(FULL), j, rows, tile)
            spread(grad_s, grad_ref[:, cut] * gate * jax.nn.sigmoid(gate), j, rows, tile)
        else:
            for target in (size_s, input_s, grad_s):
                spread(target, blank, j, rows, tile)
    splat(b_s, coef_ref, 0, rows)
    splat(c_s, coef_ref, N, rows)
    for low in range(0, N, part):
        rate = [rate_ref[n] for n in range(low, low + part)]

        def body(step, carry):
            state, total = list(carry[0]), list(carry[1])
            t = rows - 1 - step
            place = pl.ds(pl.multiple_of(t * tile, tile), tile)
            size, term, grad = size_s[place, :], input_s[place, :], grad_s[place, :]
            along = rated = None
            for k in range(part):
                n = low + k
                adjoint = c_s[pl.ds(t * N + n, 1), :] * grad + state[k]
                state[k] = jnp.exp2(size * rate[k]) * adjoint
                through = state[k] * before_ref[t, n]
                first = adjoint * b_s[pl.ds(t * N + n, 1), :]
                second = through * rate[k]
                along = first if along is None else along + first
                rated = second if rated is None else rated + second
                total[k] = total[k] + through * size
                product_s[place, columns_of(n)] = adjoint * term
            if low == 0:
                along_s[place, :] = along
                rated_s[place, :] = rated
            else:
                along_s[place, :] = along_s[place, :] + along
                rated_s[place, :] = rated_s[place, :] + rated
            return tuple(state), tuple(total)

        place = range(low, low + part)
        first = (tuple(state_s[n] for n in place), tuple(grad_rate_ref[n] for n in place))
        state, total = lax.fori_loop(0, rows, body, first, unroll=unroll)
        for k in range(part):
            state_s[low + k] = state[k]
            grad_rate_ref[low + k] = total[k]
    for j in range(groups):
        cut = columns_of(j)
        size = size_ref[:, cut]
        along = along_s[pl.ds(j, rows, stride=tile), :]
        rated = rated_s[pl.ds(j, rows, stride=tile), :]
        grad_size = along * value_ref[:, cut].astype(FULL) + LOG_2 * rated
        grad_pre = grad_size * (jnp.tanh(0.5 * size) * (1.0 + jnp.exp(-size)))
        pre_low_ref[:, cut] = grad_pre.astype(LOW)
        grad_bias_ref[:, cut] += jnp.sum(grad_pre, axis=0, keepdims=True)
        scan_grad = grad_s[pl.ds(j, rows, stride=tile), :]
        grad_value_ref[:, cut] = along * size + skip_ref[:, cut] * scan_grad
    sums = jnp.dot(product_s[...].astype(LOW), pick_s[...], preferred_element_type=FULL)
    grad_b_ref[...] = jnp.sum(sums.reshape(rows, tile, LANES), axis=1)


def set_picker(pick_s):
    state = lax.broadcasted_iota(jnp.int32, pick_s.shape, 0) // LANES
    pick_s[...] = (state == lax.broadcasted_iota(jnp.int32, pick_s.shape, 1)).astype(LOW)


def tiles(channels):
    groups = channels // LANES
    return groups, 8 * pl.cdiv(groups, 8)


def tiled(table):
    groups, tile = tiles(table.shape[-1])
    table = table.reshape(table.shape[:-1] + (groups, LANES))
    pads = [(0, 0)] * (table.ndim - 2) + [(0, tile - groups), (0, 0)]
    return jnp.pad(table, pads)


def flat(table, channels):
    groups, _ = tiles(channels)
    return table[..., :groups, :].reshape(table.shape[:-2] + (channels,))


def cost(micro, length, ops, size):
    work = micro * length * N * 1024 * ops * 100
    return pl.CostEstimate(flops=work, bytes_accessed=size, transcendentals=0)


def limits():
    return pltpu.CompilerParams(vmem_limit_bytes=56 * 1024 * 1024)


def scan_edge(flag, size, value, grad, gate, coef, rate):
    length, channels = size.shape
    groups, tile = tiles(channels)
    rows = min(64, length)
    count = length // rows

    def place(i, f):
        return (jnp.where(f[0] == 0, i, count - 1 - i), 0)

    wide = pl.BlockSpec((rows, channels), place)
    cube = pl.BlockSpec((N, tile, LANES), lambda i, f: (0, 0, 0))
    return pl.pallas_call(
        functools.partial(edge_kernel, rows, groups, tile, 4),
        grid_spec=pltpu.PrefetchScalarGridSpec(
            num_scalar_prefetch=1,
            grid=(count,),
            in_specs=[wide] * 4 + [pl.BlockSpec((rows, 2 * N), place), cube],
            out_specs=cube,
            scratch_shapes=[pltpu.VMEM((rows * tile, LANES), FULL)] * 2
            + [pltpu.VMEM((rows * N, LANES), FULL)],
        ),
        out_shape=jax.ShapeDtypeStruct((N, tile, LANES), FULL),
        compiler_params=limits(),
        cost_estimate=cost(1, length, 8, size.size * 12),
        name="scan_edge",
    )(flag, size, value, grad, gate, coef, rate)


def scan_forward(size, value, grad, gate, coef, rate, start, skip):
    length, channels = size.shape
    groups, tile = tiles(channels)
    rows = min(64, length)
    wide = pl.BlockSpec((rows, channels), lambda i: (i, 0))
    row = pl.BlockSpec((1, channels), lambda i: (0, 0))
    cube = pl.BlockSpec((N, tile, LANES), lambda i: (0, 0, 0))
    return pl.pallas_call(
        functools.partial(forward_kernel, rows, groups, tile, 8, 4),
        grid=(length // rows,),
        in_specs=[wide] * 4
        + [
            pl.BlockSpec((rows, 2 * N), lambda i: (i, 0)),
            cube,
            cube,
            row,
        ],
        out_specs=[
            wide,
            wide,
            pl.BlockSpec((rows, N, tile, LANES), lambda i: (i, 0, 0, 0)),
            pl.BlockSpec((rows, LANES), lambda i: (i, 0)),
            row,
        ],
        out_shape=[
            jax.ShapeDtypeStruct(size.shape, LOW),
            jax.ShapeDtypeStruct(size.shape, LOW),
            jax.ShapeDtypeStruct((length, N, tile, LANES), FULL),
            jax.ShapeDtypeStruct((length, LANES), FULL),
            jax.ShapeDtypeStruct((1, channels), FULL),
        ],
        scratch_shapes=[pltpu.VMEM((rows * tile, LANES), FULL)] * 4
        + [pltpu.VMEM((rows * N, LANES), FULL)] * 2
        + [pltpu.VMEM((rows * tile, N * LANES), FULL), pltpu.VMEM((N, tile, LANES), FULL)]
        + [pltpu.VMEM((N * LANES, LANES), LOW)],
        compiler_params=limits(),
        cost_estimate=cost(1, length, 15, size.size * 80),
        name="scan_forward",
    )(size, value, grad, gate, coef, rate, start, skip)


def scan_backward(size, value, grad, gate, coef, rate, tail, skip, before):
    length, channels = size.shape
    groups, tile = tiles(channels)
    rows = min(64, length)
    last = length // rows - 1
    wide = pl.BlockSpec((rows, channels), lambda i: (last - i, 0))
    row = pl.BlockSpec((1, channels), lambda i: (0, 0))
    cube = pl.BlockSpec((N, tile, LANES), lambda i: (0, 0, 0))
    return pl.pallas_call(
        functools.partial(backward_kernel, rows, groups, tile, 8, 4),
        grid=(length // rows,),
        in_specs=[wide] * 4
        + [
            pl.BlockSpec((rows, 2 * N), lambda i: (last - i, 0)),
            cube,
            cube,
            row,
            pl.BlockSpec((rows, N, tile, LANES), lambda i: (last - i, 0, 0, 0)),
        ],
        out_specs=[wide, wide, pl.BlockSpec((rows, LANES), lambda i: (last - i, 0)), cube, row],
        out_shape=[
            jax.ShapeDtypeStruct(size.shape, LOW),
            jax.ShapeDtypeStruct(size.shape, FULL),
            jax.ShapeDtypeStruct((length, LANES), FULL),
            jax.ShapeDtypeStruct((N, tile, LANES), FULL),
            jax.ShapeDtypeStruct((1, channels), FULL),
        ],
        scratch_shapes=[pltpu.VMEM((rows * tile, LANES), FULL)] * 5
        + [pltpu.VMEM((rows * N, LANES), FULL)] * 2
        + [pltpu.VMEM((rows * tile, N * LANES), FULL), pltpu.VMEM((N, tile, LANES), FULL)]
        + [pltpu.VMEM((N * LANES, LANES), LOW)],
        compiler_params=limits(),
        cost_estimate=cost(1, length, 20, size.size * 80),
        name="scan_backward",
    )(size, value, grad, gate, coef, rate, tail, skip, before)


def edges(size, value, grad, gate, coef, rate):
    count, place = lax.axis_size("ctx"), lax.axis_index("ctx")
    args = (size, value, grad, gate, coef, rate)
    if count == 2:
        edge = scan_edge(place.astype(jnp.int32)[None], *args)
        other = swap(edge, "ctx", 1)
        return jnp.where(place == 1, other, 0.0), jnp.where(place == 0, other, 0.0)
    last = scan_edge(jnp.zeros((1,), jnp.int32), *args)
    head = scan_edge(jnp.ones((1,), jnp.int32), *args)
    through = jnp.exp2(rate * tiled(jnp.sum(size, axis=0, keepdims=True)))
    lasts, heads, throughs = (lax.all_gather(a, "ctx") for a in (last, head, through))
    start = tail = jnp.zeros(last.shape, FULL)
    for i in range(count):
        start = jnp.where(i < place, throughs[i] * start + lasts[i], start)
        j = count - 1 - i
        tail = jnp.where(j > place, throughs[j] * tail + heads[j], tail)
    return start, tail


def block_of(index, width):
    return pl.ds(pl.multiple_of(index * width, width), width)


def normalize_kernel(width, chunks, order, x_ref, grad_ref, gain_ref, *outs):
    x = x_ref[...].astype(FULL)
    inverse = lax.rsqrt(jnp.mean(x * x, axis=1, keepdims=True) + norm_epsilon)
    columns = D // chunks
    for chunk in range(chunks):
        for low in range(0, columns, width):
            q = (chunk * columns + low) // width
            source = block_of(order[q], width)
            place = slice(low, low + width)
            value = x_ref[:, source].astype(FULL) * inverse * gain_ref[q : q + 1, :]
            outs[chunk][:, place] = value.astype(LOW)
            outs[chunks + chunk][:, place] = grad_ref[:, source]


def normalize(order, m, length, x, grad, gain, n_ctx):
    height, width = length, D // len(order)
    if width % LANES:
        x, grad = x[m * length : (m + 1) * length], grad[m * length : (m + 1) * length]
        full = x.astype(FULL)
        inverse = lax.rsqrt(jnp.mean(full * full, axis=1, keepdims=True) + norm_epsilon)

        def arrange(array):
            blocks = jnp.swapaxes(array.reshape(height, len(order), width), 0, 1)
            blocks = pick(blocks, order).reshape(n_ctx, -1, height, width)
            return list(jnp.swapaxes(blocks, 1, 2).reshape(n_ctx, height, D // n_ctx))

        gain = pick(gain, inverse_of(order))
        return arrange((full * inverse * gain.reshape(1, D)).astype(LOW)), arrange(grad)
    rows = min(128, height)
    wide = pl.BlockSpec((rows, D), lambda i, o: (m * (length // rows) + i, 0))
    out = pl.BlockSpec((rows, D // n_ctx), lambda i, o: (i, 0))
    shape = jax.ShapeDtypeStruct((height, D // n_ctx), LOW)
    outs = pl.pallas_call(
        functools.partial(normalize_kernel, width, n_ctx),
        grid_spec=pltpu.PrefetchScalarGridSpec(
            num_scalar_prefetch=1,
            grid=(height // rows,),
            in_specs=[wide, wide, pl.BlockSpec((len(order), width), lambda i, o: (0, 0))],
            out_specs=[out] * (2 * n_ctx),
        ),
        out_shape=[shape] * (2 * n_ctx),
        compiler_params=limits(),
        name="normalize",
    )(jnp.stack(order).astype(jnp.int32), x, grad, gain)
    return outs[:n_ctx], outs[n_ctx:]


def inverse_of(order):
    return relative_blocks()[1]


def unpermuted(chunks, inverse_order):
    rows, width = jnp.concatenate(chunks, axis=1), D // len(inverse_order)
    return jnp.concatenate(
        [lax.dynamic_slice_in_dim(rows, q * width, width, 1) for q in inverse_order], axis=1
    )


def own_block(block, share):
    return pl.BlockSpec((share, D), lambda i, o: (o[block], 0))


def whole_of(array):
    return pl.BlockSpec(array.shape, lambda i, o: (0,) * array.ndim)


def mix_kernel(width, per_chunk, order, x_ref, branch_ref, out_ref):
    for q in range(D // width):
        place = block_of(order[q], width)
        value = branch_ref[:, q * width : (q + 1) * width].astype(FULL)
        out_ref[:, place] = (x_ref[:, place].astype(FULL) + value).astype(LOW)


def mix(order, block, x, branch):
    width, share = D // len(order), branch.shape[0]
    if width % LANES:
        x = lax.dynamic_slice_in_dim(x, block * share, share, 0)
        return (x.astype(FULL) + unpermuted([branch.astype(FULL)], inverse_of(order))).astype(LOW)
    return pl.pallas_call(
        functools.partial(mix_kernel, width, 0),
        grid_spec=pltpu.PrefetchScalarGridSpec(
            num_scalar_prefetch=1,
            grid=(1,),
            in_specs=[own_block(len(order), share), whole_of(branch)],
            out_specs=whole_of(branch),
        ),
        out_shape=jax.ShapeDtypeStruct((share, D), LOW),
        compiler_params=limits(),
        name="mix",
    )(jnp.stack(order + [block]).astype(jnp.int32), x, branch)


def token_kernel(width, order, x_ref, grad_ref, gain_ref, normed_ref, out_ref, gain_out_ref, scaled_s):
    x = x_ref[...].astype(FULL)
    inverse = lax.rsqrt(jnp.mean(x * x, axis=1, keepdims=True) + norm_epsilon)
    total = jnp.zeros_like(inverse)
    for q in range(D // width):
        place = block_of(order[q], width)
        value = normed_ref[:, q * width : (q + 1) * width].astype(FULL)
        part = x_ref[:, place].astype(FULL)
        gain_out_ref[pl.ds(order[q], 1), :] = jnp.sum(
            value * part * inverse, axis=0, keepdims=True
        )
        scaled = value * gain_ref[q : q + 1, :]
        total = total + jnp.sum(part * scaled, axis=1, keepdims=True)
        scaled_s[:, place] = scaled
    slope = inverse * inverse * inverse * (total / D)
    out_ref[...] = (
        grad_ref[...].astype(FULL) + inverse * scaled_s[...] - x * slope
    ).astype(LOW)


def token_rows(order, block, x, grad, gain, normed):
    width, share = D // len(order), normed.shape[0]
    if width % LANES:
        x = lax.dynamic_slice_in_dim(x, block * share, share, 0).astype(FULL)
        grad = lax.dynamic_slice_in_dim(grad, block * share, share, 0).astype(FULL)
        value = unpermuted([normed.astype(FULL)], inverse_of(order))
        inverse = lax.rsqrt(jnp.mean(x * x, axis=1, keepdims=True) + norm_epsilon)
        part = jnp.sum(value * x * inverse, axis=0).reshape(len(order), width)
        scaled = value * pick(gain, inverse_of(order)).reshape(1, D)
        slope = inverse * inverse * inverse * jnp.mean(x * scaled, axis=1, keepdims=True)
        return (grad + inverse * scaled - x * slope).astype(LOW), part
    wide = own_block(len(order), share)
    return pl.pallas_call(
        functools.partial(token_kernel, width),
        grid_spec=pltpu.PrefetchScalarGridSpec(
            num_scalar_prefetch=1,
            grid=(1,),
            in_specs=[wide, wide, whole_of(gain), whole_of(normed)],
            out_specs=[whole_of(normed), whole_of(gain)],
            scratch_shapes=[pltpu.VMEM((share, D), FULL)],
        ),
        out_shape=[
            jax.ShapeDtypeStruct((share, D), LOW),
            jax.ShapeDtypeStruct((len(order), width), FULL),
        ],
        compiler_params=limits(),
        name="token_rows",
    )(jnp.stack(order + [block]).astype(jnp.int32), x, grad, gain, normed)


def update_kernel(owners, *refs):
    n = len(owners)
    grads, scales, cols_ref, table_ref, out_ref = refs[:n], refs[n : 2 * n], *refs[2 * n :]
    out_ref[...] = jnp.zeros_like(out_ref)

    def lanes(squares):
        total = jnp.sum(squares, axis=0, keepdims=True)
        cuts = [total[:, columns_of(j)] for j in range(total.shape[1] // LANES)]
        return in_order(cuts)

    for i, owner in enumerate(owners):
        update = grads[i][...] * scales[i][...] * cols_ref[i : i + 1, :]
        out_ref[owner : owner + 1, :] += lanes(update * update)
    out_ref[5:6, :] = lanes(table_ref[...] * table_ref[...])


def update_squares(grads, scales, cols, table):
    return pl.pallas_call(
        functools.partial(update_kernel, (1, 1, 2, 3, 4)),
        out_shape=jax.ShapeDtypeStruct((6, LANES), FULL),
        compiler_params=limits(),
        name="update_squares",
    )(*grads, *scales, cols, table)


def pick_kernel(order, blocks_ref, out_ref):
    for j in range(blocks_ref.shape[0]):
        out_ref[j] = blocks_ref[order[j]]


def pick_rows(blocks, order):
    return pl.pallas_call(
        pick_kernel,
        in_specs=[pl.BlockSpec(memory_space=pltpu.SMEM), pl.BlockSpec(memory_space=pltpu.VMEM)],
        out_specs=pl.BlockSpec(memory_space=pltpu.VMEM),
        out_shape=jax.ShapeDtypeStruct(blocks.shape, blocks.dtype),
        compiler_params=limits(),
        name="pick_rows",
    )(jnp.stack(order).astype(jnp.int32), blocks)


def fill_kernel(part_ref, *refs):
    refs[-1][...] = part_ref[...]


def fill(whole, count, m, part):
    height, columns = part.shape
    rows = min(256, height)
    spec = pl.BlockSpec((None, rows, columns), lambda i: (m, i, 0))
    kept = [] if whole is None else [whole]
    return pl.pallas_call(
        fill_kernel,
        grid=(height // rows,),
        in_specs=[pl.BlockSpec((rows, columns), lambda i: (i, 0))]
        + [pl.BlockSpec(memory_space=pl.ANY)] * len(kept),
        out_specs=spec,
        out_shape=jax.ShapeDtypeStruct((count, height, columns), part.dtype),
        input_output_aliases={1: 0} if kept else {},
        compiler_params=limits(),
        name="fill",
    )(part, *kept)


def conv_kernel(
    value_grad_ref, proj_ref, xproj_ref, conv_in_ref, earlier_ref, table_ref,
    out_ref, last_ref, head_ref, sums_ref, padded_s, grad_s,
):
    length = conv_in_ref.shape[0]
    taps = [table_ref[k : k + 1, :] for k in range(K)]
    padded_s[pl.ds(0, 8), :] = earlier_ref[...].astype(FULL)
    padded_s[pl.ds(8, length), :] = conv_in_ref[...].astype(FULL)
    conv = table_ref[K : K + 1, :] + taps[0] * padded_s[pl.ds(9 - K, length), :]
    for k in range(1, K):
        conv = conv + taps[k] * padded_s[pl.ds(9 - K + k, length), :]
    sigma = jax.nn.sigmoid(conv)
    slope = sigma * (1.0 + conv * (1.0 - sigma))
    grad_values = value_grad_ref[...] + jnp.dot(
        proj_ref[...], xproj_ref[...], preferred_element_type=FULL
    )
    grad_conv = grad_values * slope
    grad_s[pl.ds(0, length), :] = grad_conv
    grad_s[pl.ds(length, 8), :] = jnp.zeros((8, grad_conv.shape[1]), FULL)
    for k in range(K):
        sums_ref[k : k + 1, :] = jnp.sum(
            grad_conv * padded_s[pl.ds(9 - K + k, length), :], axis=0, keepdims=True
        )
    sums_ref[K : K + 1, :] = jnp.sum(grad_conv, axis=0, keepdims=True)
    sums_ref[K + 1 :, :] = jnp.zeros((7 - K, grad_conv.shape[1]), FULL)
    total = taps[K - 1] * grad_conv
    for k in range(K - 1):
        total = total + taps[k] * grad_s[pl.ds(K - 1 - k, length), :]
    out_ref[...] = total.astype(LOW)
    last_ref[...] = total[length - 8 :]
    head_ref[...] = jnp.zeros_like(head_ref)
    for p in range(K - 1):
        row = taps[0] * grad_s[pl.ds(p, 1), :]
        for k in range(1, p + 1):
            row = row + taps[k] * grad_s[pl.ds(p - k, 1), :]
        head_ref[9 - K + p : 10 - K + p, :] = row


def conv_backward(value_grad, proj_grad, xproj_low, conv_in, earlier, table):
    length, channels = value_grad.shape
    width = min(256, channels)
    tall = pl.BlockSpec((length, width), lambda j: (0, j))
    short = pl.BlockSpec((8, width), lambda j: (0, j))
    few = jax.ShapeDtypeStruct((8, channels), FULL)
    return pl.pallas_call(
        conv_kernel,
        grid=(channels // width,),
        in_specs=[
            tall,
            pl.BlockSpec(proj_grad.shape, lambda j: (0, 0)),
            pl.BlockSpec((proj_grad.shape[1], width), lambda j: (0, j)),
            tall,
            short,
            pl.BlockSpec((8, width), lambda j: (0, j)),
        ],
        out_specs=[tall, short, short, short],
        out_shape=[jax.ShapeDtypeStruct((length, channels), LOW), few, few, few],
        scratch_shapes=[pltpu.VMEM((length + 8, width), FULL)] * 2,
        compiler_params=limits(),
        name="conv_backward",
    )(value_grad, proj_grad, xproj_low, conv_in, earlier, table)


def dot(a, b, dims, kind=FULL):
    return lax.dot_general(a, b, (dims, ((), ())), preferred_element_type=FULL).astype(kind)


def per_device(
    tokens,
    out_grad,
    norm_gain,
    in_weight,
    xproj_weight,
    step_weight,
    outproj_weight,
    channel_table,
    gain_second,
    in_rows,
    in_cols,
    xproj_rows,
    xproj_cols,
    step_rows,
    step_cols,
    out_rows,
    out_cols,
    table_second,
):
    micro = tokens.shape[0]
    length = tokens.shape[2]
    inner = in_weight.shape[2]
    n_tensor = lax.axis_size("tensor")
    n_owner = lax.axis_size("dp") * lax.axis_size("ctx")
    owned = in_weight.shape[0]
    order, inverse_order = relative_blocks()
    n_ctx = lax.axis_size("ctx")
    own_axes = ("ctx", "dp")
    me = lax.axis_index("tensor")

    n_x, n_s = xproj_weight.shape[0], step_weight.shape[0]
    every = range(micro)
    tokens_flat = tokens.reshape(micro * length, D)
    grad_flat = out_grad.reshape(micro * length, D)
    gain_rounded = after(norm_gain.astype(LOW), gain_second).astype(FULL)
    gain_row = jnp.stack([gain_rounded, gain_second])[None]
    for bit in bits("dp"):
        gain_row = jnp.concatenate([gain_row, swap(gain_row, "dp", bit)], axis=0)
    gain_low = gain_row
    for bit in bits("ctx"):
        gain_low = jnp.concatenate([gain_low, swap(gain_low, "ctx", bit)], axis=0)
    gain_low, second_low = gain_low[:, 0], gain_low[:, 1]
    normed, grad_rel = zip(
        *(normalize(order, m, length, tokens_flat, grad_flat, gain_low, n_ctx) for m in every)
    )
    normed, grad_rel = list(normed), list(grad_rel)
    in_own = in_weight.reshape(owned, 2 * inner).astype(LOW)
    first_own = [in_own[:, :inner], xproj_weight.astype(LOW), step_weight.astype(LOW)]
    pad_rows = -(owned + n_x + n_s) % 64
    if pad_rows:
        first_own.append(jnp.zeros((pad_rows, inner), LOW))
    blocks = fetch(after(jnp.concatenate(first_own, axis=0), gain_row), [n[0] for n in normed])
    conv_low = join([block[:owned] for block in blocks])
    small = jnp.concatenate(join([block[owned:] for block in blocks]), axis=0)
    small = pick_rows(small.reshape(n_owner, -1, inner), inverse_order)
    xproj_low = small[:, :n_x].reshape(n_owner * n_x, inner)
    step_low = small[:, n_x : n_x + n_s].reshape(n_owner * n_s, inner)
    gate_own, out_own = in_own[:, inner:], outproj_weight.astype(LOW)

    taps = channel_table[:K]
    conv_bias = channel_table[K]
    step_bias = channel_table[K + 1]
    skip = channel_table[K + 2][None]
    a_neg = -jnp.exp(channel_table[K + 3 :])
    rate = tiled(a_neg / LOG_2)

    def contract(parts, weights):
        total = dot(parts[0], weights[0], ((1,), (0,)))
        for part, weight in zip(parts[1:], weights[1:]):
            total = total + dot(part, weight, ((1,), (0,)))
        return total

    conv_in, earlier, values, part_proj, proj_steps = [], [], [], [], []
    for m in every:
        parts = normed[m] if m == 0 else after_all(normed[m], proj_steps[-1][-1])
        conv_in.append(contract(parts, conv_low).astype(LOW))
        earlier.append(shifted(conv_in[m][length - 8 :], "ctx", 1))
        padded = jnp.concatenate([earlier[m], conv_in[m]], axis=0).astype(FULL)
        conv = conv_bias + taps[0] * padded[9 - K : 9 - K + length]
        for k in range(1, K):
            conv = conv + taps[k] * padded[9 - K + k : 9 - K + k + length]
        values.append(jax.nn.silu(conv).astype(LOW))
        part_proj.append(dot(values[m], xproj_low, ((1,), (1,))))
        proj_steps.append(tensor_steps(part_proj[m]))
    gate_blocks, out_blocks = fetch_two(gate_own, out_own, conv_in[0], proj_steps[0][:1])
    gate_low, out_low = join(gate_blocks), join(out_blocks)
    weights = (in_weight, xproj_weight, step_weight, outproj_weight)
    all_weights = [norm_gain] + list(weights) + [channel_table]
    shares = jnp.array([1.0 / n_tensor, 1.0, 1.0, 1.0, 1.0, 1.0 / n_owner], FULL)
    gate_in, grad_gated, size, coef, rank_low, own_mixed, mixed = [], [], [], [], [], [], []
    gated, gate_grad, before, grad_c, grad_skip, tail, branch = [], [], [], [], [], [], []
    for m in every:
        proj = proj_steps[m][-2]
        rank_low.append(proj[:, :R].astype(LOW))
        coef.append(proj[:, R:])
        now_low, now_rel, now_normed = rank_low[m], grad_rel[m], normed[m]
        if m > 0:
            now_low = after(now_low, branch[-1])
            now_rel, now_normed = after_all(now_rel, branch[-1]), after_all(now_normed, branch[-1])
        pre = dot(now_low, step_low, ((1,), (0,))) + step_bias
        size.append(jax.nn.softplus(pre))
        gate_in.append(contract(now_normed, gate_low).astype(LOW))
        grad_gated.append(contract(now_rel, out_low))
        args = (size[m], values[m], grad_gated[m], gate_in[m], coef[m], rate)
        entering, leaving = edges(*args)
        tail.append(leaving)
        outs = scan_forward(*args, entering, skip)
        for held, out in zip((gated, gate_grad, before, grad_c, grad_skip), outs):
            held.append(out)
        branch.append(
            jnp.concatenate([dot(gated[m], w, ((1,), (1,)), LOW) for w in out_low], axis=1)
        )
        own_mixed.append(mix(order, m * n_tensor + me, tokens_flat, line_scatter(branch[m])))

    def over_micros(left, right):
        total = dot(left[0], right[0], ((0,), (0,)))
        for a, b in zip(left[1:], right[1:]):
            total = total + dot(a, b, ((0,), (0,)))
        return total

    def chunks_of(parts):
        return list(zip(*parts))

    backs, parts, steps_of, gate_parts, part_out = [], [], [], [], []
    for m in every:
        leaving = after(tail[m], branch[-1], own_mixed[0])
        if m > 0:
            leaving = after(leaving, steps_of[0][0], *part_out, *gate_parts[0], *own_mixed)
        pre_low, value_grad, grad_b, grad_rate, grad_bias = scan_backward(
            size[m], values[m], grad_gated[m], gate_in[m], coef[m], rate, leaving, skip, before[m]
        )
        backs.append((pre_low, value_grad, grad_rate, grad_bias))
        grad_rank = dot(pre_low, step_low, ((1,), (1,)))
        parts.append(jnp.concatenate([grad_rank, grad_b[:, :N], grad_c[m][:, :N]], axis=1))
        steps_of.append(tensor_steps(parts[m]))
        if m == 0:
            for side in chunks_of(grad_rel):
                part_out.append(over_micros(after_all(side, parts[0]), gated).astype(LOW))
            gate_grad_then = after(gate_grad[0], parts[0], *own_mixed)
            gate_parts.append([dot(gate_grad_then, g, ((1,), (1,))) for g in gate_low])
    mixed = [line_gather(own_mixed[0])]
    pre_lows = [back[0] for back in backs]
    conv_grads, proj_grads, gain_parts, tables, partial, tokens_out = [], [], [], [], [], []
    part_gate = []
    for m in every:
        _, value_grad, grad_rate, grad_bias = backs[m]
        proj_grad = steps_of[m][-2].astype(LOW)
        proj_grads.append(proj_grad)
        wait_for = [mixed[0], parts[-1]]
        if m > 0:
            started = [partial[0], steps_of[m][0]]
            gate_grad_then = after(gate_grad[m], *started)
            gate_parts.append([dot(gate_grad_then, g, ((1,), (1,))) for g in gate_low])
            if m == micro - 1:
                for c, side in enumerate(chunks_of(normed)):
                    arrived = started + steps_of[m][-2:-1] if c else started
                    part_gate.append(over_micros(after_all(side, *arrived), gate_grad).astype(LOW))
            wait_for = wait_for + gate_parts[m] + part_gate
        conv_grad, last, head, sums = conv_backward(
            after(value_grad, *wait_for),
            proj_grad, xproj_low, conv_in[m], earlier[m], channel_table[:8],
        )
        last = last + shifted(head, "ctx", -1)
        conv_grad = lax.dynamic_update_slice(conv_grad, last.astype(LOW), (length - 8, 0))
        if m == 0:
            conv_grad = after(conv_grad, steps_of[-1][0])
        conv_grads.append(conv_grad)
        partial.append(
            jnp.concatenate(
                [
                    (g + dot(conv_grad, c, ((1,), (1,)))).astype(LOW)
                    for g, c in zip(gate_parts[m], conv_low)
                ],
                axis=1,
            )
        )
        sent = after(partial[m], steps_of[-1][-2])
        token, gain_part = token_rows(
            order, m * n_tensor + me, tokens_flat, grad_flat, gain_low, line_scatter(sent)
        )
        gain_parts.append(gain_part)
        tokens_out.append(token)
        rates = flat(grad_rate, inner) * a_neg
        tables.append(jnp.concatenate([sums[: K + 1], grad_bias, grad_skip[m], rates], axis=0))
    normed_then = [after_all(sides, partial[-1]) for sides in normed]
    part_conv = [over_micros(g, conv_grads).astype(LOW) for g in chunks_of(normed_then)]
    shard_conv, middle = scatter(part_conv)
    shard_out, _ = scatter(part_out, [middle])
    shard_gate, _ = scatter(part_gate, [middle])
    weight_sq = vector([jnp.sum(jnp.square(after(w, middle))) for w in all_weights]) * shares
    mixed = mixed + [line_gather(after(own, partial[-1])) for own in own_mixed[1:]]
    whole_mixed = token_grad = None
    for m in every:
        whole_mixed = fill(whole_mixed, micro, m, after(mixed[m], middle))
        token_grad = fill(token_grad, micro, m, line_gather(tokens_out[m]))
        token_first = token_grad if m == 0 else token_first
    mixed = whole_mixed.reshape(tokens.shape)
    token_grad = token_grad.reshape(tokens.shape)
    pre_lows, proj_grads = after_all(pre_lows, middle), after_all(proj_grads, middle)
    part_step = over_micros(rank_low, pre_lows)
    part_xproj = over_micros(proj_grads, values)
    part_small = jnp.concatenate(
        [part_xproj.reshape(n_owner, n_x, inner), part_step.reshape(n_owner, n_s, inner)], axis=1
    )
    pad_rows = -(n_x + n_s) % 16
    part_small = jnp.pad(part_small, ((0, 0), (0, pad_rows), (0, 0))).astype(LOW)
    shard_small, _ = scatter(list(pick_rows(part_small, order).reshape(n_ctx, -1, inner)))
    shard_xproj = shard_small[:n_x]
    shard_step = shard_small[n_x : n_x + n_s]
    grad_table = in_order(tables)

    shard_in = jnp.stack([shard_conv, shard_gate], axis=1)
    matrices = (shard_in, shard_xproj, shard_step, shard_out)
    old_rows = (in_rows, xproj_rows, step_rows, out_rows)
    old_cols = (in_cols, xproj_cols, step_cols, out_cols)
    width_cols = (2 * E, E, E, E)
    width_rows = (D, R + 2 * N, R, D)
    squares = [matrix * matrix + square_floor for matrix in matrices]
    row_parts = [jnp.sum(square.reshape(square.shape[0], -1), axis=1) for square in squares]
    col_parts = [jnp.sum(square, axis=0).reshape(-1, inner) for square in squares]
    row_sums = butterfly(
        jnp.concatenate(row_parts + [weight_sq, in_order(gain_parts).reshape(-1)]), ("tensor",)
    )
    heights = [part.shape[0] for part in row_parts]
    ends = np.cumsum([0] + heights)
    n_rows = int(ends[-1])
    per_row = np.repeat((1.0 - decay_rate) / np.array(width_cols), heights).astype(np.float32)
    row_all = decay_rate * jnp.concatenate(old_rows) + per_row * row_sums[:n_rows]
    row_news = [row_all[ends[i] : ends[i + 1]] for i in range(4)]
    segment = (np.arange(4)[:, None] == np.repeat(np.arange(4), heights)[None]).astype(np.float32)
    gain_sums = row_sums[n_rows + 6 :].reshape(-1, inner)
    n_gain = gain_sums.shape[0]
    summed = butterfly(jnp.concatenate(col_parts + [gain_sums, grad_table], axis=0), own_axes)
    gain_grad = summed[5 : 5 + n_gain].reshape(n_owner, owned)
    owner = lax.axis_index("dp") * n_ctx + lax.axis_index("ctx")
    shard_gain = lax.dynamic_index_in_dim(gain_grad, owner, 0, False)
    col_sums = [summed[0:2], summed[2], summed[3], summed[4]]
    table_grad = summed[5 + n_gain :]
    col_news = [
        decay_rate * old_cols[i] + (1.0 - decay_rate) * col_sums[i] / width_rows[i]
        for i in range(4)
    ]
    every_second = decay_rate * pick(second_low, inverse_order) + (
        1.0 - decay_rate
    ) * (gain_grad * gain_grad + square_floor)
    every_update = gain_grad * lax.rsqrt(every_second)
    new_gain_second = lax.dynamic_index_in_dim(every_second, owner, 0, False)
    gain_update = lax.dynamic_index_in_dim(every_update, owner, 0, False)
    new_table_second = decay_rate * table_second + (1.0 - decay_rate) * (
        table_grad * table_grad + square_floor
    )
    table_update = table_grad * lax.rsqrt(new_table_second)
    inverse_cols = lax.rsqrt(jnp.concatenate([col.reshape(-1, inner) for col in col_news], axis=0))
    inverse_rows = lax.rsqrt(row_all)
    scaled_sq = update_squares(
        [shard_conv, shard_gate, shard_xproj, shard_step, shard_out],
        [inverse_rows[ends[i] : ends[i + 1]][:, None] for i in (0, 0, 1, 2, 3)],
        inverse_cols,
        table_update,
    )
    sums = jnp.concatenate(
        [
            jnp.sum(scaled_sq, axis=1) * shares,
            jnp.sum(segment * row_all[None], axis=1) / n_tensor,
            row_sums[n_rows : n_rows + 6] / n_tensor,
        ]
    )
    sums = butterfly(after(sums, token_first), own_axes + ("tensor",))
    row_means = sums[6:10] / np.array(width_rows, np.float32)
    total_weight = sums[10:]
    gain_sq = jnp.sum(every_update * every_update)
    counts = jnp.array([D, 2 * D * E, (R + 2 * N) * E, R * E, D * E, (K + 3 + N) * E], FULL)
    ones = jnp.ones((1,), FULL)
    means = jnp.concatenate([ones, row_means, ones])
    total_update = jnp.where(jnp.arange(6) == 0, gain_sq, sums[:6] * means)
    update_rms = jnp.sqrt(total_update / counts)
    factor = jnp.maximum(1.0, update_rms / clip_limit)
    scale = jnp.sqrt(total_weight / counts)
    stride = step_rate * scale / factor * jnp.sqrt(means)
    new_weights = [norm_gain - stride[0] * gain_update]
    for i in range(4):
        shape = (-1,) + (1,) * (matrices[i].ndim - 1)
        second = inverse_rows[ends[i] : ends[i + 1]].reshape(shape) * lax.rsqrt(col_news[i])[None]
        new_weights.append(weights[i] - stride[i + 1] * matrices[i] * second)
    new_weights.append(channel_table - stride[5] * table_update)
    return (
        mixed,
        token_grad,
        shard_gain,
        shard_in,
        shard_xproj,
        shard_step,
        shard_out,
        table_grad,
        new_weights[0],
        new_weights[1],
        new_weights[2],
        new_weights[3],
        new_weights[4],
        new_weights[5],
        new_gain_second,
        row_news[0],
        col_news[0],
        row_news[1],
        col_news[1],
        row_news[2],
        col_news[2],
        row_news[3],
        col_news[3],
        new_table_second,
        update_rms,
    )


def solution(mesh):
    rows = P(("dp", "ctx"))
    matrix = P(("dp", "ctx"), "tensor")
    cube = P(("dp", "ctx"), None, "tensor")
    table = P(None, "tensor")
    block = P(None, "dp", "ctx", None)
    cols = P("tensor")
    return jax.shard_map(
        per_device,
        mesh=mesh,
        in_specs=(block, block, rows, cube, matrix, matrix, matrix, table, rows)
        + (rows, table, rows, cols, rows, cols, rows, cols, table),
        out_specs=(block, block, rows, cube, matrix, matrix, matrix, table)
        + (rows, cube, matrix, matrix, matrix, table, rows)
        + (rows, table, rows, cols, rows, cols, rows, cols, table, P()),
        check_vma=False,
    )
```

```python
import functools
import math

import jax
import jax.numpy as jnp
import numpy as np
from jax import lax
from jax.experimental import pallas as pl
from jax.experimental.pallas import tpu as pltpu
from jax.sharding import PartitionSpec as P

D = 2048
E = 4096
N = 16
R = 128
K = 4
LANES = 128
LOG_2 = math.log(2.0)
LOW = jnp.bfloat16
FULL = jnp.float32

norm_epsilon = 1e-05
square_floor = 1e-30
decay_rate = 0.5
clip_limit = 0.5
step_rate = 1.0


def after(value, *others):
    return lax.optimization_barrier((value,) + others)[0]


def after_all(values, *others):
    return list(lax.optimization_barrier(tuple(values) + others)[: len(values)])


def vector(scalars):
    place = lax.iota(jnp.int32, len(scalars))
    return in_order([jnp.where(place == i, s, 0.0) for i, s in enumerate(scalars)])


def bits(axis):
    size = lax.axis_size(axis)
    return [1 << b for b in range(size.bit_length() - 1)]


def swap(block, axis, bit):
    return lax.ppermute(block, axis, [(i, i ^ bit) for i in range(lax.axis_size(axis))])


def shifted(block, axis, distance):
    devices = range(lax.axis_size(axis))
    route = [(i - distance, i) for i in devices if i - distance in devices]
    return lax.ppermute(block, axis, route)


def butterfly(value, axes):
    for axis in axes:
        for bit in bits(axis):
            value = value + swap(value, axis, bit)
    return value


def relative_blocks():
    n_dp, n_ctx = lax.axis_size("dp"), lax.axis_size("ctx")
    dp, ctx = lax.axis_index("dp"), lax.axis_index("ctx")
    return [
        (dp ^ (q % n_dp)) * n_ctx + (ctx ^ (q // n_dp)) for q in range(n_dp * n_ctx)
    ], [
        (ctx ^ (j % n_ctx)) * n_dp + (dp ^ (j // n_ctx)) for j in range(n_dp * n_ctx)
    ]


def pick(blocks, order):
    return jnp.stack([lax.dynamic_index_in_dim(blocks, q, 0, False) for q in order])


def fetch(own, release_far=()):
    if lax.axis_size("dp") != 4:
        blocks = [own]
        for bit in bits("dp"):
            blocks = blocks + [swap(block, "dp", bit) for block in blocks]
        return blocks
    half = own.shape[0] // 2
    one, two = after_all([swap(own, "dp", 1), swap(own, "dp", 2)], *release_far)
    far = [swap(two[:half], "dp", 1), swap(one[half:], "dp", 2)]
    return [own, one, two, jnp.concatenate(far, axis=0)]


def fetch_two(left, right, release_far, release_all):
    if lax.axis_size("dp") != 4:
        return fetch(left), fetch(right)
    left_one, left_two = swap(left, "dp", 1), swap(left, "dp", 2)
    right_one, right_two = swap(right, "dp", 1), swap(right, "dp", 2)
    left_far = swap(after(left_two, release_far), "dp", 1)
    right_far = swap(after(right_one, release_far), "dp", 2)
    left_far, right_far = after(left_far, *release_all), after(right_far, *release_all)
    return [left, left_one, left_two, left_far], [right, right_one, right_two, right_far]


def join(blocks):
    chunks = [jnp.concatenate(blocks, axis=0)]
    for bit in bits("ctx"):
        chunks = chunks + [swap(chunk, "ctx", bit) for chunk in chunks]
    return chunks


def scatter(chunks, release=()):
    for bit in reversed(bits("ctx")):
        half = len(chunks) // 2
        chunks = [
            (keep.astype(FULL) + swap(send, "ctx", bit).astype(FULL)).astype(LOW)
            for keep, send in zip(chunks[:half], chunks[half:])
        ]
    return scatter_dp(chunks[0], release), chunks[0]


def scatter_dp(chunk, release):
    n_dp = lax.axis_size("dp")
    parts = chunk.reshape(n_dp, -1, chunk.shape[-1])
    if n_dp == 4:
        half = parts.shape[2] // 2
        left, right = parts[:, :, :half], parts[:, :, half:]
        got = [swap(jnp.stack([left[1], left[3]]), "dp", 1), swap(right[2:], "dp", 2)]
        got_left, got_right = (g.astype(FULL) for g in after_all(got, *release))
        far_left = (left[2].astype(FULL) + got_left[1]).astype(LOW)
        far_right = (right[1].astype(FULL) + got_right[1]).astype(LOW)
        end_left = swap(far_left, "dp", 2).astype(FULL)
        end_right = swap(far_right, "dp", 1).astype(FULL)
        return jnp.concatenate(
            [
                left[0].astype(FULL) + got_left[0] + end_left,
                right[0].astype(FULL) + got_right[0] + end_right,
            ],
            axis=1,
        )
    for bit in reversed(bits("dp")):
        half = parts.shape[0] // 2
        parts = parts[:half].astype(FULL) + swap(parts[half:].astype(LOW), "dp", bit).astype(FULL)
    return parts[0].astype(FULL)


def line_scatter(part):
    return lax.psum_scatter(part, "tensor", scatter_dimension=0, tiled=True)


def line_gather(own):
    return lax.all_gather(own, "tensor", axis=0, tiled=True)


def tensor_total(term):
    return tensor_steps(term)[-2]


def tensor_first(term):
    low = term.astype(LOW)
    return low.astype(FULL) + swap(low, "tensor", 1).astype(FULL)


def tensor_rest(term):
    for bit in bits("tensor")[1:]:
        low = term.astype(LOW)
        term = low.astype(FULL) + swap(low, "tensor", bit).astype(FULL)
    return term


def tensor_steps(term):
    steps, sent = [], []
    for bit in bits("tensor"):
        low = term.astype(LOW)
        term = low.astype(FULL) + swap(low, "tensor", bit).astype(FULL)
        steps.append(term)
        sent.append(low)
    return steps + sent[:1]


def gather_few(row):
    return pick(gather_relative(row), relative_blocks()[1])


def gather_relative(row):
    for axis in ("dp", "ctx"):
        for bit in bits(axis):
            row = jnp.concatenate([row, swap(row, axis, bit)], axis=0)
    return row


def in_order(parts):
    total = parts[0]
    for part in parts[1:]:
        total = total + part
    return total


def spread(target, columns, place, rows, tile):
    target[pl.ds(place, rows, stride=tile), :] = columns


def columns_of(j):
    return slice(j * LANES, (j + 1) * LANES)


def edge_kernel(
    rows, groups, tile, unroll, flag, size_ref, value_ref, grad_ref, gate_ref, coef_ref, rate_ref,
    edge_ref, size_s, term_s,
):
    backward = flag[0] == 1

    @pl.when(pl.program_id(0) == 0)
    def _():
        edge_ref[...] = jnp.zeros_like(edge_ref)

    for j in range(tile):
        if j < groups:
            spread(size_s, size_ref[:, columns_of(j)], j, rows, tile)
        else:
            spread(size_s, jnp.zeros((rows, LANES), FULL), j, rows, tile)
            spread(term_s, jnp.zeros((rows, LANES), FULL), j, rows, tile)

    def loop(body):
        first = tuple(edge_ref[n] for n in range(N))
        last = lax.fori_loop(0, rows, body, first, unroll=unroll)
        for n in range(N):
            edge_ref[n] = last[n]

    @pl.when(jnp.logical_not(backward))
    def _():
        for j in range(groups):
            cut = columns_of(j)
            spread(term_s, size_ref[:, cut] * value_ref[:, cut].astype(FULL), j, rows, tile)

        def body(t, state):
            place = pl.ds(pl.multiple_of(t * tile, tile), tile)
            size, term = size_s[place, :], term_s[place, :]
            return tuple(
                jnp.exp2(size * rate_ref[n]) * state[n] + term * coef_ref[t, n]
                for n in range(N)
            )

        loop(body)

    @pl.when(backward)
    def _():
        for j in range(groups):
            cut = columns_of(j)
            gate = gate_ref[:, cut].astype(FULL)
            spread(term_s, grad_ref[:, cut] * gate * jax.nn.sigmoid(gate), j, rows, tile)

        def body(step, state):
            t = rows - 1 - step
            place = pl.ds(pl.multiple_of(t * tile, tile), tile)
            size, term = size_s[place, :], term_s[place, :]
            return tuple(
                jnp.exp2(size * rate_ref[n])
                * (state[n] + term * coef_ref[t, N + n])
                for n in range(N)
            )

        loop(body)


def forward_kernel(
    rows, groups, tile, part, unroll,
    size_ref, value_ref, grad_ref, gate_ref, coef_ref, rate_ref, start_ref, skip_ref,
    gated_ref, gate_grad_ref, before_ref, grad_c_ref, grad_skip_ref,
    size_s, input_s, grad_s, out_s, product_s, state_s, pick_s,
):
    @pl.when(pl.program_id(0) == 0)
    def _():
        state_s[...] = start_ref[...]
        set_picker(pick_s)
        grad_skip_ref[...] = jnp.zeros_like(grad_skip_ref)

    blank = jnp.zeros((rows, LANES), FULL)
    for j in range(tile):
        if j < groups:
            cut = columns_of(j)
            size = size_ref[:, cut]
            value = value_ref[:, cut].astype(FULL)
            gate = gate_ref[:, cut].astype(FULL)
            scan_grad = grad_ref[:, cut] * gate * jax.nn.sigmoid(gate)
            spread(size_s, size, j, rows, tile)
            spread(input_s, size * value, j, rows, tile)
            spread(grad_s, scan_grad, j, rows, tile)
            grad_skip_ref[:, cut] += jnp.sum(scan_grad * value, axis=0, keepdims=True)
        else:
            for target in (size_s, input_s, grad_s):
                spread(target, blank, j, rows, tile)
    for low in range(0, N, part):
        rate = [rate_ref[n] for n in range(low, low + part)]

        def body(t, state):
            state = list(state)
            place = pl.ds(pl.multiple_of(t * tile, tile), tile)
            size, term, grad = size_s[place, :], input_s[place, :], grad_s[place, :]
            out = None
            for k in range(part):
                n = low + k
                before_ref[t, n] = state[k]
                state[k] = (
                    jnp.exp2(size * rate[k]) * state[k] + term * coef_ref[t, n]
                )
                read = coef_ref[t, N + n] * state[k]
                out = read if out is None else out + read
                product_s[place, columns_of(n)] = state[k] * grad
            if low == 0:
                out_s[place, :] = out
            else:
                out_s[place, :] = out_s[place, :] + out
            return tuple(state)

        first = tuple(state_s[n] for n in range(low, low + part))
        last = lax.fori_loop(0, rows, body, first, unroll=unroll)
        for k in range(part):
            state_s[low + k] = last[k]
    for j in range(groups):
        cut = columns_of(j)
        scan_out = out_s[pl.ds(j, rows, stride=tile), :] + skip_ref[:, cut] * value_ref[
            :, cut
        ].astype(FULL)
        gate = gate_ref[:, cut].astype(FULL)
        sigma = jax.nn.sigmoid(gate)
        gated_ref[:, cut] = (scan_out * (gate * sigma)).astype(LOW)
        slope = sigma * (1.0 + gate * (1.0 - sigma))
        gate_grad_ref[:, cut] = (grad_ref[:, cut] * scan_out * slope).astype(LOW)
    sums = jnp.dot(product_s[...].astype(LOW), pick_s[...], preferred_element_type=FULL)
    grad_c_ref[...] = jnp.sum(sums.reshape(rows, tile, LANES), axis=1)


def backward_kernel(
    rows, groups, tile, part, unroll,
    size_ref, value_ref, grad_ref, gate_ref, coef_ref, rate_ref, tail_ref, skip_ref,
    before_ref,
    pre_low_ref, grad_value_ref, grad_b_ref, grad_rate_ref, grad_bias_ref,
    size_s, input_s, grad_s, along_s, rated_s, product_s, state_s, pick_s,
):
    @pl.when(pl.program_id(0) == 0)
    def _():
        state_s[...] = tail_ref[...]
        set_picker(pick_s)
        grad_rate_ref[...] = jnp.zeros_like(grad_rate_ref)
        grad_bias_ref[...] = jnp.zeros_like(grad_bias_ref)

    blank = jnp.zeros((rows, LANES), FULL)
    for j in range(tile):
        if j < groups:
            cut = columns_of(j)
            size = size_ref[:, cut]
            gate = gate_ref[:, cut].astype(FULL)
            spread(size_s, size, j, rows, tile)
            spread(input_s, size * value_ref[:, cut].astype(FULL), j, rows, tile)
            spread(grad_s, grad_ref[:, cut] * gate * jax.nn.sigmoid(gate), j, rows, tile)
        else:
            for target in (size_s, input_s, grad_s):
                spread(target, blank, j, rows, tile)
    for low in range(0, N, part):
        rate = [rate_ref[n] for n in range(low, low + part)]

        def body(step, carry):
            state, total = list(carry[0]), list(carry[1])
            t = rows - 1 - step
            place = pl.ds(pl.multiple_of(t * tile, tile), tile)
            size, term, grad = size_s[place, :], input_s[place, :], grad_s[place, :]
            along = rated = None
            for k in range(part):
                n = low + k
                adjoint = coef_ref[t, N + n] * grad + state[k]
                state[k] = jnp.exp2(size * rate[k]) * adjoint
                through = state[k] * before_ref[t, n]
                first = adjoint * coef_ref[t, n]
                second = through * rate[k]
                along = first if along is None else along + first
                rated = second if rated is None else rated + second
                total[k] = total[k] + through * size
                product_s[place, columns_of(n)] = adjoint * term
            if low == 0:
                along_s[place, :] = along
                rated_s[place, :] = rated
            else:
                along_s[place, :] = along_s[place, :] + along
                rated_s[place, :] = rated_s[place, :] + rated
            return tuple(state), tuple(total)

        place = range(low, low + part)
        first = (tuple(state_s[n] for n in place), tuple(grad_rate_ref[n] for n in place))
        state, total = lax.fori_loop(0, rows, body, first, unroll=unroll)
        for k in range(part):
            state_s[low + k] = state[k]
            grad_rate_ref[low + k] = total[k]
    for j in range(groups):
        cut = columns_of(j)
        size = size_ref[:, cut]
        along = along_s[pl.ds(j, rows, stride=tile), :]
        rated = rated_s[pl.ds(j, rows, stride=tile), :]
        grad_size = along * value_ref[:, cut].astype(FULL) + LOG_2 * rated
        grad_pre = grad_size * (jnp.tanh(0.5 * size) * (1.0 + jnp.exp(-size)))
        pre_low_ref[:, cut] = grad_pre.astype(LOW)
        grad_bias_ref[:, cut] += jnp.sum(grad_pre, axis=0, keepdims=True)
        scan_grad = grad_s[pl.ds(j, rows, stride=tile), :]
        grad_value_ref[:, cut] = along * size + skip_ref[:, cut] * scan_grad
    sums = jnp.dot(product_s[...].astype(LOW), pick_s[...], preferred_element_type=FULL)
    grad_b_ref[...] = jnp.sum(sums.reshape(rows, tile, LANES), axis=1)


def set_picker(pick_s):
    state = lax.broadcasted_iota(jnp.int32, pick_s.shape, 0) // LANES
    pick_s[...] = (state == lax.broadcasted_iota(jnp.int32, pick_s.shape, 1)).astype(LOW)


def tiles(channels):
    groups = channels // LANES
    return groups, 8 * pl.cdiv(groups, 8)


def tiled(table):
    groups, tile = tiles(table.shape[-1])
    table = table.reshape(table.shape[:-1] + (groups, LANES))
    pads = [(0, 0)] * (table.ndim - 2) + [(0, tile - groups), (0, 0)]
    return jnp.pad(table, pads)


def flat(table, channels):
    groups, _ = tiles(channels)
    return table[..., :groups, :].reshape(table.shape[:-2] + (channels,))


def cost(micro, length, ops, size):
    work = micro * length * N * 1024 * ops * 100
    return pl.CostEstimate(flops=work, bytes_accessed=size, transcendentals=0)


def limits():
    return pltpu.CompilerParams(vmem_limit_bytes=56 * 1024 * 1024)


def scan_edge(flag, size, value, grad, gate, coef, rate):
    length, channels = size.shape
    groups, tile = tiles(channels)
    rows = min(64, length)
    count = length // rows

    def place(i, f):
        return (jnp.where(f[0] == 0, i, count - 1 - i), 0)

    wide = pl.BlockSpec((rows, channels), place)
    cube = pl.BlockSpec((N, tile, LANES), lambda i, f: (0, 0, 0))
    return pl.pallas_call(
        functools.partial(edge_kernel, rows, groups, tile, 4),
        grid_spec=pltpu.PrefetchScalarGridSpec(
            num_scalar_prefetch=1,
            grid=(count,),
            in_specs=[wide] * 4
            + [pl.BlockSpec((rows, 2 * N), place, memory_space=pltpu.SMEM), cube],
            out_specs=cube,
            scratch_shapes=[pltpu.VMEM((rows * tile, LANES), FULL)] * 2,
        ),
        out_shape=jax.ShapeDtypeStruct((N, tile, LANES), FULL),
        compiler_params=limits(),
        cost_estimate=cost(1, length, 8, size.size * 12),
        name="scan_edge",
    )(flag, size, value, grad, gate, coef, rate)


def scan_forward(size, value, grad, gate, coef, rate, start, skip):
    length, channels = size.shape
    groups, tile = tiles(channels)
    rows = min(64, length)
    wide = pl.BlockSpec((rows, channels), lambda i: (i, 0))
    row = pl.BlockSpec((1, channels), lambda i: (0, 0))
    cube = pl.BlockSpec((N, tile, LANES), lambda i: (0, 0, 0))
    return pl.pallas_call(
        functools.partial(forward_kernel, rows, groups, tile, 8, 4),
        grid=(length // rows,),
        in_specs=[wide] * 4
        + [
            pl.BlockSpec((rows, 2 * N), lambda i: (i, 0), memory_space=pltpu.SMEM),
            cube,
            cube,
            row,
        ],
        out_specs=[
            wide,
            wide,
            pl.BlockSpec((rows, N, tile, LANES), lambda i: (i, 0, 0, 0)),
            pl.BlockSpec((rows, LANES), lambda i: (i, 0)),
            row,
        ],
        out_shape=[
            jax.ShapeDtypeStruct(size.shape, LOW),
            jax.ShapeDtypeStruct(size.shape, LOW),
            jax.ShapeDtypeStruct((length, N, tile, LANES), FULL),
            jax.ShapeDtypeStruct((length, LANES), FULL),
            jax.ShapeDtypeStruct((1, channels), FULL),
        ],
        scratch_shapes=[pltpu.VMEM((rows * tile, LANES), FULL)] * 4
        + [pltpu.VMEM((rows * tile, N * LANES), FULL), pltpu.VMEM((N, tile, LANES), FULL)]
        + [pltpu.VMEM((N * LANES, LANES), LOW)],
        compiler_params=limits(),
        cost_estimate=cost(1, length, 15, size.size * 80),
        name="scan_forward",
    )(size, value, grad, gate, coef, rate, start, skip)


def scan_backward(size, value, grad, gate, coef, rate, tail, skip, before):
    length, channels = size.shape
    groups, tile = tiles(channels)
    rows = min(64, length)
    last = length // rows - 1
    wide = pl.BlockSpec((rows, channels), lambda i: (last - i, 0))
    row = pl.BlockSpec((1, channels), lambda i: (0, 0))
    cube = pl.BlockSpec((N, tile, LANES), lambda i: (0, 0, 0))
    return pl.pallas_call(
        functools.partial(backward_kernel, rows, groups, tile, 8, 4),
        grid=(length // rows,),
        in_specs=[wide] * 4
        + [
            pl.BlockSpec((rows, 2 * N), lambda i: (last - i, 0), memory_space=pltpu.SMEM),
            cube,
            cube,
            row,
            pl.BlockSpec((rows, N, tile, LANES), lambda i: (last - i, 0, 0, 0)),
        ],
        out_specs=[wide, wide, pl.BlockSpec((rows, LANES), lambda i: (last - i, 0)), cube, row],
        out_shape=[
            jax.ShapeDtypeStruct(size.shape, LOW),
            jax.ShapeDtypeStruct(size.shape, FULL),
            jax.ShapeDtypeStruct((length, LANES), FULL),
            jax.ShapeDtypeStruct((N, tile, LANES), FULL),
            jax.ShapeDtypeStruct((1, channels), FULL),
        ],
        scratch_shapes=[pltpu.VMEM((rows * tile, LANES), FULL)] * 5
        + [pltpu.VMEM((rows * tile, N * LANES), FULL), pltpu.VMEM((N, tile, LANES), FULL)]
        + [pltpu.VMEM((N * LANES, LANES), LOW)],
        compiler_params=limits(),
        cost_estimate=cost(1, length, 20, size.size * 80),
        name="scan_backward",
    )(size, value, grad, gate, coef, rate, tail, skip, before)


def edges(size, value, grad, gate, coef, rate):
    count, place = lax.axis_size("ctx"), lax.axis_index("ctx")
    args = (size, value, grad, gate, coef, rate)
    if count == 2:
        edge = scan_edge(place.astype(jnp.int32)[None], *args)
        other = swap(edge, "ctx", 1)
        return jnp.where(place == 1, other, 0.0), jnp.where(place == 0, other, 0.0)
    last = scan_edge(jnp.zeros((1,), jnp.int32), *args)
    head = scan_edge(jnp.ones((1,), jnp.int32), *args)
    through = jnp.exp2(rate * tiled(jnp.sum(size, axis=0, keepdims=True)))
    lasts, heads, throughs = (lax.all_gather(a, "ctx") for a in (last, head, through))
    start = tail = jnp.zeros(last.shape, FULL)
    for i in range(count):
        start = jnp.where(i < place, throughs[i] * start + lasts[i], start)
        j = count - 1 - i
        tail = jnp.where(j > place, throughs[j] * tail + heads[j], tail)
    return start, tail


def block_of(index, width):
    return pl.ds(pl.multiple_of(index * width, width), width)


def normalize_kernel(width, chunks, order, x_ref, grad_ref, gain_ref, *outs):
    x = x_ref[...].astype(FULL)
    inverse = lax.rsqrt(jnp.mean(x * x, axis=1, keepdims=True) + norm_epsilon)
    columns = D // chunks
    for chunk in range(chunks):
        for low in range(0, columns, width):
            q = (chunk * columns + low) // width
            source = block_of(order[q], width)
            place = slice(low, low + width)
            value = x_ref[:, source].astype(FULL) * inverse * gain_ref[q : q + 1, :]
            outs[chunk][:, place] = value.astype(LOW)
            outs[chunks + chunk][:, place] = grad_ref[:, source]


def normalize(order, m, length, x, grad, gain, n_ctx):
    height, width = length, D // len(order)
    if width % LANES:
        x, grad = x[m * length : (m + 1) * length], grad[m * length : (m + 1) * length]
        full = x.astype(FULL)
        inverse = lax.rsqrt(jnp.mean(full * full, axis=1, keepdims=True) + norm_epsilon)

        def arrange(array):
            blocks = jnp.swapaxes(array.reshape(height, len(order), width), 0, 1)
            blocks = pick(blocks, order).reshape(n_ctx, -1, height, width)
            return list(jnp.swapaxes(blocks, 1, 2).reshape(n_ctx, height, D // n_ctx))

        gain = pick(gain, inverse_of(order))
        return arrange((full * inverse * gain.reshape(1, D)).astype(LOW)), arrange(grad)
    rows = min(128, height)
    wide = pl.BlockSpec((rows, D), lambda i, o: (m * (length // rows) + i, 0))
    out = pl.BlockSpec((rows, D // n_ctx), lambda i, o: (i, 0))
    shape = jax.ShapeDtypeStruct((height, D // n_ctx), LOW)
    outs = pl.pallas_call(
        functools.partial(normalize_kernel, width, n_ctx),
        grid_spec=pltpu.PrefetchScalarGridSpec(
            num_scalar_prefetch=1,
            grid=(height // rows,),
            in_specs=[wide, wide, pl.BlockSpec((len(order), width), lambda i, o: (0, 0))],
            out_specs=[out] * (2 * n_ctx),
        ),
        out_shape=[shape] * (2 * n_ctx),
        compiler_params=limits(),
        name="normalize",
    )(jnp.stack(order).astype(jnp.int32), x, grad, gain)
    return outs[:n_ctx], outs[n_ctx:]


def inverse_of(order):
    return relative_blocks()[1]


def unpermuted(chunks, inverse_order):
    rows, width = jnp.concatenate(chunks, axis=1), D // len(inverse_order)
    return jnp.concatenate(
        [lax.dynamic_slice_in_dim(rows, q * width, width, 1) for q in inverse_order], axis=1
    )


def own_block(block, share):
    return pl.BlockSpec((share, D), lambda i, o: (o[block], 0))


def whole_of(array):
    return pl.BlockSpec(array.shape, lambda i, o: (0,) * array.ndim)


def mix_kernel(width, per_chunk, order, x_ref, branch_ref, out_ref):
    for q in range(D // width):
        place = block_of(order[q], width)
        value = branch_ref[:, q * width : (q + 1) * width].astype(FULL)
        out_ref[:, place] = (x_ref[:, place].astype(FULL) + value).astype(LOW)


def mix(order, block, x, branch):
    width, share = D // len(order), branch.shape[0]
    if width % LANES:
        x = lax.dynamic_slice_in_dim(x, block * share, share, 0)
        return (x.astype(FULL) + unpermuted([branch.astype(FULL)], inverse_of(order))).astype(LOW)
    return pl.pallas_call(
        functools.partial(mix_kernel, width, 0),
        grid_spec=pltpu.PrefetchScalarGridSpec(
            num_scalar_prefetch=1,
            grid=(1,),
            in_specs=[own_block(len(order), share), whole_of(branch)],
            out_specs=whole_of(branch),
        ),
        out_shape=jax.ShapeDtypeStruct((share, D), LOW),
        compiler_params=limits(),
        name="mix",
    )(jnp.stack(order + [block]).astype(jnp.int32), x, branch)


def token_kernel(width, order, x_ref, grad_ref, gain_ref, normed_ref, out_ref, gain_out_ref, scaled_s):
    x = x_ref[...].astype(FULL)
    inverse = lax.rsqrt(jnp.mean(x * x, axis=1, keepdims=True) + norm_epsilon)
    total = jnp.zeros_like(inverse)
    for q in range(D // width):
        place = block_of(order[q], width)
        value = normed_ref[:, q * width : (q + 1) * width].astype(FULL)
        part = x_ref[:, place].astype(FULL)
        gain_out_ref[pl.ds(order[q], 1), :] = jnp.sum(
            value * part * inverse, axis=0, keepdims=True
        )
        scaled = value * gain_ref[q : q + 1, :]
        total = total + jnp.sum(part * scaled, axis=1, keepdims=True)
        scaled_s[:, place] = scaled
    slope = inverse * inverse * inverse * (total / D)
    out_ref[...] = (
        grad_ref[...].astype(FULL) + inverse * scaled_s[...] - x * slope
    ).astype(LOW)


def token_rows(order, block, x, grad, gain, normed):
    width, share = D // len(order), normed.shape[0]
    if width % LANES:
        x = lax.dynamic_slice_in_dim(x, block * share, share, 0).astype(FULL)
        grad = lax.dynamic_slice_in_dim(grad, block * share, share, 0).astype(FULL)
        value = unpermuted([normed.astype(FULL)], inverse_of(order))
        inverse = lax.rsqrt(jnp.mean(x * x, axis=1, keepdims=True) + norm_epsilon)
        part = jnp.sum(value * x * inverse, axis=0).reshape(len(order), width)
        scaled = value * pick(gain, inverse_of(order)).reshape(1, D)
        slope = inverse * inverse * inverse * jnp.mean(x * scaled, axis=1, keepdims=True)
        return (grad + inverse * scaled - x * slope).astype(LOW), part
    wide = own_block(len(order), share)
    return pl.pallas_call(
        functools.partial(token_kernel, width),
        grid_spec=pltpu.PrefetchScalarGridSpec(
            num_scalar_prefetch=1,
            grid=(1,),
            in_specs=[wide, wide, whole_of(gain), whole_of(normed)],
            out_specs=[whole_of(normed), whole_of(gain)],
            scratch_shapes=[pltpu.VMEM((share, D), FULL)],
        ),
        out_shape=[
            jax.ShapeDtypeStruct((share, D), LOW),
            jax.ShapeDtypeStruct((len(order), width), FULL),
        ],
        compiler_params=limits(),
        name="token_rows",
    )(jnp.stack(order + [block]).astype(jnp.int32), x, grad, gain, normed)


def update_kernel(owners, *refs):
    n = len(owners)
    grads, scales, cols_ref, table_ref, out_ref = refs[:n], refs[n : 2 * n], *refs[2 * n :]
    out_ref[...] = jnp.zeros_like(out_ref)

    def lanes(squares):
        total = jnp.sum(squares, axis=0, keepdims=True)
        cuts = [total[:, columns_of(j)] for j in range(total.shape[1] // LANES)]
        return in_order(cuts)

    for i, owner in enumerate(owners):
        update = grads[i][...] * scales[i][...] * cols_ref[i : i + 1, :]
        out_ref[owner : owner + 1, :] += lanes(update * update)
    out_ref[5:6, :] = lanes(table_ref[...] * table_ref[...])


def update_squares(grads, scales, cols, table):
    return pl.pallas_call(
        functools.partial(update_kernel, (1, 1, 2, 3, 4)),
        out_shape=jax.ShapeDtypeStruct((6, LANES), FULL),
        compiler_params=limits(),
        name="update_squares",
    )(*grads, *scales, cols, table)


def pick_kernel(order, blocks_ref, out_ref):
    for j in range(blocks_ref.shape[0]):
        out_ref[j] = blocks_ref[order[j]]


def pick_rows(blocks, order):
    return pl.pallas_call(
        pick_kernel,
        in_specs=[pl.BlockSpec(memory_space=pltpu.SMEM), pl.BlockSpec(memory_space=pltpu.VMEM)],
        out_specs=pl.BlockSpec(memory_space=pltpu.VMEM),
        out_shape=jax.ShapeDtypeStruct(blocks.shape, blocks.dtype),
        compiler_params=limits(),
        name="pick_rows",
    )(jnp.stack(order).astype(jnp.int32), blocks)


def fill_kernel(part_ref, *refs):
    refs[-1][...] = part_ref[...]


def fill(whole, count, m, part):
    height, columns = part.shape
    rows = min(256, height)
    spec = pl.BlockSpec((None, rows, columns), lambda i: (m, i, 0))
    kept = [] if whole is None else [whole]
    return pl.pallas_call(
        fill_kernel,
        grid=(height // rows,),
        in_specs=[pl.BlockSpec((rows, columns), lambda i: (i, 0))]
        + [pl.BlockSpec(memory_space=pl.ANY)] * len(kept),
        out_specs=spec,
        out_shape=jax.ShapeDtypeStruct((count, height, columns), part.dtype),
        input_output_aliases={1: 0} if kept else {},
        compiler_params=limits(),
        name="fill",
    )(part, *kept)


def conv_kernel(
    value_grad_ref, proj_ref, xproj_ref, conv_in_ref, earlier_ref, table_ref,
    out_ref, last_ref, head_ref, sums_ref, padded_s, grad_s,
):
    length = conv_in_ref.shape[0]
    taps = [table_ref[k : k + 1, :] for k in range(K)]
    padded_s[pl.ds(0, 8), :] = earlier_ref[...].astype(FULL)
    padded_s[pl.ds(8, length), :] = conv_in_ref[...].astype(FULL)
    conv = table_ref[K : K + 1, :] + taps[0] * padded_s[pl.ds(9 - K, length), :]
    for k in range(1, K):
        conv = conv + taps[k] * padded_s[pl.ds(9 - K + k, length), :]
    sigma = jax.nn.sigmoid(conv)
    slope = sigma * (1.0 + conv * (1.0 - sigma))
    grad_values = value_grad_ref[...] + jnp.dot(
        proj_ref[...], xproj_ref[...], preferred_element_type=FULL
    )
    grad_conv = grad_values * slope
    grad_s[pl.ds(0, length), :] = grad_conv
    grad_s[pl.ds(length, 8), :] = jnp.zeros((8, grad_conv.shape[1]), FULL)
    for k in range(K):
        sums_ref[k : k + 1, :] = jnp.sum(
            grad_conv * padded_s[pl.ds(9 - K + k, length), :], axis=0, keepdims=True
        )
    sums_ref[K : K + 1, :] = jnp.sum(grad_conv, axis=0, keepdims=True)
    sums_ref[K + 1 :, :] = jnp.zeros((7 - K, grad_conv.shape[1]), FULL)
    total = taps[K - 1] * grad_conv
    for k in range(K - 1):
        total = total + taps[k] * grad_s[pl.ds(K - 1 - k, length), :]
    out_ref[...] = total.astype(LOW)
    last_ref[...] = total[length - 8 :]
    head_ref[...] = jnp.zeros_like(head_ref)
    for p in range(K - 1):
        row = taps[0] * grad_s[pl.ds(p, 1), :]
        for k in range(1, p + 1):
            row = row + taps[k] * grad_s[pl.ds(p - k, 1), :]
        head_ref[9 - K + p : 10 - K + p, :] = row


def conv_backward(value_grad, proj_grad, xproj_low, conv_in, earlier, table):
    length, channels = value_grad.shape
    width = min(256, channels)
    tall = pl.BlockSpec((length, width), lambda j: (0, j))
    short = pl.BlockSpec((8, width), lambda j: (0, j))
    few = jax.ShapeDtypeStruct((8, channels), FULL)
    return pl.pallas_call(
        conv_kernel,
        grid=(channels // width,),
        in_specs=[
            tall,
            pl.BlockSpec(proj_grad.shape, lambda j: (0, 0)),
            pl.BlockSpec((proj_grad.shape[1], width), lambda j: (0, j)),
            tall,
            short,
            pl.BlockSpec((8, width), lambda j: (0, j)),
        ],
        out_specs=[tall, short, short, short],
        out_shape=[jax.ShapeDtypeStruct((length, channels), LOW), few, few, few],
        scratch_shapes=[pltpu.VMEM((length + 8, width), FULL)] * 2,
        compiler_params=limits(),
        name="conv_backward",
    )(value_grad, proj_grad, xproj_low, conv_in, earlier, table)


def dot(a, b, dims, kind=FULL):
    return lax.dot_general(a, b, (dims, ((), ())), preferred_element_type=FULL).astype(kind)


def per_device(
    tokens,
    out_grad,
    norm_gain,
    in_weight,
    xproj_weight,
    step_weight,
    outproj_weight,
    channel_table,
    gain_second,
    in_rows,
    in_cols,
    xproj_rows,
    xproj_cols,
    step_rows,
    step_cols,
    out_rows,
    out_cols,
    table_second,
):
    micro = tokens.shape[0]
    length = tokens.shape[2]
    inner = in_weight.shape[2]
    n_tensor = lax.axis_size("tensor")
    n_owner = lax.axis_size("dp") * lax.axis_size("ctx")
    owned = in_weight.shape[0]
    order, inverse_order = relative_blocks()
    n_ctx = lax.axis_size("ctx")
    own_axes = ("ctx", "dp")
    me = lax.axis_index("tensor")

    n_x, n_s = xproj_weight.shape[0], step_weight.shape[0]
    every = range(micro)
    tokens_flat = tokens.reshape(micro * length, D)
    grad_flat = out_grad.reshape(micro * length, D)
    gain_rounded = after(norm_gain.astype(LOW), gain_second).astype(FULL)
    gain_row = jnp.stack([gain_rounded, gain_second])[None]
    for bit in bits("dp"):
        gain_row = jnp.concatenate([gain_row, swap(gain_row, "dp", bit)], axis=0)
    gain_low = gain_row
    for bit in bits("ctx"):
        gain_low = jnp.concatenate([gain_low, swap(gain_low, "ctx", bit)], axis=0)
    gain_low, second_low = gain_low[:, 0], gain_low[:, 1]
    normed, grad_rel = zip(
        *(normalize(order, m, length, tokens_flat, grad_flat, gain_low, n_ctx) for m in every)
    )
    normed, grad_rel = list(normed), list(grad_rel)
    in_own = in_weight.reshape(owned, 2 * inner).astype(LOW)
    first_own = [in_own[:, :inner], xproj_weight.astype(LOW), step_weight.astype(LOW)]
    pad_rows = -(owned + n_x + n_s) % 64
    if pad_rows:
        first_own.append(jnp.zeros((pad_rows, inner), LOW))
    blocks = fetch(after(jnp.concatenate(first_own, axis=0), gain_row), [n[0] for n in normed])
    conv_low = join([block[:owned] for block in blocks])
    small = jnp.concatenate(join([block[owned:] for block in blocks]), axis=0)
    small = pick_rows(small.reshape(n_owner, -1, inner), inverse_order)
    xproj_low = small[:, :n_x].reshape(n_owner * n_x, inner)
    step_low = small[:, n_x : n_x + n_s].reshape(n_owner * n_s, inner)
    gate_own, out_own = in_own[:, inner:], outproj_weight.astype(LOW)

    taps = channel_table[:K]
    conv_bias = channel_table[K]
    step_bias = channel_table[K + 1]
    skip = channel_table[K + 2][None]
    a_neg = -jnp.exp(channel_table[K + 3 :])
    rate = tiled(a_neg / LOG_2)

    def contract(parts, weights):
        total = dot(parts[0], weights[0], ((1,), (0,)))
        for part, weight in zip(parts[1:], weights[1:]):
            total = total + dot(part, weight, ((1,), (0,)))
        return total

    conv_in, earlier, values, part_proj, proj_steps = [], [], [], [], []
    for m in every:
        parts = normed[m] if m == 0 else after_all(normed[m], proj_steps[-1][-1])
        conv_in.append(contract(parts, conv_low).astype(LOW))
        earlier.append(shifted(conv_in[m][length - 8 :], "ctx", 1))
        padded = jnp.concatenate([earlier[m], conv_in[m]], axis=0).astype(FULL)
        conv = conv_bias + taps[0] * padded[9 - K : 9 - K + length]
        for k in range(1, K):
            conv = conv + taps[k] * padded[9 - K + k : 9 - K + k + length]
        values.append(jax.nn.silu(conv).astype(LOW))
        part_proj.append(dot(values[m], xproj_low, ((1,), (1,))))
        proj_steps.append(tensor_steps(part_proj[m]))
    gate_blocks, out_blocks = fetch_two(gate_own, out_own, conv_in[0], proj_steps[0][:1])
    gate_low, out_low = join(gate_blocks), join(out_blocks)
    weights = (in_weight, xproj_weight, step_weight, outproj_weight)
    all_weights = [norm_gain] + list(weights) + [channel_table]
    shares = jnp.array([1.0 / n_tensor, 1.0, 1.0, 1.0, 1.0, 1.0 / n_owner], FULL)
    gate_in, grad_gated, size, coef, rank_low, own_mixed, mixed = [], [], [], [], [], [], []
    gated, gate_grad, before, grad_c, grad_skip, tail, branch = [], [], [], [], [], [], []
    for m in every:
        proj = proj_steps[m][-2]
        rank_low.append(proj[:, :R].astype(LOW))
        coef.append(proj[:, R:])
        now_low, now_rel, now_normed = rank_low[m], grad_rel[m], normed[m]
        if m > 0:
            now_low = after(now_low, branch[-1])
            now_rel, now_normed = after_all(now_rel, branch[-1]), after_all(now_normed, branch[-1])
        pre = dot(now_low, step_low, ((1,), (0,))) + step_bias
        size.append(jax.nn.softplus(pre))
        gate_in.append(contract(now_normed, gate_low).astype(LOW))
        grad_gated.append(contract(now_rel, out_low))
        args = (size[m], values[m], grad_gated[m], gate_in[m], coef[m], rate)
        entering, leaving = edges(*args)
        tail.append(leaving)
        outs = scan_forward(*args, entering, skip)
        for held, out in zip((gated, gate_grad, before, grad_c, grad_skip), outs):
            held.append(out)
        branch.append(
            jnp.concatenate([dot(gated[m], w, ((1,), (1,)), LOW) for w in out_low], axis=1)
        )
        own_mixed.append(mix(order, m * n_tensor + me, tokens_flat, line_scatter(branch[m])))

    def over_micros(left, right):
        total = dot(left[0], right[0], ((0,), (0,)))
        for a, b in zip(left[1:], right[1:]):
            total = total + dot(a, b, ((0,), (0,)))
        return total

    def chunks_of(parts):
        return list(zip(*parts))

    backs, parts, first_of, gate_parts, part_out = [], [], [], [], []
    for m in every:
        leaving = after(tail[m], branch[-1], own_mixed[0])
        if m > 0:
            leaving = after(leaving, first_of[0], *part_out, *gate_parts[0], *own_mixed)
        pre_low, value_grad, grad_b, grad_rate, grad_bias = scan_backward(
            size[m], values[m], grad_gated[m], gate_in[m], coef[m], rate, leaving, skip, before[m]
        )
        backs.append((pre_low, value_grad, grad_rate, grad_bias))
        grad_rank = dot(pre_low, step_low, ((1,), (1,)))
        parts.append(jnp.concatenate([grad_rank, grad_b[:, :N], grad_c[m][:, :N]], axis=1))
        first_of.append(tensor_first(parts[m]))
        if m == 0:
            for side in chunks_of(grad_rel):
                part_out.append(over_micros(after_all(side, parts[0]), gated).astype(LOW))
            gate_grad_then = after(gate_grad[0], parts[0], *own_mixed)
            gate_parts.append([dot(gate_grad_then, g, ((1,), (1,))) for g in gate_low])
    mixed = [line_gather(own_mixed[0])]
    pre_lows = [back[0] for back in backs]
    conv_grads, proj_grads, gain_parts, tables, partial, tokens_out = [], [], [], [], [], []
    part_gate, totals = [], [tensor_rest(first_of[0])]
    for m in every:
        _, value_grad, grad_rate, grad_bias = backs[m]
        proj_grad = totals[m].astype(LOW)
        proj_grads.append(proj_grad)
        wait_for = [mixed[0], parts[-1]]
        if m > 0:
            started = [partial[0], first_of[m]]
            gate_grad_then = after(gate_grad[m], *started)
            gate_parts.append([dot(gate_grad_then, g, ((1,), (1,))) for g in gate_low])
            if m == micro - 1:
                for c, side in enumerate(chunks_of(normed)):
                    arrived = started + [totals[m]] if c else started
                    part_gate.append(over_micros(after_all(side, *arrived), gate_grad).astype(LOW))
            wait_for = wait_for + gate_parts[m] + part_gate
        conv_grad, last, head, sums = conv_backward(
            after(value_grad, *wait_for),
            proj_grad, xproj_low, conv_in[m], earlier[m], channel_table[:8],
        )
        last = last + shifted(head, "ctx", -1)
        conv_grad = lax.dynamic_update_slice(conv_grad, last.astype(LOW), (length - 8, 0))
        if m == 0:
            totals = totals + [tensor_rest(after(first, sums)) for first in first_of[1:]]
        conv_grads.append(conv_grad)
        partial.append(
            jnp.concatenate(
                [
                    (g + dot(conv_grad, c, ((1,), (1,)))).astype(LOW)
                    for g, c in zip(gate_parts[m], conv_low)
                ],
                axis=1,
            )
        )
        sent = after(partial[m], totals[-1])
        token, gain_part = token_rows(
            order, m * n_tensor + me, tokens_flat, grad_flat, gain_low, line_scatter(sent)
        )
        gain_parts.append(gain_part)
        tokens_out.append(token)
        rates = flat(grad_rate, inner) * a_neg
        tables.append(jnp.concatenate([sums[: K + 1], grad_bias, grad_skip[m], rates], axis=0))
    normed_then = [after_all(sides, partial[-1]) for sides in normed]
    part_conv = [over_micros(g, conv_grads).astype(LOW) for g in chunks_of(normed_then)]
    shard_conv, middle = scatter(part_conv)
    shard_out, _ = scatter(part_out, [middle])
    shard_gate, _ = scatter(part_gate, [middle])
    weight_sq = vector([jnp.sum(jnp.square(after(w, middle))) for w in all_weights]) * shares
    mixed = mixed + [line_gather(after(own, partial[-1])) for own in own_mixed[1:]]
    whole_mixed = token_grad = None
    for m in every:
        whole_mixed = fill(whole_mixed, micro, m, after(mixed[m], middle))
        token_grad = fill(token_grad, micro, m, line_gather(tokens_out[m]))
        token_first = token_grad if m == 0 else token_first
    mixed = whole_mixed.reshape(tokens.shape)
    token_grad = token_grad.reshape(tokens.shape)
    pre_lows, proj_grads = after_all(pre_lows, middle), after_all(proj_grads, middle)
    part_step = over_micros(rank_low, pre_lows)
    part_xproj = over_micros(proj_grads, values)
    part_small = jnp.concatenate(
        [part_xproj.reshape(n_owner, n_x, inner), part_step.reshape(n_owner, n_s, inner)], axis=1
    )
    pad_rows = -(n_x + n_s) % 16
    part_small = jnp.pad(part_small, ((0, 0), (0, pad_rows), (0, 0))).astype(LOW)
    shard_small, _ = scatter(list(pick_rows(part_small, order).reshape(n_ctx, -1, inner)))
    shard_xproj = shard_small[:n_x]
    shard_step = shard_small[n_x : n_x + n_s]
    grad_table = in_order(tables)

    shard_in = jnp.stack([shard_conv, shard_gate], axis=1)
    matrices = (shard_in, shard_xproj, shard_step, shard_out)
    old_rows = (in_rows, xproj_rows, step_rows, out_rows)
    old_cols = (in_cols, xproj_cols, step_cols, out_cols)
    width_cols = (2 * E, E, E, E)
    width_rows = (D, R + 2 * N, R, D)
    squares = [matrix * matrix + square_floor for matrix in matrices]
    row_parts = [jnp.sum(square.reshape(square.shape[0], -1), axis=1) for square in squares]
    col_parts = [jnp.sum(square, axis=0).reshape(-1, inner) for square in squares]
    row_sums = butterfly(
        jnp.concatenate(row_parts + [weight_sq, in_order(gain_parts).reshape(-1)]), ("tensor",)
    )
    heights = [part.shape[0] for part in row_parts]
    ends = np.cumsum([0] + heights)
    n_rows = int(ends[-1])
    per_row = np.repeat((1.0 - decay_rate) / np.array(width_cols), heights).astype(np.float32)
    row_all = decay_rate * jnp.concatenate(old_rows) + per_row * row_sums[:n_rows]
    row_news = [row_all[ends[i] : ends[i + 1]] for i in range(4)]
    segment = (np.arange(4)[:, None] == np.repeat(np.arange(4), heights)[None]).astype(np.float32)
    gain_sums = row_sums[n_rows + 6 :].reshape(-1, inner)
    n_gain = gain_sums.shape[0]
    summed = butterfly(jnp.concatenate(col_parts + [gain_sums, grad_table], axis=0), own_axes)
    gain_grad = summed[5 : 5 + n_gain].reshape(n_owner, owned)
    owner = lax.axis_index("dp") * n_ctx + lax.axis_index("ctx")
    shard_gain = lax.dynamic_index_in_dim(gain_grad, owner, 0, False)
    col_sums = [summed[0:2], summed[2], summed[3], summed[4]]
    table_grad = summed[5 + n_gain :]
    col_news = [
        decay_rate * old_cols[i] + (1.0 - decay_rate) * col_sums[i] / width_rows[i]
        for i in range(4)
    ]
    every_second = decay_rate * pick(second_low, inverse_order) + (
        1.0 - decay_rate
    ) * (gain_grad * gain_grad + square_floor)
    every_update = gain_grad * lax.rsqrt(every_second)
    new_gain_second = lax.dynamic_index_in_dim(every_second, owner, 0, False)
    gain_update = lax.dynamic_index_in_dim(every_update, owner, 0, False)
    new_table_second = decay_rate * table_second + (1.0 - decay_rate) * (
        table_grad * table_grad + square_floor
    )
    table_update = table_grad * lax.rsqrt(new_table_second)
    inverse_cols = lax.rsqrt(jnp.concatenate([col.reshape(-1, inner) for col in col_news], axis=0))
    inverse_rows = lax.rsqrt(row_all)
    scaled_sq = update_squares(
        [shard_conv, shard_gate, shard_xproj, shard_step, shard_out],
        [inverse_rows[ends[i] : ends[i + 1]][:, None] for i in (0, 0, 1, 2, 3)],
        inverse_cols,
        table_update,
    )
    sums = jnp.concatenate(
        [
            jnp.sum(scaled_sq, axis=1) * shares,
            jnp.sum(segment * row_all[None], axis=1) / n_tensor,
            row_sums[n_rows : n_rows + 6] / n_tensor,
        ]
    )
    sums = butterfly(after(sums, token_first), own_axes + ("tensor",))
    row_means = sums[6:10] / np.array(width_rows, np.float32)
    total_weight = sums[10:]
    gain_sq = jnp.sum(every_update * every_update)
    counts = jnp.array([D, 2 * D * E, (R + 2 * N) * E, R * E, D * E, (K + 3 + N) * E], FULL)
    ones = jnp.ones((1,), FULL)
    means = jnp.concatenate([ones, row_means, ones])
    total_update = jnp.where(jnp.arange(6) == 0, gain_sq, sums[:6] * means)
    update_rms = jnp.sqrt(total_update / counts)
    factor = jnp.maximum(1.0, update_rms / clip_limit)
    scale = jnp.sqrt(total_weight / counts)
    stride = step_rate * scale / factor * jnp.sqrt(means)
    new_weights = [norm_gain - stride[0] * gain_update]
    for i in range(4):
        shape = (-1,) + (1,) * (matrices[i].ndim - 1)
        second = inverse_rows[ends[i] : ends[i + 1]].reshape(shape) * lax.rsqrt(col_news[i])[None]
        new_weights.append(weights[i] - stride[i + 1] * matrices[i] * second)
    new_weights.append(channel_table - stride[5] * table_update)
    return (
        mixed,
        token_grad,
        shard_gain,
        shard_in,
        shard_xproj,
        shard_step,
        shard_out,
        table_grad,
        new_weights[0],
        new_weights[1],
        new_weights[2],
        new_weights[3],
        new_weights[4],
        new_weights[5],
        new_gain_second,
        row_news[0],
        col_news[0],
        row_news[1],
        col_news[1],
        row_news[2],
        col_news[2],
        row_news[3],
        col_news[3],
        new_table_second,
        update_rms,
    )


def solution(mesh):
    rows = P(("dp", "ctx"))
    matrix = P(("dp", "ctx"), "tensor")
    cube = P(("dp", "ctx"), None, "tensor")
    table = P(None, "tensor")
    block = P(None, "dp", "ctx", None)
    cols = P("tensor")
    return jax.shard_map(
        per_device,
        mesh=mesh,
        in_specs=(block, block, rows, cube, matrix, matrix, matrix, table, rows)
        + (rows, table, rows, cols, rows, cols, rows, cols, table),
        out_specs=(block, block, rows, cube, matrix, matrix, matrix, table)
        + (rows, cube, matrix, matrix, matrix, table, rows)
        + (rows, table, rows, cols, rows, cols, rows, cols, table, P()),
        check_vma=False,
    )
```

```python
import functools
import math

import jax
import jax.numpy as jnp
import numpy as np
from jax import lax
from jax.experimental import pallas as pl
from jax.experimental.pallas import tpu as pltpu
from jax.sharding import PartitionSpec as P

D = 2048
E = 4096
N = 16
R = 128
K = 4
LANES = 128
LOG_2 = math.log(2.0)
LOW = jnp.bfloat16
FULL = jnp.float32

norm_epsilon = 1e-05
square_floor = 1e-30
decay_rate = 0.5
clip_limit = 0.5
step_rate = 1.0


def after(value, *others):
    return lax.optimization_barrier((value,) + others)[0]


def after_all(values, *others):
    return list(lax.optimization_barrier(tuple(values) + others)[: len(values)])


def vector(scalars):
    place = lax.iota(jnp.int32, len(scalars))
    return in_order([jnp.where(place == i, s, 0.0) for i, s in enumerate(scalars)])


def bits(axis):
    size = lax.axis_size(axis)
    return [1 << b for b in range(size.bit_length() - 1)]


def swap(block, axis, bit):
    return lax.ppermute(block, axis, [(i, i ^ bit) for i in range(lax.axis_size(axis))])


def shifted(block, axis, distance):
    devices = range(lax.axis_size(axis))
    route = [(i - distance, i) for i in devices if i - distance in devices]
    return lax.ppermute(block, axis, route)


def butterfly(value, axes):
    for axis in axes:
        for bit in bits(axis):
            value = value + swap(value, axis, bit)
    return value


def relative_blocks():
    n_dp, n_ctx = lax.axis_size("dp"), lax.axis_size("ctx")
    dp, ctx = lax.axis_index("dp"), lax.axis_index("ctx")
    return [
        (dp ^ (q % n_dp)) * n_ctx + (ctx ^ (q // n_dp)) for q in range(n_dp * n_ctx)
    ], [
        (ctx ^ (j % n_ctx)) * n_dp + (dp ^ (j // n_ctx)) for j in range(n_dp * n_ctx)
    ]


def pick(blocks, order):
    return jnp.stack([lax.dynamic_index_in_dim(blocks, q, 0, False) for q in order])


def fetch(own, release_far=()):
    if lax.axis_size("dp") != 4:
        blocks = [own]
        for bit in bits("dp"):
            blocks = blocks + [swap(block, "dp", bit) for block in blocks]
        return blocks
    half = own.shape[0] // 2
    one, two = after_all([swap(own, "dp", 1), swap(own, "dp", 2)], *release_far)
    far = [swap(two[:half], "dp", 1), swap(one[half:], "dp", 2)]
    return [own, one, two, jnp.concatenate(far, axis=0)]


def fetch_two(left, right, release_far, release_all):
    if lax.axis_size("dp") != 4:
        return fetch(left), fetch(right)
    left_one, left_two = swap(left, "dp", 1), swap(left, "dp", 2)
    right_one, right_two = swap(right, "dp", 1), swap(right, "dp", 2)
    left_far = swap(after(left_two, release_far), "dp", 1)
    right_far = swap(after(right_one, release_far), "dp", 2)
    left_far, right_far = after(left_far, *release_all), after(right_far, *release_all)
    return [left, left_one, left_two, left_far], [right, right_one, right_two, right_far]


def join(blocks):
    chunks = [jnp.concatenate(blocks, axis=0)]
    for bit in bits("ctx"):
        chunks = chunks + [swap(chunk, "ctx", bit) for chunk in chunks]
    return chunks


def scatter(chunks, release=()):
    for bit in reversed(bits("ctx")):
        half = len(chunks) // 2
        chunks = [
            (keep.astype(FULL) + swap(send, "ctx", bit).astype(FULL)).astype(LOW)
            for keep, send in zip(chunks[:half], chunks[half:])
        ]
    return scatter_dp(chunks[0], release), chunks[0]


def scatter_dp(chunk, release):
    n_dp = lax.axis_size("dp")
    parts = chunk.reshape(n_dp, -1, chunk.shape[-1])
    if n_dp == 4:
        half = parts.shape[2] // 2
        left, right = parts[:, :, :half], parts[:, :, half:]
        got = [swap(jnp.stack([left[1], left[3]]), "dp", 1), swap(right[2:], "dp", 2)]
        got_left, got_right = (g.astype(FULL) for g in after_all(got, *release))
        far_left = (left[2].astype(FULL) + got_left[1]).astype(LOW)
        far_right = (right[1].astype(FULL) + got_right[1]).astype(LOW)
        end_left = swap(far_left, "dp", 2).astype(FULL)
        end_right = swap(far_right, "dp", 1).astype(FULL)
        return jnp.concatenate(
            [
                left[0].astype(FULL) + got_left[0] + end_left,
                right[0].astype(FULL) + got_right[0] + end_right,
            ],
            axis=1,
        )
    for bit in reversed(bits("dp")):
        half = parts.shape[0] // 2
        parts = parts[:half].astype(FULL) + swap(parts[half:].astype(LOW), "dp", bit).astype(FULL)
    return parts[0].astype(FULL)


def line_scatter(part):
    return lax.psum_scatter(part, "tensor", scatter_dimension=0, tiled=True)


def line_gather(own):
    return lax.all_gather(own, "tensor", axis=0, tiled=True)


def tensor_total(term):
    return tensor_steps(term)[-2]


def tensor_first(term):
    low = term.astype(LOW)
    return low.astype(FULL) + swap(low, "tensor", 1).astype(FULL)


def tensor_rest(term):
    for bit in bits("tensor")[1:]:
        low = term.astype(LOW)
        term = low.astype(FULL) + swap(low, "tensor", bit).astype(FULL)
    return term


def tensor_steps(term):
    steps, sent = [], []
    for bit in bits("tensor"):
        low = term.astype(LOW)
        term = low.astype(FULL) + swap(low, "tensor", bit).astype(FULL)
        steps.append(term)
        sent.append(low)
    return steps + sent[:1]


def gather_few(row):
    return pick(gather_relative(row), relative_blocks()[1])


def gather_relative(row):
    for axis in ("dp", "ctx"):
        for bit in bits(axis):
            row = jnp.concatenate([row, swap(row, axis, bit)], axis=0)
    return row


def in_order(parts):
    total = parts[0]
    for part in parts[1:]:
        total = total + part
    return total


def spread(target, columns, place, rows, tile):
    target[pl.ds(place, rows, stride=tile), :] = columns


def columns_of(j):
    return slice(j * LANES, (j + 1) * LANES)


def edge_kernel(
    rows, groups, tile, unroll, flag, size_ref, value_ref, grad_ref, gate_ref, coef_ref, rate_ref,
    edge_ref, size_s, term_s,
):
    backward = flag[0] == 1

    @pl.when(pl.program_id(0) == 0)
    def _():
        edge_ref[...] = jnp.zeros_like(edge_ref)

    for j in range(tile):
        if j < groups:
            spread(size_s, size_ref[:, columns_of(j)], j, rows, tile)
        else:
            spread(size_s, jnp.zeros((rows, LANES), FULL), j, rows, tile)
            spread(term_s, jnp.zeros((rows, LANES), FULL), j, rows, tile)

    def loop(body):
        first = tuple(edge_ref[n] for n in range(N))
        last = lax.fori_loop(0, rows, body, first, unroll=unroll)
        for n in range(N):
            edge_ref[n] = last[n]

    @pl.when(jnp.logical_not(backward))
    def _():
        for j in range(groups):
            cut = columns_of(j)
            spread(term_s, size_ref[:, cut] * value_ref[:, cut].astype(FULL), j, rows, tile)

        def body(t, state):
            place = pl.ds(pl.multiple_of(t * tile, tile), tile)
            size, term = size_s[place, :], term_s[place, :]
            return tuple(
                jnp.exp2(size * rate_ref[n]) * state[n] + term * coef_ref[t, n]
                for n in range(N)
            )

        loop(body)

    @pl.when(backward)
    def _():
        for j in range(groups):
            cut = columns_of(j)
            gate = gate_ref[:, cut].astype(FULL)
            spread(term_s, grad_ref[:, cut] * gate * jax.nn.sigmoid(gate), j, rows, tile)

        def body(step, state):
            t = rows - 1 - step
            place = pl.ds(pl.multiple_of(t * tile, tile), tile)
            size, term = size_s[place, :], term_s[place, :]
            return tuple(
                jnp.exp2(size * rate_ref[n])
                * (state[n] + term * coef_ref[t, N + n])
                for n in range(N)
            )

        loop(body)


def forward_kernel(
    rows, groups, tile, part, unroll,
    size_ref, value_ref, grad_ref, gate_ref, coef_ref, rate_ref, start_ref, skip_ref,
    gated_ref, gate_grad_ref, before_ref, grad_c_ref, grad_skip_ref,
    size_s, input_s, grad_s, out_s, product_s, state_s, pick_s,
):
    @pl.when(pl.program_id(0) == 0)
    def _():
        state_s[...] = start_ref[...]
        set_picker(pick_s)
        grad_skip_ref[...] = jnp.zeros_like(grad_skip_ref)

    blank = jnp.zeros((rows, LANES), FULL)
    for j in range(tile):
        if j < groups:
            cut = columns_of(j)
            size = size_ref[:, cut]
            value = value_ref[:, cut].astype(FULL)
            gate = gate_ref[:, cut].astype(FULL)
            scan_grad = grad_ref[:, cut] * gate * jax.nn.sigmoid(gate)
            spread(size_s, size, j, rows, tile)
            spread(input_s, size * value, j, rows, tile)
            spread(grad_s, scan_grad, j, rows, tile)
            grad_skip_ref[:, cut] += jnp.sum(scan_grad * value, axis=0, keepdims=True)
        else:
            for target in (size_s, input_s, grad_s):
                spread(target, blank, j, rows, tile)
    for low in range(0, N, part):
        rate = [rate_ref[n] for n in range(low, low + part)]

        def body(t, state):
            state = list(state)
            place = pl.ds(pl.multiple_of(t * tile, tile), tile)
            size, term, grad = size_s[place, :], input_s[place, :], grad_s[place, :]
            out = None
            for k in range(part):
                n = low + k
                before_ref[t, n] = state[k]
                state[k] = (
                    jnp.exp2(size * rate[k]) * state[k] + term * coef_ref[t, n]
                )
                read = coef_ref[t, N + n] * state[k]
                out = read if out is None else out + read
                product_s[place, columns_of(n)] = state[k] * grad
            if low == 0:
                out_s[place, :] = out
            else:
                out_s[place, :] = out_s[place, :] + out
            return tuple(state)

        first = tuple(state_s[n] for n in range(low, low + part))
        last = lax.fori_loop(0, rows, body, first, unroll=unroll)
        for k in range(part):
            state_s[low + k] = last[k]
    for j in range(groups):
        cut = columns_of(j)
        scan_out = out_s[pl.ds(j, rows, stride=tile), :] + skip_ref[:, cut] * value_ref[
            :, cut
        ].astype(FULL)
        gate = gate_ref[:, cut].astype(FULL)
        sigma = jax.nn.sigmoid(gate)
        gated_ref[:, cut] = (scan_out * (gate * sigma)).astype(LOW)
        slope = sigma * (1.0 + gate * (1.0 - sigma))
        gate_grad_ref[:, cut] = (grad_ref[:, cut] * scan_out * slope).astype(LOW)
    sums = jnp.dot(product_s[...].astype(LOW), pick_s[...], preferred_element_type=FULL)
    grad_c_ref[...] = jnp.sum(sums.reshape(rows, tile, LANES), axis=1)


def backward_kernel(
    rows, groups, tile, part, unroll,
    size_ref, value_ref, grad_ref, gate_ref, coef_ref, rate_ref, tail_ref, skip_ref,
    before_ref,
    pre_low_ref, grad_value_ref, grad_b_ref, grad_rate_ref, grad_bias_ref,
    size_s, input_s, grad_s, along_s, rated_s, product_s, state_s, pick_s,
):
    @pl.when(pl.program_id(0) == 0)
    def _():
        state_s[...] = tail_ref[...]
        set_picker(pick_s)
        grad_rate_ref[...] = jnp.zeros_like(grad_rate_ref)
        grad_bias_ref[...] = jnp.zeros_like(grad_bias_ref)

    blank = jnp.zeros((rows, LANES), FULL)
    for j in range(tile):
        if j < groups:
            cut = columns_of(j)
            size = size_ref[:, cut]
            gate = gate_ref[:, cut].astype(FULL)
            spread(size_s, size, j, rows, tile)
            spread(input_s, size * value_ref[:, cut].astype(FULL), j, rows, tile)
            spread(grad_s, grad_ref[:, cut] * gate * jax.nn.sigmoid(gate), j, rows, tile)
        else:
            for target in (size_s, input_s, grad_s):
                spread(target, blank, j, rows, tile)
    for low in range(0, N, part):
        rate = [rate_ref[n] for n in range(low, low + part)]

        def body(step, carry):
            state, total = list(carry[0]), list(carry[1])
            t = rows - 1 - step
            place = pl.ds(pl.multiple_of(t * tile, tile), tile)
            size, term, grad = size_s[place, :], input_s[place, :], grad_s[place, :]
            along = rated = None
            for k in range(part):
                n = low + k
                adjoint = coef_ref[t, N + n] * grad + state[k]
                state[k] = jnp.exp2(size * rate[k]) * adjoint
                through = state[k] * before_ref[t, n]
                first = adjoint * coef_ref[t, n]
                second = through * rate[k]
                along = first if along is None else along + first
                rated = second if rated is None else rated + second
                total[k] = total[k] + through * size
                product_s[place, columns_of(n)] = adjoint * term
            if low == 0:
                along_s[place, :] = along
                rated_s[place, :] = rated
            else:
                along_s[place, :] = along_s[place, :] + along
                rated_s[place, :] = rated_s[place, :] + rated
            return tuple(state), tuple(total)

        place = range(low, low + part)
        first = (tuple(state_s[n] for n in place), tuple(grad_rate_ref[n] for n in place))
        state, total = lax.fori_loop(0, rows, body, first, unroll=unroll)
        for k in range(part):
            state_s[low + k] = state[k]
            grad_rate_ref[low + k] = total[k]
    for j in range(groups):
        cut = columns_of(j)
        size = size_ref[:, cut]
        along = along_s[pl.ds(j, rows, stride=tile), :]
        rated = rated_s[pl.ds(j, rows, stride=tile), :]
        grad_size = along * value_ref[:, cut].astype(FULL) + LOG_2 * rated
        grad_pre = grad_size * (jnp.tanh(0.5 * size) * (1.0 + jnp.exp(-size)))
        pre_low_ref[:, cut] = grad_pre.astype(LOW)
        grad_bias_ref[:, cut] += jnp.sum(grad_pre, axis=0, keepdims=True)
        scan_grad = grad_s[pl.ds(j, rows, stride=tile), :]
        grad_value_ref[:, cut] = along * size + skip_ref[:, cut] * scan_grad
    sums = jnp.dot(product_s[...].astype(LOW), pick_s[...], preferred_element_type=FULL)
    grad_b_ref[...] = jnp.sum(sums.reshape(rows, tile, LANES), axis=1)


def set_picker(pick_s):
    state = lax.broadcasted_iota(jnp.int32, pick_s.shape, 0) // LANES
    pick_s[...] = (state == lax.broadcasted_iota(jnp.int32, pick_s.shape, 1)).astype(LOW)


def tiles(channels):
    groups = channels // LANES
    return groups, 8 * pl.cdiv(groups, 8)


def tiled(table):
    groups, tile = tiles(table.shape[-1])
    table = table.reshape(table.shape[:-1] + (groups, LANES))
    pads = [(0, 0)] * (table.ndim - 2) + [(0, tile - groups), (0, 0)]
    return jnp.pad(table, pads)


def flat(table, channels):
    groups, _ = tiles(channels)
    return table[..., :groups, :].reshape(table.shape[:-2] + (channels,))


def cost(micro, length, ops, size):
    work = micro * length * N * 1024 * ops * 100
    return pl.CostEstimate(flops=work, bytes_accessed=size, transcendentals=0)


def limits():
    return pltpu.CompilerParams(vmem_limit_bytes=56 * 1024 * 1024)


def scan_edge(flag, size, value, grad, gate, coef, rate):
    length, channels = size.shape
    groups, tile = tiles(channels)
    rows = min(64, length)
    count = length // rows

    def place(i, f):
        return (jnp.where(f[0] == 0, i, count - 1 - i), 0)

    wide = pl.BlockSpec((rows, channels), place)
    cube = pl.BlockSpec((N, tile, LANES), lambda i, f: (0, 0, 0))
    return pl.pallas_call(
        functools.partial(edge_kernel, rows, groups, tile, 4),
        grid_spec=pltpu.PrefetchScalarGridSpec(
            num_scalar_prefetch=1,
            grid=(count,),
            in_specs=[wide] * 4
            + [pl.BlockSpec((rows, 2 * N), place, memory_space=pltpu.SMEM), cube],
            out_specs=cube,
            scratch_shapes=[pltpu.VMEM((rows * tile, LANES), FULL)] * 2,
        ),
        out_shape=jax.ShapeDtypeStruct((N, tile, LANES), FULL),
        compiler_params=limits(),
        cost_estimate=cost(1, length, 8, size.size * 12),
        name="scan_edge",
    )(flag, size, value, grad, gate, coef, rate)


def scan_forward(size, value, grad, gate, coef, rate, start, skip):
    length, channels = size.shape
    groups, tile = tiles(channels)
    rows = min(64, length)
    wide = pl.BlockSpec((rows, channels), lambda i: (i, 0))
    row = pl.BlockSpec((1, channels), lambda i: (0, 0))
    cube = pl.BlockSpec((N, tile, LANES), lambda i: (0, 0, 0))
    return pl.pallas_call(
        functools.partial(forward_kernel, rows, groups, tile, 8, 4),
        grid=(length // rows,),
        in_specs=[wide] * 4
        + [
            pl.BlockSpec((rows, 2 * N), lambda i: (i, 0), memory_space=pltpu.SMEM),
            cube,
            cube,
            row,
        ],
        out_specs=[
            wide,
            wide,
            pl.BlockSpec((rows, N, tile, LANES), lambda i: (i, 0, 0, 0)),
            pl.BlockSpec((rows, LANES), lambda i: (i, 0)),
            row,
        ],
        out_shape=[
            jax.ShapeDtypeStruct(size.shape, LOW),
            jax.ShapeDtypeStruct(size.shape, LOW),
            jax.ShapeDtypeStruct((length, N, tile, LANES), FULL),
            jax.ShapeDtypeStruct((length, LANES), FULL),
            jax.ShapeDtypeStruct((1, channels), FULL),
        ],
        scratch_shapes=[pltpu.VMEM((rows * tile, LANES), FULL)] * 4
        + [pltpu.VMEM((rows * tile, N * LANES), FULL), pltpu.VMEM((N, tile, LANES), FULL)]
        + [pltpu.VMEM((N * LANES, LANES), LOW)],
        compiler_params=limits(),
        cost_estimate=cost(1, length, 15, size.size * 80),
        name="scan_forward",
    )(size, value, grad, gate, coef, rate, start, skip)


def scan_backward(size, value, grad, gate, coef, rate, tail, skip, before):
    length, channels = size.shape
    groups, tile = tiles(channels)
    rows = min(64, length)
    last = length // rows - 1
    wide = pl.BlockSpec((rows, channels), lambda i: (last - i, 0))
    row = pl.BlockSpec((1, channels), lambda i: (0, 0))
    cube = pl.BlockSpec((N, tile, LANES), lambda i: (0, 0, 0))
    return pl.pallas_call(
        functools.partial(backward_kernel, rows, groups, tile, 8, 4),
        grid=(length // rows,),
        in_specs=[wide] * 4
        + [
            pl.BlockSpec((rows, 2 * N), lambda i: (last - i, 0), memory_space=pltpu.SMEM),
            cube,
            cube,
            row,
            pl.BlockSpec((rows, N, tile, LANES), lambda i: (last - i, 0, 0, 0)),
        ],
        out_specs=[wide, wide, pl.BlockSpec((rows, LANES), lambda i: (last - i, 0)), cube, row],
        out_shape=[
            jax.ShapeDtypeStruct(size.shape, LOW),
            jax.ShapeDtypeStruct(size.shape, FULL),
            jax.ShapeDtypeStruct((length, LANES), FULL),
            jax.ShapeDtypeStruct((N, tile, LANES), FULL),
            jax.ShapeDtypeStruct((1, channels), FULL),
        ],
        scratch_shapes=[pltpu.VMEM((rows * tile, LANES), FULL)] * 5
        + [pltpu.VMEM((rows * tile, N * LANES), FULL), pltpu.VMEM((N, tile, LANES), FULL)]
        + [pltpu.VMEM((N * LANES, LANES), LOW)],
        compiler_params=limits(),
        cost_estimate=cost(1, length, 20, size.size * 80),
        name="scan_backward",
    )(size, value, grad, gate, coef, rate, tail, skip, before)


def edges(size, value, grad, gate, coef, rate):
    count, place = lax.axis_size("ctx"), lax.axis_index("ctx")
    args = (size, value, grad, gate, coef, rate)
    if count == 2:
        edge = scan_edge(place.astype(jnp.int32)[None], *args)
        other = swap(edge, "ctx", 1)
        return jnp.where(place == 1, other, 0.0), jnp.where(place == 0, other, 0.0)
    last = scan_edge(jnp.zeros((1,), jnp.int32), *args)
    head = scan_edge(jnp.ones((1,), jnp.int32), *args)
    through = jnp.exp2(rate * tiled(jnp.sum(size, axis=0, keepdims=True)))
    lasts, heads, throughs = (lax.all_gather(a, "ctx") for a in (last, head, through))
    start = tail = jnp.zeros(last.shape, FULL)
    for i in range(count):
        start = jnp.where(i < place, throughs[i] * start + lasts[i], start)
        j = count - 1 - i
        tail = jnp.where(j > place, throughs[j] * tail + heads[j], tail)
    return start, tail


def block_of(index, width):
    return pl.ds(pl.multiple_of(index * width, width), width)


def normalize_kernel(width, chunks, order, x_ref, grad_ref, gain_ref, *outs):
    x = x_ref[...].astype(FULL)
    inverse = lax.rsqrt(jnp.mean(x * x, axis=1, keepdims=True) + norm_epsilon)
    columns = D // chunks
    for chunk in range(chunks):
        for low in range(0, columns, width):
            q = (chunk * columns + low) // width
            source = block_of(order[q], width)
            place = slice(low, low + width)
            value = x_ref[:, source].astype(FULL) * inverse * gain_ref[q : q + 1, :]
            outs[chunk][:, place] = value.astype(LOW)
            outs[chunks + chunk][:, place] = grad_ref[:, source]


def normalize(order, m, length, x, grad, gain, n_ctx):
    height, width = length, D // len(order)
    if width % LANES:
        x, grad = x[m * length : (m + 1) * length], grad[m * length : (m + 1) * length]
        full = x.astype(FULL)
        inverse = lax.rsqrt(jnp.mean(full * full, axis=1, keepdims=True) + norm_epsilon)

        def arrange(array):
            blocks = jnp.swapaxes(array.reshape(height, len(order), width), 0, 1)
            blocks = pick(blocks, order).reshape(n_ctx, -1, height, width)
            return list(jnp.swapaxes(blocks, 1, 2).reshape(n_ctx, height, D // n_ctx))

        gain = pick(gain, inverse_of(order))
        return arrange((full * inverse * gain.reshape(1, D)).astype(LOW)), arrange(grad)
    rows = min(128, height)
    wide = pl.BlockSpec((rows, D), lambda i, o: (m * (length // rows) + i, 0))
    out = pl.BlockSpec((rows, D // n_ctx), lambda i, o: (i, 0))
    shape = jax.ShapeDtypeStruct((height, D // n_ctx), LOW)
    outs = pl.pallas_call(
        functools.partial(normalize_kernel, width, n_ctx),
        grid_spec=pltpu.PrefetchScalarGridSpec(
            num_scalar_prefetch=1,
            grid=(height // rows,),
            in_specs=[wide, wide, pl.BlockSpec((len(order), width), lambda i, o: (0, 0))],
            out_specs=[out] * (2 * n_ctx),
        ),
        out_shape=[shape] * (2 * n_ctx),
        compiler_params=limits(),
        name="normalize",
    )(jnp.stack(order).astype(jnp.int32), x, grad, gain)
    return outs[:n_ctx], outs[n_ctx:]


def inverse_of(order):
    return relative_blocks()[1]


def unpermuted(chunks, inverse_order):
    rows, width = jnp.concatenate(chunks, axis=1), D // len(inverse_order)
    return jnp.concatenate(
        [lax.dynamic_slice_in_dim(rows, q * width, width, 1) for q in inverse_order], axis=1
    )


def own_block(block, share):
    return pl.BlockSpec((share, D), lambda i, o: (o[block], 0))


def whole_of(array):
    return pl.BlockSpec(array.shape, lambda i, o: (0,) * array.ndim)


def mix_kernel(width, per_chunk, order, x_ref, branch_ref, out_ref):
    for q in range(D // width):
        place = block_of(order[q], width)
        value = branch_ref[:, q * width : (q + 1) * width].astype(FULL)
        out_ref[:, place] = (x_ref[:, place].astype(FULL) + value).astype(LOW)


def mix(order, block, x, branch):
    width, share = D // len(order), branch.shape[0]
    if width % LANES:
        x = lax.dynamic_slice_in_dim(x, block * share, share, 0)
        return (x.astype(FULL) + unpermuted([branch.astype(FULL)], inverse_of(order))).astype(LOW)
    return pl.pallas_call(
        functools.partial(mix_kernel, width, 0),
        grid_spec=pltpu.PrefetchScalarGridSpec(
            num_scalar_prefetch=1,
            grid=(1,),
            in_specs=[own_block(len(order), share), whole_of(branch)],
            out_specs=whole_of(branch),
        ),
        out_shape=jax.ShapeDtypeStruct((share, D), LOW),
        compiler_params=limits(),
        name="mix",
    )(jnp.stack(order + [block]).astype(jnp.int32), x, branch)


def token_kernel(width, order, x_ref, grad_ref, gain_ref, normed_ref, out_ref, gain_out_ref, scaled_s):
    x = x_ref[...].astype(FULL)
    inverse = lax.rsqrt(jnp.mean(x * x, axis=1, keepdims=True) + norm_epsilon)
    total = jnp.zeros_like(inverse)
    for q in range(D // width):
        place = block_of(order[q], width)
        value = normed_ref[:, q * width : (q + 1) * width].astype(FULL)
        part = x_ref[:, place].astype(FULL)
        gain_out_ref[pl.ds(order[q], 1), :] = jnp.sum(
            value * part * inverse, axis=0, keepdims=True
        )
        scaled = value * gain_ref[q : q + 1, :]
        total = total + jnp.sum(part * scaled, axis=1, keepdims=True)
        scaled_s[:, place] = scaled
    slope = inverse * inverse * inverse * (total / D)
    out_ref[...] = (
        grad_ref[...].astype(FULL) + inverse * scaled_s[...] - x * slope
    ).astype(LOW)


def token_rows(order, block, x, grad, gain, normed):
    width, share = D // len(order), normed.shape[0]
    if width % LANES:
        x = lax.dynamic_slice_in_dim(x, block * share, share, 0).astype(FULL)
        grad = lax.dynamic_slice_in_dim(grad, block * share, share, 0).astype(FULL)
        value = unpermuted([normed.astype(FULL)], inverse_of(order))
        inverse = lax.rsqrt(jnp.mean(x * x, axis=1, keepdims=True) + norm_epsilon)
        part = jnp.sum(value * x * inverse, axis=0).reshape(len(order), width)
        scaled = value * pick(gain, inverse_of(order)).reshape(1, D)
        slope = inverse * inverse * inverse * jnp.mean(x * scaled, axis=1, keepdims=True)
        return (grad + inverse * scaled - x * slope).astype(LOW), part
    wide = own_block(len(order), share)
    return pl.pallas_call(
        functools.partial(token_kernel, width),
        grid_spec=pltpu.PrefetchScalarGridSpec(
            num_scalar_prefetch=1,
            grid=(1,),
            in_specs=[wide, wide, whole_of(gain), whole_of(normed)],
            out_specs=[whole_of(normed), whole_of(gain)],
            scratch_shapes=[pltpu.VMEM((share, D), FULL)],
        ),
        out_shape=[
            jax.ShapeDtypeStruct((share, D), LOW),
            jax.ShapeDtypeStruct((len(order), width), FULL),
        ],
        compiler_params=limits(),
        name="token_rows",
    )(jnp.stack(order + [block]).astype(jnp.int32), x, grad, gain, normed)


def update_kernel(owners, *refs):
    n = len(owners)
    grads, scales, cols_ref, table_ref, out_ref = refs[:n], refs[n : 2 * n], *refs[2 * n :]
    out_ref[...] = jnp.zeros_like(out_ref)

    def lanes(squares):
        total = jnp.sum(squares, axis=0, keepdims=True)
        cuts = [total[:, columns_of(j)] for j in range(total.shape[1] // LANES)]
        return in_order(cuts)

    for i, owner in enumerate(owners):
        update = grads[i][...] * scales[i][...] * cols_ref[i : i + 1, :]
        out_ref[owner : owner + 1, :] += lanes(update * update)
    out_ref[5:6, :] = lanes(table_ref[...] * table_ref[...])


def update_squares(grads, scales, cols, table):
    return pl.pallas_call(
        functools.partial(update_kernel, (1, 1, 2, 3, 4)),
        out_shape=jax.ShapeDtypeStruct((6, LANES), FULL),
        compiler_params=limits(),
        name="update_squares",
    )(*grads, *scales, cols, table)


def pick_kernel(order, blocks_ref, out_ref):
    for j in range(blocks_ref.shape[0]):
        out_ref[j] = blocks_ref[order[j]]


def pick_rows(blocks, order):
    return pl.pallas_call(
        pick_kernel,
        in_specs=[pl.BlockSpec(memory_space=pltpu.SMEM), pl.BlockSpec(memory_space=pltpu.VMEM)],
        out_specs=pl.BlockSpec(memory_space=pltpu.VMEM),
        out_shape=jax.ShapeDtypeStruct(blocks.shape, blocks.dtype),
        compiler_params=limits(),
        name="pick_rows",
    )(jnp.stack(order).astype(jnp.int32), blocks)


def fill_kernel(part_ref, *refs):
    refs[-1][...] = part_ref[...]


def fill(whole, count, m, gathered, parts=1, k=0):
    height, columns = gathered.shape[0] // parts, gathered.shape[1]
    rows = height // lax.axis_size("tensor") if parts > 1 else min(256, height)
    kept = [] if whole is None else [whole]
    return pl.pallas_call(
        fill_kernel,
        grid=(height // rows,),
        in_specs=[pl.BlockSpec((rows, columns), lambda i: (i * parts + k, 0))]
        + [pl.BlockSpec(memory_space=pl.ANY)] * len(kept),
        out_specs=pl.BlockSpec((None, rows, columns), lambda i: (m, i, 0)),
        out_shape=jax.ShapeDtypeStruct((count, height, columns), gathered.dtype),
        input_output_aliases={1: 0} if kept else {},
        compiler_params=limits(),
        name="fill",
    )(gathered, *kept)


def conv_kernel(
    value_grad_ref, proj_ref, xproj_ref, conv_in_ref, earlier_ref, table_ref,
    out_ref, last_ref, head_ref, sums_ref, padded_s, grad_s,
):
    length = conv_in_ref.shape[0]
    taps = [table_ref[k : k + 1, :] for k in range(K)]
    padded_s[pl.ds(0, 8), :] = earlier_ref[...].astype(FULL)
    padded_s[pl.ds(8, length), :] = conv_in_ref[...].astype(FULL)
    conv = table_ref[K : K + 1, :] + taps[0] * padded_s[pl.ds(9 - K, length), :]
    for k in range(1, K):
        conv = conv + taps[k] * padded_s[pl.ds(9 - K + k, length), :]
    sigma = jax.nn.sigmoid(conv)
    slope = sigma * (1.0 + conv * (1.0 - sigma))
    grad_values = value_grad_ref[...] + jnp.dot(
        proj_ref[...], xproj_ref[...], preferred_element_type=FULL
    )
    grad_conv = grad_values * slope
    grad_s[pl.ds(0, length), :] = grad_conv
    grad_s[pl.ds(length, 8), :] = jnp.zeros((8, grad_conv.shape[1]), FULL)
    for k in range(K):
        sums_ref[k : k + 1, :] = jnp.sum(
            grad_conv * padded_s[pl.ds(9 - K + k, length), :], axis=0, keepdims=True
        )
    sums_ref[K : K + 1, :] = jnp.sum(grad_conv, axis=0, keepdims=True)
    sums_ref[K + 1 :, :] = jnp.zeros((7 - K, grad_conv.shape[1]), FULL)
    total = taps[K - 1] * grad_conv
    for k in range(K - 1):
        total = total + taps[k] * grad_s[pl.ds(K - 1 - k, length), :]
    out_ref[...] = total.astype(LOW)
    last_ref[...] = total[length - 8 :]
    head_ref[...] = jnp.zeros_like(head_ref)
    for p in range(K - 1):
        row = taps[0] * grad_s[pl.ds(p, 1), :]
        for k in range(1, p + 1):
            row = row + taps[k] * grad_s[pl.ds(p - k, 1), :]
        head_ref[9 - K + p : 10 - K + p, :] = row


def conv_backward(value_grad, proj_grad, xproj_low, conv_in, earlier, table):
    length, channels = value_grad.shape
    width = min(256, channels)
    tall = pl.BlockSpec((length, width), lambda j: (0, j))
    short = pl.BlockSpec((8, width), lambda j: (0, j))
    few = jax.ShapeDtypeStruct((8, channels), FULL)
    return pl.pallas_call(
        conv_kernel,
        grid=(channels // width,),
        in_specs=[
            tall,
            pl.BlockSpec(proj_grad.shape, lambda j: (0, 0)),
            pl.BlockSpec((proj_grad.shape[1], width), lambda j: (0, j)),
            tall,
            short,
            pl.BlockSpec((8, width), lambda j: (0, j)),
        ],
        out_specs=[tall, short, short, short],
        out_shape=[jax.ShapeDtypeStruct((length, channels), LOW), few, few, few],
        scratch_shapes=[pltpu.VMEM((length + 8, width), FULL)] * 2,
        compiler_params=limits(),
        name="conv_backward",
    )(value_grad, proj_grad, xproj_low, conv_in, earlier, table)


def dot(a, b, dims, kind=FULL):
    return lax.dot_general(a, b, (dims, ((), ())), preferred_element_type=FULL).astype(kind)


def per_device(
    tokens,
    out_grad,
    norm_gain,
    in_weight,
    xproj_weight,
    step_weight,
    outproj_weight,
    channel_table,
    gain_second,
    in_rows,
    in_cols,
    xproj_rows,
    xproj_cols,
    step_rows,
    step_cols,
    out_rows,
    out_cols,
    table_second,
):
    micro = tokens.shape[0]
    length = tokens.shape[2]
    inner = in_weight.shape[2]
    n_tensor = lax.axis_size("tensor")
    n_owner = lax.axis_size("dp") * lax.axis_size("ctx")
    owned = in_weight.shape[0]
    order, inverse_order = relative_blocks()
    n_ctx = lax.axis_size("ctx")
    own_axes = ("ctx", "dp")
    me = lax.axis_index("tensor")

    n_x, n_s = xproj_weight.shape[0], step_weight.shape[0]
    every = range(micro)
    tokens_flat = tokens.reshape(micro * length, D)
    grad_flat = out_grad.reshape(micro * length, D)
    gain_rounded = after(norm_gain.astype(LOW), gain_second).astype(FULL)
    gain_row = jnp.stack([gain_rounded, gain_second])[None]
    for bit in bits("dp"):
        gain_row = jnp.concatenate([gain_row, swap(gain_row, "dp", bit)], axis=0)
    gain_low = gain_row
    for bit in bits("ctx"):
        gain_low = jnp.concatenate([gain_low, swap(gain_low, "ctx", bit)], axis=0)
    gain_low, second_low = gain_low[:, 0], gain_low[:, 1]
    normed, grad_rel = zip(
        *(normalize(order, m, length, tokens_flat, grad_flat, gain_low, n_ctx) for m in every)
    )
    normed, grad_rel = list(normed), list(grad_rel)
    in_own = in_weight.reshape(owned, 2 * inner).astype(LOW)
    first_own = [in_own[:, :inner], xproj_weight.astype(LOW), step_weight.astype(LOW)]
    pad_rows = -(owned + n_x + n_s) % 64
    if pad_rows:
        first_own.append(jnp.zeros((pad_rows, inner), LOW))
    blocks = fetch(after(jnp.concatenate(first_own, axis=0), gain_row), [n[0] for n in normed])
    conv_low = join([block[:owned] for block in blocks])
    small = jnp.concatenate(join([block[owned:] for block in blocks]), axis=0)
    small = pick_rows(small.reshape(n_owner, -1, inner), inverse_order)
    xproj_low = small[:, :n_x].reshape(n_owner * n_x, inner)
    step_low = small[:, n_x : n_x + n_s].reshape(n_owner * n_s, inner)
    gate_own = in_own[:, inner:]
    out_own = after(outproj_weight.astype(LOW), conv_low[-1])

    taps = channel_table[:K]
    conv_bias = channel_table[K]
    step_bias = channel_table[K + 1]
    skip = channel_table[K + 2][None]
    a_neg = -jnp.exp(channel_table[K + 3 :])
    rate = tiled(a_neg / LOG_2)

    def contract(parts, weights):
        total = dot(parts[0], weights[0], ((1,), (0,)))
        for part, weight in zip(parts[1:], weights[1:]):
            total = total + dot(part, weight, ((1,), (0,)))
        return total

    conv_in, earlier, values, part_proj, proj_steps = [], [], [], [], []
    for m in every:
        parts = normed[m] if m == 0 else after_all(normed[m], proj_steps[-1][-1])
        conv_in.append(contract(parts, conv_low).astype(LOW))
        earlier.append(shifted(conv_in[m][length - 8 :], "ctx", 1))
        padded = jnp.concatenate([earlier[m], conv_in[m]], axis=0).astype(FULL)
        conv = conv_bias + taps[0] * padded[9 - K : 9 - K + length]
        for k in range(1, K):
            conv = conv + taps[k] * padded[9 - K + k : 9 - K + k + length]
        values.append(jax.nn.silu(conv).astype(LOW))
        part_proj.append(dot(values[m], xproj_low, ((1,), (1,))))
        proj_steps.append(tensor_steps(part_proj[m]))
    gate_blocks, out_blocks = fetch_two(gate_own, out_own, conv_in[0], proj_steps[0][:1])
    gate_low, out_low = join(gate_blocks), join(out_blocks)
    weights = (in_weight, xproj_weight, step_weight, outproj_weight)
    all_weights = [norm_gain] + list(weights) + [channel_table]
    shares = jnp.array([1.0 / n_tensor, 1.0, 1.0, 1.0, 1.0, 1.0 / n_owner], FULL)
    gate_in, grad_gated, size, coef, rank_low, own_mixed, mixed = [], [], [], [], [], [], []
    gated, gate_grad, before, grad_c, grad_skip, tail, branch = [], [], [], [], [], [], []
    for m in every:
        proj = proj_steps[m][-2]
        rank_low.append(proj[:, :R].astype(LOW))
        coef.append(proj[:, R:])
        now_low, now_rel, now_normed = rank_low[m], grad_rel[m], normed[m]
        if m > 0:
            now_low = after(now_low, branch[-1])
            now_rel, now_normed = after_all(now_rel, branch[-1]), after_all(now_normed, branch[-1])
        pre = dot(now_low, step_low, ((1,), (0,))) + step_bias
        size.append(jax.nn.softplus(pre))
        gate_in.append(contract(now_normed, gate_low).astype(LOW))
        grad_gated.append(contract(now_rel, out_low))
        args = (size[m], values[m], grad_gated[m], gate_in[m], coef[m], rate)
        entering, leaving = edges(*args)
        tail.append(leaving)
        outs = scan_forward(*args, entering, skip)
        for held, out in zip((gated, gate_grad, before, grad_c, grad_skip), outs):
            held.append(out)
        branch.append(
            jnp.concatenate([dot(gated[m], w, ((1,), (1,)), LOW) for w in out_low], axis=1)
        )
        own_mixed.append(mix(order, m * n_tensor + me, tokens_flat, line_scatter(branch[m])))

    def over_micros(left, right):
        total = dot(left[0], right[0], ((0,), (0,)))
        for a, b in zip(left[1:], right[1:]):
            total = total + dot(a, b, ((0,), (0,)))
        return total

    def chunks_of(parts):
        return list(zip(*parts))

    backs, parts, first_of, gate_parts, part_out = [], [], [], [], []
    for m in every:
        leaving = after(tail[m], branch[-1], own_mixed[0])
        if m > 0:
            leaving = after(leaving, first_of[0], *part_out, *gate_parts[0], *own_mixed)
        pre_low, value_grad, grad_b, grad_rate, grad_bias = scan_backward(
            size[m], values[m], grad_gated[m], gate_in[m], coef[m], rate, leaving, skip, before[m]
        )
        backs.append((pre_low, value_grad, grad_rate, grad_bias))
        grad_rank = dot(pre_low, step_low, ((1,), (1,)))
        parts.append(jnp.concatenate([grad_rank, grad_b[:, :N], grad_c[m][:, :N]], axis=1))
        first_of.append(tensor_first(parts[m]))
        if m == 0:
            for side in chunks_of(grad_rel):
                part_out.append(over_micros(after_all(side, parts[0]), gated).astype(LOW))
            gate_grad_then = after(gate_grad[0], parts[0], *own_mixed)
            gate_parts.append([dot(gate_grad_then, g, ((1,), (1,))) for g in gate_low])
    mixed = [line_gather(own_mixed[0])]
    pre_lows = [back[0] for back in backs]
    conv_grads, proj_grads, gain_parts, tables, partial, tokens_out = [], [], [], [], [], []
    part_gate, totals = [], [tensor_rest(first_of[0])]
    for m in every:
        _, value_grad, grad_rate, grad_bias = backs[m]
        proj_grad = totals[m].astype(LOW)
        proj_grads.append(proj_grad)
        wait_for = [mixed[0], parts[-1]]
        if m > 0:
            started = [partial[0], first_of[m]]
            gate_grad_then = after(gate_grad[m], *started)
            gate_parts.append([dot(gate_grad_then, g, ((1,), (1,))) for g in gate_low])
            if m == micro - 1:
                for c, side in enumerate(chunks_of(normed)):
                    arrived = started + [totals[m]] if c else started
                    part_gate.append(over_micros(after_all(side, *arrived), gate_grad).astype(LOW))
            wait_for = wait_for + gate_parts[m] + part_gate
        conv_grad, last, head, sums = conv_backward(
            after(value_grad, *wait_for),
            proj_grad, xproj_low, conv_in[m], earlier[m], channel_table[:8],
        )
        last = last + shifted(head, "ctx", -1)
        conv_grad = lax.dynamic_update_slice(conv_grad, last.astype(LOW), (length - 8, 0))
        if m == 0:
            totals = totals + [tensor_rest(after(first, sums)) for first in first_of[1:]]
        conv_grads.append(conv_grad)
        partial.append(
            jnp.concatenate(
                [
                    (g + dot(conv_grad, c, ((1,), (1,)))).astype(LOW)
                    for g, c in zip(gate_parts[m], conv_low)
                ],
                axis=1,
            )
        )
        sent = after(partial[m], totals[-1])
        token, gain_part = token_rows(
            order, m * n_tensor + me, tokens_flat, grad_flat, gain_low, line_scatter(sent)
        )
        gain_parts.append(gain_part)
        tokens_out.append(token)
        rates = flat(grad_rate, inner) * a_neg
        tables.append(jnp.concatenate([sums[: K + 1], grad_bias, grad_skip[m], rates], axis=0))
    normed_then = [after_all(sides, partial[-1]) for sides in normed]
    part_conv = [over_micros(g, conv_grads).astype(LOW) for g in chunks_of(normed_then)]
    shard_conv, middle = scatter(part_conv)
    shard_out, _ = scatter(part_out, [middle])
    shard_gate, _ = scatter(part_gate, [middle])
    weight_sq = vector([jnp.sum(jnp.square(after(w, middle))) for w in all_weights]) * shares
    group = own_mixed[1:] + tokens_out[:-1]
    whole_mixed = fill(None, micro, 0, after(mixed[0], middle))
    token_grad = None
    if group:
        group_all, parts_all = line_gather(jnp.concatenate(group, axis=0)), len(group)
    for m in range(1, micro):
        whole_mixed = fill(whole_mixed, micro, m, group_all, parts_all, m - 1)
    for m in range(micro - 1):
        token_grad = fill(token_grad, micro, m, group_all, parts_all, micro - 1 + m)
    token_first = whole_mixed if token_grad is None else token_grad
    token_last = line_gather(tokens_out[-1])
    mixed = whole_mixed.reshape(tokens.shape)
    pre_lows = after_all(pre_lows, middle, tokens_out[0])
    proj_grads = after_all(proj_grads, middle, tokens_out[0])
    part_step = over_micros(rank_low, pre_lows)
    part_xproj = over_micros(proj_grads, values)
    part_small = jnp.concatenate(
        [part_xproj.reshape(n_owner, n_x, inner), part_step.reshape(n_owner, n_s, inner)], axis=1
    )
    pad_rows = -(n_x + n_s) % 16
    part_small = jnp.pad(part_small, ((0, 0), (0, pad_rows), (0, 0))).astype(LOW)
    shard_small, _ = scatter(list(pick_rows(part_small, order).reshape(n_ctx, -1, inner)))
    shard_xproj = shard_small[:n_x]
    shard_step = shard_small[n_x : n_x + n_s]
    grad_table = in_order(tables)

    shard_in = jnp.stack([shard_conv, shard_gate], axis=1)
    matrices = (shard_in, shard_xproj, shard_step, shard_out)
    old_rows = (in_rows, xproj_rows, step_rows, out_rows)
    old_cols = (in_cols, xproj_cols, step_cols, out_cols)
    width_cols = (2 * E, E, E, E)
    width_rows = (D, R + 2 * N, R, D)
    squares = [matrix * matrix + square_floor for matrix in matrices]
    row_parts = [jnp.sum(square.reshape(square.shape[0], -1), axis=1) for square in squares]
    col_parts = [jnp.sum(square, axis=0).reshape(-1, inner) for square in squares]
    row_sums = butterfly(
        jnp.concatenate(row_parts + [weight_sq, in_order(gain_parts).reshape(-1)]), ("tensor",)
    )
    heights = [part.shape[0] for part in row_parts]
    ends = np.cumsum([0] + heights)
    n_rows = int(ends[-1])
    per_row = np.repeat((1.0 - decay_rate) / np.array(width_cols), heights).astype(np.float32)
    row_all = decay_rate * jnp.concatenate(old_rows) + per_row * row_sums[:n_rows]
    row_news = [row_all[ends[i] : ends[i + 1]] for i in range(4)]
    segment = (np.arange(4)[:, None] == np.repeat(np.arange(4), heights)[None]).astype(np.float32)
    gain_sums = row_sums[n_rows + 6 :].reshape(-1, inner)
    n_gain = gain_sums.shape[0]
    summed = butterfly(jnp.concatenate(col_parts + [gain_sums, grad_table], axis=0), own_axes)
    gain_grad = summed[5 : 5 + n_gain].reshape(n_owner, owned)
    owner = lax.axis_index("dp") * n_ctx + lax.axis_index("ctx")
    shard_gain = lax.dynamic_index_in_dim(gain_grad, owner, 0, False)
    col_sums = [summed[0:2], summed[2], summed[3], summed[4]]
    table_grad = summed[5 + n_gain :]
    col_news = [
        decay_rate * old_cols[i] + (1.0 - decay_rate) * col_sums[i] / width_rows[i]
        for i in range(4)
    ]
    every_second = decay_rate * pick(second_low, inverse_order) + (
        1.0 - decay_rate
    ) * (gain_grad * gain_grad + square_floor)
    every_update = gain_grad * lax.rsqrt(every_second)
    new_gain_second = lax.dynamic_index_in_dim(every_second, owner, 0, False)
    gain_update = lax.dynamic_index_in_dim(every_update, owner, 0, False)
    new_table_second = decay_rate * table_second + (1.0 - decay_rate) * (
        table_grad * table_grad + square_floor
    )
    table_update = table_grad * lax.rsqrt(new_table_second)
    inverse_cols = lax.rsqrt(jnp.concatenate([col.reshape(-1, inner) for col in col_news], axis=0))
    inverse_rows = lax.rsqrt(row_all)
    scaled_sq = update_squares(
        [shard_conv, shard_gate, shard_xproj, shard_step, shard_out],
        [inverse_rows[ends[i] : ends[i + 1]][:, None] for i in (0, 0, 1, 2, 3)],
        inverse_cols,
        table_update,
    )
    sums = jnp.concatenate(
        [
            jnp.sum(scaled_sq, axis=1) * shares,
            jnp.sum(segment * row_all[None], axis=1) / n_tensor,
            row_sums[n_rows : n_rows + 6] / n_tensor,
        ]
    )
    sums = butterfly(after(sums, token_first), own_axes + ("tensor",))
    row_means = sums[6:10] / np.array(width_rows, np.float32)
    total_weight = sums[10:]
    gain_sq = jnp.sum(every_update * every_update)
    counts = jnp.array([D, 2 * D * E, (R + 2 * N) * E, R * E, D * E, (K + 3 + N) * E], FULL)
    ones = jnp.ones((1,), FULL)
    means = jnp.concatenate([ones, row_means, ones])
    total_update = jnp.where(jnp.arange(6) == 0, gain_sq, sums[:6] * means)
    update_rms = jnp.sqrt(total_update / counts)
    factor = jnp.maximum(1.0, update_rms / clip_limit)
    scale = jnp.sqrt(total_weight / counts)
    stride = step_rate * scale / factor * jnp.sqrt(means)
    new_weights = [norm_gain - stride[0] * gain_update]
    for i in range(4):
        shape = (-1,) + (1,) * (matrices[i].ndim - 1)
        second = inverse_rows[ends[i] : ends[i + 1]].reshape(shape) * lax.rsqrt(col_news[i])[None]
        new_weights.append(weights[i] - stride[i + 1] * matrices[i] * second)
    new_weights.append(channel_table - stride[5] * table_update)
    token_last = after(token_last, *new_weights)
    token_grad = fill(token_grad, micro, micro - 1, token_last).reshape(tokens.shape)
    return (
        mixed,
        token_grad,
        shard_gain,
        shard_in,
        shard_xproj,
        shard_step,
        shard_out,
        table_grad,
        new_weights[0],
        new_weights[1],
        new_weights[2],
        new_weights[3],
        new_weights[4],
        new_weights[5],
        new_gain_second,
        row_news[0],
        col_news[0],
        row_news[1],
        col_news[1],
        row_news[2],
        col_news[2],
        row_news[3],
        col_news[3],
        new_table_second,
        update_rms,
    )


def solution(mesh):
    rows = P(("dp", "ctx"))
    matrix = P(("dp", "ctx"), "tensor")
    cube = P(("dp", "ctx"), None, "tensor")
    table = P(None, "tensor")
    block = P(None, "dp", "ctx", None)
    cols = P("tensor")
    return jax.shard_map(
        per_device,
        mesh=mesh,
        in_specs=(block, block, rows, cube, matrix, matrix, matrix, table, rows)
        + (rows, table, rows, cols, rows, cols, rows, cols, table),
        out_specs=(block, block, rows, cube, matrix, matrix, matrix, table)
        + (rows, cube, matrix, matrix, matrix, table, rows)
        + (rows, table, rows, cols, rows, cols, rows, cols, table, P()),
        check_vma=False,
    )
```

```python
import functools
import math

import jax
import jax.numpy as jnp
import numpy as np
from jax import lax
from jax.experimental import pallas as pl
from jax.experimental.pallas import tpu as pltpu
from jax.sharding import PartitionSpec as P

D = 2048
E = 4096
N = 16
R = 128
K = 4
LANES = 128
LOG_2 = math.log(2.0)
LOW = jnp.bfloat16
FULL = jnp.float32

norm_epsilon = 1e-05
square_floor = 1e-30
decay_rate = 0.5
clip_limit = 0.5
step_rate = 1.0


def after(value, *others):
    return lax.optimization_barrier((value,) + others)[0]


def after_all(values, *others):
    return list(lax.optimization_barrier(tuple(values) + others)[: len(values)])


def vector(scalars):
    place = lax.iota(jnp.int32, len(scalars))
    return in_order([jnp.where(place == i, s, 0.0) for i, s in enumerate(scalars)])


def bits(axis):
    size = lax.axis_size(axis)
    return [1 << b for b in range(size.bit_length() - 1)]


def swap(block, axis, bit):
    return lax.ppermute(block, axis, [(i, i ^ bit) for i in range(lax.axis_size(axis))])


def shifted(block, axis, distance):
    devices = range(lax.axis_size(axis))
    route = [(i - distance, i) for i in devices if i - distance in devices]
    return lax.ppermute(block, axis, route)


def butterfly(value, axes):
    for axis in axes:
        for bit in bits(axis):
            value = value + swap(value, axis, bit)
    return value


def relative_blocks():
    n_dp, n_ctx = lax.axis_size("dp"), lax.axis_size("ctx")
    dp, ctx = lax.axis_index("dp"), lax.axis_index("ctx")
    return [
        (dp ^ (q % n_dp)) * n_ctx + (ctx ^ (q // n_dp)) for q in range(n_dp * n_ctx)
    ], [
        (ctx ^ (j % n_ctx)) * n_dp + (dp ^ (j // n_ctx)) for j in range(n_dp * n_ctx)
    ]


def pick(blocks, order):
    return jnp.stack([lax.dynamic_index_in_dim(blocks, q, 0, False) for q in order])


def fetch(own, release_far=()):
    if lax.axis_size("dp") != 4:
        blocks = [own]
        for bit in bits("dp"):
            blocks = blocks + [swap(block, "dp", bit) for block in blocks]
        return blocks
    half = own.shape[0] // 2
    one, two = after_all([swap(own, "dp", 1), swap(own, "dp", 2)], *release_far)
    far = [swap(two[:half], "dp", 1), swap(one[half:], "dp", 2)]
    return [own, one, two, jnp.concatenate(far, axis=0)]


def fetch_two(left, right, release_far, release_all):
    if lax.axis_size("dp") != 4:
        return fetch(left), fetch(right)
    left_one, left_two = swap(left, "dp", 1), swap(left, "dp", 2)
    right_one, right_two = swap(right, "dp", 1), swap(right, "dp", 2)
    left_far = swap(after(left_two, release_far), "dp", 1)
    right_far = swap(after(right_one, release_far), "dp", 2)
    left_far, right_far = after(left_far, *release_all), after(right_far, *release_all)
    return [left, left_one, left_two, left_far], [right, right_one, right_two, right_far]


def join(blocks):
    chunks = [jnp.concatenate(blocks, axis=0)]
    for bit in bits("ctx"):
        chunks = chunks + [swap(chunk, "ctx", bit) for chunk in chunks]
    return chunks


def scatter(chunks, release=()):
    for bit in reversed(bits("ctx")):
        half = len(chunks) // 2
        chunks = [
            (keep.astype(FULL) + swap(send, "ctx", bit).astype(FULL)).astype(LOW)
            for keep, send in zip(chunks[:half], chunks[half:])
        ]
    return scatter_dp(chunks[0], release), chunks[0]


def scatter_dp(chunk, release):
    n_dp = lax.axis_size("dp")
    parts = chunk.reshape(n_dp, -1, chunk.shape[-1])
    if n_dp == 4:
        half = parts.shape[2] // 2
        left, right = parts[:, :, :half], parts[:, :, half:]
        got = [swap(jnp.stack([left[1], left[3]]), "dp", 1), swap(right[2:], "dp", 2)]
        got_left, got_right = (g.astype(FULL) for g in after_all(got, *release))
        far_left = (left[2].astype(FULL) + got_left[1]).astype(LOW)
        far_right = (right[1].astype(FULL) + got_right[1]).astype(LOW)
        end_left = swap(far_left, "dp", 2).astype(FULL)
        end_right = swap(far_right, "dp", 1).astype(FULL)
        return jnp.concatenate(
            [
                left[0].astype(FULL) + got_left[0] + end_left,
                right[0].astype(FULL) + got_right[0] + end_right,
            ],
            axis=1,
        )
    for bit in reversed(bits("dp")):
        half = parts.shape[0] // 2
        parts = parts[:half].astype(FULL) + swap(parts[half:].astype(LOW), "dp", bit).astype(FULL)
    return parts[0].astype(FULL)


def line_scatter(part):
    return lax.psum_scatter(part, "tensor", scatter_dimension=0, tiled=True)


def line_gather(own):
    return lax.all_gather(own, "tensor", axis=0, tiled=True)


def tensor_total(term):
    return tensor_steps(term)[-2]


def tensor_first(term):
    low = term.astype(LOW)
    return low.astype(FULL) + swap(low, "tensor", 1).astype(FULL)


def tensor_rest(term):
    for bit in bits("tensor")[1:]:
        low = term.astype(LOW)
        term = low.astype(FULL) + swap(low, "tensor", bit).astype(FULL)
    return term


def tensor_steps(term):
    steps, sent = [], []
    for bit in bits("tensor"):
        low = term.astype(LOW)
        term = low.astype(FULL) + swap(low, "tensor", bit).astype(FULL)
        steps.append(term)
        sent.append(low)
    return steps + sent[:1]


def gather_few(row):
    return pick(gather_relative(row), relative_blocks()[1])


def gather_relative(row):
    for axis in ("dp", "ctx"):
        for bit in bits(axis):
            row = jnp.concatenate([row, swap(row, axis, bit)], axis=0)
    return row


def in_order(parts):
    total = parts[0]
    for part in parts[1:]:
        total = total + part
    return total


def spread(target, columns, place, rows, tile):
    target[pl.ds(place, rows, stride=tile), :] = columns


def columns_of(j):
    return slice(j * LANES, (j + 1) * LANES)


def edge_kernel(
    rows, groups, tile, unroll, flag, size_ref, value_ref, grad_ref, gate_ref, coef_ref, rate_ref,
    edge_ref, size_s, term_s,
):
    backward = flag[0] == 1

    @pl.when(pl.program_id(0) == 0)
    def _():
        edge_ref[...] = jnp.zeros_like(edge_ref)

    for j in range(tile):
        if j < groups:
            spread(size_s, size_ref[:, columns_of(j)], j, rows, tile)
        else:
            spread(size_s, jnp.zeros((rows, LANES), FULL), j, rows, tile)
            spread(term_s, jnp.zeros((rows, LANES), FULL), j, rows, tile)

    def loop(body):
        first = tuple(edge_ref[n] for n in range(N))
        last = lax.fori_loop(0, rows, body, first, unroll=unroll)
        for n in range(N):
            edge_ref[n] = last[n]

    @pl.when(jnp.logical_not(backward))
    def _():
        for j in range(groups):
            cut = columns_of(j)
            spread(term_s, size_ref[:, cut] * value_ref[:, cut].astype(FULL), j, rows, tile)

        def body(t, state):
            place = pl.ds(pl.multiple_of(t * tile, tile), tile)
            size, term = size_s[place, :], term_s[place, :]
            return tuple(
                jnp.exp2(size * rate_ref[n]) * state[n] + term * coef_ref[t, n]
                for n in range(N)
            )

        loop(body)

    @pl.when(backward)
    def _():
        for j in range(groups):
            cut = columns_of(j)
            gate = gate_ref[:, cut].astype(FULL)
            spread(term_s, grad_ref[:, cut] * gate * jax.nn.sigmoid(gate), j, rows, tile)

        def body(step, state):
            t = rows - 1 - step
            place = pl.ds(pl.multiple_of(t * tile, tile), tile)
            size, term = size_s[place, :], term_s[place, :]
            return tuple(
                jnp.exp2(size * rate_ref[n])
                * (state[n] + term * coef_ref[t, N + n])
                for n in range(N)
            )

        loop(body)


def forward_kernel(
    rows, groups, tile, part, unroll,
    size_ref, value_ref, grad_ref, gate_ref, coef_ref, rate_ref, start_ref, skip_ref,
    gated_ref, gate_grad_ref, before_ref, grad_c_ref, grad_skip_ref,
    size_s, input_s, grad_s, out_s, product_s, state_s, pick_s,
):
    @pl.when(pl.program_id(0) == 0)
    def _():
        state_s[...] = start_ref[...]
        set_picker(pick_s)
        grad_skip_ref[...] = jnp.zeros_like(grad_skip_ref)

    blank = jnp.zeros((rows, LANES), FULL)
    for j in range(tile):
        if j < groups:
            cut = columns_of(j)
            size = size_ref[:, cut]
            value = value_ref[:, cut].astype(FULL)
            gate = gate_ref[:, cut].astype(FULL)
            scan_grad = grad_ref[:, cut] * gate * jax.nn.sigmoid(gate)
            spread(size_s, size, j, rows, tile)
            spread(input_s, size * value, j, rows, tile)
            spread(grad_s, scan_grad, j, rows, tile)
            grad_skip_ref[:, cut] += jnp.sum(scan_grad * value, axis=0, keepdims=True)
        else:
            for target in (size_s, input_s, grad_s):
                spread(target, blank, j, rows, tile)
    for low in range(0, N, part):
        rate = [rate_ref[n] for n in range(low, low + part)]

        def body(t, state):
            state = list(state)
            place = pl.ds(pl.multiple_of(t * tile, tile), tile)
            size, term, grad = size_s[place, :], input_s[place, :], grad_s[place, :]
            out = None
            for k in range(part):
                n = low + k
                before_ref[t, n] = state[k]
                state[k] = (
                    jnp.exp2(size * rate[k]) * state[k] + term * coef_ref[t, n]
                )
                read = coef_ref[t, N + n] * state[k]
                out = read if out is None else out + read
                product_s[place, columns_of(n)] = state[k] * grad
            if low == 0:
                out_s[place, :] = out
            else:
                out_s[place, :] = out_s[place, :] + out
            return tuple(state)

        first = tuple(state_s[n] for n in range(low, low + part))
        last = lax.fori_loop(0, rows, body, first, unroll=unroll)
        for k in range(part):
            state_s[low + k] = last[k]
    for j in range(groups):
        cut = columns_of(j)
        scan_out = out_s[pl.ds(j, rows, stride=tile), :] + skip_ref[:, cut] * value_ref[
            :, cut
        ].astype(FULL)
        gate = gate_ref[:, cut].astype(FULL)
        sigma = jax.nn.sigmoid(gate)
        gated_ref[:, cut] = (scan_out * (gate * sigma)).astype(LOW)
        slope = sigma * (1.0 + gate * (1.0 - sigma))
        gate_grad_ref[:, cut] = (grad_ref[:, cut] * scan_out * slope).astype(LOW)
    sums = jnp.dot(product_s[...].astype(LOW), pick_s[...], preferred_element_type=FULL)
    grad_c_ref[...] = jnp.sum(sums.reshape(rows, tile, LANES), axis=1)


def backward_kernel(
    rows, groups, tile, part, unroll,
    size_ref, value_ref, grad_ref, gate_ref, coef_ref, rate_ref, tail_ref, skip_ref,
    before_ref,
    pre_low_ref, grad_value_ref, grad_b_ref, grad_rate_ref, grad_bias_ref,
    size_s, input_s, grad_s, along_s, rated_s, product_s, state_s, pick_s,
):
    @pl.when(pl.program_id(0) == 0)
    def _():
        state_s[...] = tail_ref[...]
        set_picker(pick_s)
        grad_rate_ref[...] = jnp.zeros_like(grad_rate_ref)
        grad_bias_ref[...] = jnp.zeros_like(grad_bias_ref)

    blank = jnp.zeros((rows, LANES), FULL)
    for j in range(tile):
        if j < groups:
            cut = columns_of(j)
            size = size_ref[:, cut]
            gate = gate_ref[:, cut].astype(FULL)
            spread(size_s, size, j, rows, tile)
            spread(input_s, size * value_ref[:, cut].astype(FULL), j, rows, tile)
            spread(grad_s, grad_ref[:, cut] * gate * jax.nn.sigmoid(gate), j, rows, tile)
        else:
            for target in (size_s, input_s, grad_s):
                spread(target, blank, j, rows, tile)
    for low in range(0, N, part):
        rate = [rate_ref[n] for n in range(low, low + part)]

        def body(step, carry):
            state, total = list(carry[0]), list(carry[1])
            t = rows - 1 - step
            place = pl.ds(pl.multiple_of(t * tile, tile), tile)
            size, term, grad = size_s[place, :], input_s[place, :], grad_s[place, :]
            along = rated = None
            for k in range(part):
                n = low + k
                adjoint = coef_ref[t, N + n] * grad + state[k]
                state[k] = jnp.exp2(size * rate[k]) * adjoint
                through = state[k] * before_ref[t, n]
                first = adjoint * coef_ref[t, n]
                second = through * rate[k]
                along = first if along is None else along + first
                rated = second if rated is None else rated + second
                total[k] = total[k] + through * size
                product_s[place, columns_of(n)] = adjoint * term
            if low == 0:
                along_s[place, :] = along
                rated_s[place, :] = rated
            else:
                along_s[place, :] = along_s[place, :] + along
                rated_s[place, :] = rated_s[place, :] + rated
            return tuple(state), tuple(total)

        place = range(low, low + part)
        first = (tuple(state_s[n] for n in place), tuple(grad_rate_ref[n] for n in place))
        state, total = lax.fori_loop(0, rows, body, first, unroll=unroll)
        for k in range(part):
            state_s[low + k] = state[k]
            grad_rate_ref[low + k] = total[k]
    for j in range(groups):
        cut = columns_of(j)
        size = size_ref[:, cut]
        along = along_s[pl.ds(j, rows, stride=tile), :]
        rated = rated_s[pl.ds(j, rows, stride=tile), :]
        grad_size = along * value_ref[:, cut].astype(FULL) + LOG_2 * rated
        grad_pre = grad_size * (jnp.tanh(0.5 * size) * (1.0 + jnp.exp(-size)))
        pre_low_ref[:, cut] = grad_pre.astype(LOW)
        grad_bias_ref[:, cut] += jnp.sum(grad_pre, axis=0, keepdims=True)
        scan_grad = grad_s[pl.ds(j, rows, stride=tile), :]
        grad_value_ref[:, cut] = along * size + skip_ref[:, cut] * scan_grad
    sums = jnp.dot(product_s[...].astype(LOW), pick_s[...], preferred_element_type=FULL)
    grad_b_ref[...] = jnp.sum(sums.reshape(rows, tile, LANES), axis=1)


def set_picker(pick_s):
    state = lax.broadcasted_iota(jnp.int32, pick_s.shape, 0) // LANES
    pick_s[...] = (state == lax.broadcasted_iota(jnp.int32, pick_s.shape, 1)).astype(LOW)


def tiles(channels):
    groups = channels // LANES
    return groups, 8 * pl.cdiv(groups, 8)


def tiled(table):
    groups, tile = tiles(table.shape[-1])
    table = table.reshape(table.shape[:-1] + (groups, LANES))
    pads = [(0, 0)] * (table.ndim - 2) + [(0, tile - groups), (0, 0)]
    return jnp.pad(table, pads)


def flat(table, channels):
    groups, _ = tiles(channels)
    return table[..., :groups, :].reshape(table.shape[:-2] + (channels,))


def cost(micro, length, ops, size):
    work = micro * length * N * 1024 * ops * 100
    return pl.CostEstimate(flops=work, bytes_accessed=size, transcendentals=0)


def limits():
    return pltpu.CompilerParams(vmem_limit_bytes=56 * 1024 * 1024)


def scan_edge(flag, size, value, grad, gate, coef, rate):
    length, channels = size.shape
    groups, tile = tiles(channels)
    rows = min(64, length)
    count = length // rows

    def place(i, f):
        return (jnp.where(f[0] == 0, i, count - 1 - i), 0)

    wide = pl.BlockSpec((rows, channels), place)
    cube = pl.BlockSpec((N, tile, LANES), lambda i, f: (0, 0, 0))
    return pl.pallas_call(
        functools.partial(edge_kernel, rows, groups, tile, 4),
        grid_spec=pltpu.PrefetchScalarGridSpec(
            num_scalar_prefetch=1,
            grid=(count,),
            in_specs=[wide] * 4
            + [pl.BlockSpec((rows, 2 * N), place, memory_space=pltpu.SMEM), cube],
            out_specs=cube,
            scratch_shapes=[pltpu.VMEM((rows * tile, LANES), FULL)] * 2,
        ),
        out_shape=jax.ShapeDtypeStruct((N, tile, LANES), FULL),
        compiler_params=limits(),
        cost_estimate=cost(1, length, 8, size.size * 12),
        name="scan_edge",
    )(flag, size, value, grad, gate, coef, rate)


def scan_forward(size, value, grad, gate, coef, rate, start, skip):
    length, channels = size.shape
    groups, tile = tiles(channels)
    rows = min(64, length)
    wide = pl.BlockSpec((rows, channels), lambda i: (i, 0))
    row = pl.BlockSpec((1, channels), lambda i: (0, 0))
    cube = pl.BlockSpec((N, tile, LANES), lambda i: (0, 0, 0))
    return pl.pallas_call(
        functools.partial(forward_kernel, rows, groups, tile, 8, 4),
        grid=(length // rows,),
        in_specs=[wide] * 4
        + [
            pl.BlockSpec((rows, 2 * N), lambda i: (i, 0), memory_space=pltpu.SMEM),
            cube,
            cube,
            row,
        ],
        out_specs=[
            wide,
            wide,
            pl.BlockSpec((rows, N, tile, LANES), lambda i: (i, 0, 0, 0)),
            pl.BlockSpec((rows, LANES), lambda i: (i, 0)),
            row,
        ],
        out_shape=[
            jax.ShapeDtypeStruct(size.shape, LOW),
            jax.ShapeDtypeStruct(size.shape, LOW),
            jax.ShapeDtypeStruct((length, N, tile, LANES), FULL),
            jax.ShapeDtypeStruct((length, LANES), FULL),
            jax.ShapeDtypeStruct((1, channels), FULL),
        ],
        scratch_shapes=[pltpu.VMEM((rows * tile, LANES), FULL)] * 4
        + [pltpu.VMEM((rows * tile, N * LANES), FULL), pltpu.VMEM((N, tile, LANES), FULL)]
        + [pltpu.VMEM((N * LANES, LANES), LOW)],
        compiler_params=limits(),
        cost_estimate=cost(1, length, 15, size.size * 80),
        name="scan_forward",
    )(size, value, grad, gate, coef, rate, start, skip)


def scan_backward(size, value, grad, gate, coef, rate, tail, skip, before):
    length, channels = size.shape
    groups, tile = tiles(channels)
    rows = min(64, length)
    last = length // rows - 1
    wide = pl.BlockSpec((rows, channels), lambda i: (last - i, 0))
    row = pl.BlockSpec((1, channels), lambda i: (0, 0))
    cube = pl.BlockSpec((N, tile, LANES), lambda i: (0, 0, 0))
    return pl.pallas_call(
        functools.partial(backward_kernel, rows, groups, tile, 8, 4),
        grid=(length // rows,),
        in_specs=[wide] * 4
        + [
            pl.BlockSpec((rows, 2 * N), lambda i: (last - i, 0), memory_space=pltpu.SMEM),
            cube,
            cube,
            row,
            pl.BlockSpec((rows, N, tile, LANES), lambda i: (last - i, 0, 0, 0)),
        ],
        out_specs=[wide, wide, pl.BlockSpec((rows, LANES), lambda i: (last - i, 0)), cube, row],
        out_shape=[
            jax.ShapeDtypeStruct(size.shape, LOW),
            jax.ShapeDtypeStruct(size.shape, FULL),
            jax.ShapeDtypeStruct((length, LANES), FULL),
            jax.ShapeDtypeStruct((N, tile, LANES), FULL),
            jax.ShapeDtypeStruct((1, channels), FULL),
        ],
        scratch_shapes=[pltpu.VMEM((rows * tile, LANES), FULL)] * 5
        + [pltpu.VMEM((rows * tile, N * LANES), FULL), pltpu.VMEM((N, tile, LANES), FULL)]
        + [pltpu.VMEM((N * LANES, LANES), LOW)],
        compiler_params=limits(),
        cost_estimate=cost(1, length, 20, size.size * 80),
        name="scan_backward",
    )(size, value, grad, gate, coef, rate, tail, skip, before)


def edges(size, value, grad, gate, coef, rate):
    count, place = lax.axis_size("ctx"), lax.axis_index("ctx")
    args = (size, value, grad, gate, coef, rate)
    if count == 2:
        edge = scan_edge(place.astype(jnp.int32)[None], *args)
        other = swap(edge, "ctx", 1)
        return jnp.where(place == 1, other, 0.0), jnp.where(place == 0, other, 0.0)
    last = scan_edge(jnp.zeros((1,), jnp.int32), *args)
    head = scan_edge(jnp.ones((1,), jnp.int32), *args)
    through = jnp.exp2(rate * tiled(jnp.sum(size, axis=0, keepdims=True)))
    lasts, heads, throughs = (lax.all_gather(a, "ctx") for a in (last, head, through))
    start = tail = jnp.zeros(last.shape, FULL)
    for i in range(count):
        start = jnp.where(i < place, throughs[i] * start + lasts[i], start)
        j = count - 1 - i
        tail = jnp.where(j > place, throughs[j] * tail + heads[j], tail)
    return start, tail


def block_of(index, width):
    return pl.ds(pl.multiple_of(index * width, width), width)


def normalize_kernel(width, chunks, order, x_ref, grad_ref, gain_ref, *outs):
    x = x_ref[...].astype(FULL)
    inverse = lax.rsqrt(jnp.mean(x * x, axis=1, keepdims=True) + norm_epsilon)
    columns = D // chunks
    for chunk in range(chunks):
        for low in range(0, columns, width):
            q = (chunk * columns + low) // width
            source = block_of(order[q], width)
            place = slice(low, low + width)
            value = x_ref[:, source].astype(FULL) * inverse * gain_ref[q : q + 1, :]
            outs[chunk][:, place] = value.astype(LOW)
            outs[chunks + chunk][:, place] = grad_ref[:, source]


def normalize(order, m, length, x, grad, gain, n_ctx):
    height, width = length, D // len(order)
    if width % LANES:
        x, grad = x[m * length : (m + 1) * length], grad[m * length : (m + 1) * length]
        full = x.astype(FULL)
        inverse = lax.rsqrt(jnp.mean(full * full, axis=1, keepdims=True) + norm_epsilon)

        def arrange(array):
            blocks = jnp.swapaxes(array.reshape(height, len(order), width), 0, 1)
            blocks = pick(blocks, order).reshape(n_ctx, -1, height, width)
            return list(jnp.swapaxes(blocks, 1, 2).reshape(n_ctx, height, D // n_ctx))

        gain = pick(gain, inverse_of(order))
        return arrange((full * inverse * gain.reshape(1, D)).astype(LOW)), arrange(grad)
    rows = min(128, height)
    wide = pl.BlockSpec((rows, D), lambda i, o: (m * (length // rows) + i, 0))
    out = pl.BlockSpec((rows, D // n_ctx), lambda i, o: (i, 0))
    shape = jax.ShapeDtypeStruct((height, D // n_ctx), LOW)
    outs = pl.pallas_call(
        functools.partial(normalize_kernel, width, n_ctx),
        grid_spec=pltpu.PrefetchScalarGridSpec(
            num_scalar_prefetch=1,
            grid=(height // rows,),
            in_specs=[wide, wide, pl.BlockSpec((len(order), width), lambda i, o: (0, 0))],
            out_specs=[out] * (2 * n_ctx),
        ),
        out_shape=[shape] * (2 * n_ctx),
        compiler_params=limits(),
        name="normalize",
    )(jnp.stack(order).astype(jnp.int32), x, grad, gain)
    return outs[:n_ctx], outs[n_ctx:]


def inverse_of(order):
    return relative_blocks()[1]


def unpermuted(chunks, inverse_order):
    rows, width = jnp.concatenate(chunks, axis=1), D // len(inverse_order)
    return jnp.concatenate(
        [lax.dynamic_slice_in_dim(rows, q * width, width, 1) for q in inverse_order], axis=1
    )


def own_block(block, share):
    return pl.BlockSpec((share, D), lambda i, o: (o[block], 0))


def whole_of(array):
    return pl.BlockSpec(array.shape, lambda i, o: (0,) * array.ndim)


def mix_kernel(width, per_chunk, order, x_ref, branch_ref, out_ref):
    for q in range(D // width):
        place = block_of(order[q], width)
        value = branch_ref[:, q * width : (q + 1) * width].astype(FULL)
        out_ref[:, place] = (x_ref[:, place].astype(FULL) + value).astype(LOW)


def mix(order, block, x, branch):
    width, share = D // len(order), branch.shape[0]
    if width % LANES:
        x = lax.dynamic_slice_in_dim(x, block * share, share, 0)
        return (x.astype(FULL) + unpermuted([branch.astype(FULL)], inverse_of(order))).astype(LOW)
    return pl.pallas_call(
        functools.partial(mix_kernel, width, 0),
        grid_spec=pltpu.PrefetchScalarGridSpec(
            num_scalar_prefetch=1,
            grid=(1,),
            in_specs=[own_block(len(order), share), whole_of(branch)],
            out_specs=whole_of(branch),
        ),
        out_shape=jax.ShapeDtypeStruct((share, D), LOW),
        compiler_params=limits(),
        name="mix",
    )(jnp.stack(order + [block]).astype(jnp.int32), x, branch)


def token_kernel(width, order, x_ref, grad_ref, gain_ref, normed_ref, out_ref, gain_out_ref, scaled_s):
    x = x_ref[...].astype(FULL)
    inverse = lax.rsqrt(jnp.mean(x * x, axis=1, keepdims=True) + norm_epsilon)
    total = jnp.zeros_like(inverse)
    for q in range(D // width):
        place = block_of(order[q], width)
        value = normed_ref[:, q * width : (q + 1) * width].astype(FULL)
        part = x_ref[:, place].astype(FULL)
        gain_out_ref[pl.ds(order[q], 1), :] = jnp.sum(
            value * part * inverse, axis=0, keepdims=True
        )
        scaled = value * gain_ref[q : q + 1, :]
        total = total + jnp.sum(part * scaled, axis=1, keepdims=True)
        scaled_s[:, place] = scaled
    slope = inverse * inverse * inverse * (total / D)
    out_ref[...] = (
        grad_ref[...].astype(FULL) + inverse * scaled_s[...] - x * slope
    ).astype(LOW)


def token_rows(order, block, x, grad, gain, normed):
    width, share = D // len(order), normed.shape[0]
    if width % LANES:
        x = lax.dynamic_slice_in_dim(x, block * share, share, 0).astype(FULL)
        grad = lax.dynamic_slice_in_dim(grad, block * share, share, 0).astype(FULL)
        value = unpermuted([normed.astype(FULL)], inverse_of(order))
        inverse = lax.rsqrt(jnp.mean(x * x, axis=1, keepdims=True) + norm_epsilon)
        part = jnp.sum(value * x * inverse, axis=0).reshape(len(order), width)
        scaled = value * pick(gain, inverse_of(order)).reshape(1, D)
        slope = inverse * inverse * inverse * jnp.mean(x * scaled, axis=1, keepdims=True)
        return (grad + inverse * scaled - x * slope).astype(LOW), part
    wide = own_block(len(order), share)
    return pl.pallas_call(
        functools.partial(token_kernel, width),
        grid_spec=pltpu.PrefetchScalarGridSpec(
            num_scalar_prefetch=1,
            grid=(1,),
            in_specs=[wide, wide, whole_of(gain), whole_of(normed)],
            out_specs=[whole_of(normed), whole_of(gain)],
            scratch_shapes=[pltpu.VMEM((share, D), FULL)],
        ),
        out_shape=[
            jax.ShapeDtypeStruct((share, D), LOW),
            jax.ShapeDtypeStruct((len(order), width), FULL),
        ],
        compiler_params=limits(),
        name="token_rows",
    )(jnp.stack(order + [block]).astype(jnp.int32), x, grad, gain, normed)


def update_kernel(owners, *refs):
    n = len(owners)
    grads, scales, cols_ref, table_ref, out_ref = refs[:n], refs[n : 2 * n], *refs[2 * n :]
    out_ref[...] = jnp.zeros_like(out_ref)

    def lanes(squares):
        total = jnp.sum(squares, axis=0, keepdims=True)
        cuts = [total[:, columns_of(j)] for j in range(total.shape[1] // LANES)]
        return in_order(cuts)

    for i, owner in enumerate(owners):
        update = grads[i][...] * scales[i][...] * cols_ref[i : i + 1, :]
        out_ref[owner : owner + 1, :] += lanes(update * update)
    out_ref[5:6, :] = lanes(table_ref[...] * table_ref[...])


def update_squares(grads, scales, cols, table):
    return pl.pallas_call(
        functools.partial(update_kernel, (1, 1, 2, 3, 4)),
        out_shape=jax.ShapeDtypeStruct((6, LANES), FULL),
        compiler_params=limits(),
        name="update_squares",
    )(*grads, *scales, cols, table)


def pick_kernel(order, blocks_ref, out_ref):
    for j in range(blocks_ref.shape[0]):
        out_ref[j] = blocks_ref[order[j]]


def pick_rows(blocks, order):
    return pl.pallas_call(
        pick_kernel,
        in_specs=[pl.BlockSpec(memory_space=pltpu.SMEM), pl.BlockSpec(memory_space=pltpu.VMEM)],
        out_specs=pl.BlockSpec(memory_space=pltpu.VMEM),
        out_shape=jax.ShapeDtypeStruct(blocks.shape, blocks.dtype),
        compiler_params=limits(),
        name="pick_rows",
    )(jnp.stack(order).astype(jnp.int32), blocks)


def fill_kernel(part_ref, *refs):
    refs[-1][...] = part_ref[...]


def fill(whole, count, m, gathered, parts=1, k=0):
    height, columns = gathered.shape[0] // parts, gathered.shape[1]
    rows = height // lax.axis_size("tensor") if parts > 1 else min(512, height)
    kept = [] if whole is None else [whole]
    return pl.pallas_call(
        fill_kernel,
        grid=(height // rows,),
        in_specs=[pl.BlockSpec((rows, columns), lambda i: (i * parts + k, 0))]
        + [pl.BlockSpec(memory_space=pl.ANY)] * len(kept),
        out_specs=pl.BlockSpec((None, rows, columns), lambda i: (m, i, 0)),
        out_shape=jax.ShapeDtypeStruct((count, height, columns), gathered.dtype),
        input_output_aliases={1: 0} if kept else {},
        compiler_params=limits(),
        name="fill",
    )(gathered, *kept)


def conv_kernel(
    value_grad_ref, proj_ref, xproj_ref, conv_in_ref, earlier_ref, table_ref,
    out_ref, last_ref, head_ref, sums_ref, padded_s, grad_s,
):
    length = conv_in_ref.shape[0]
    taps = [table_ref[k : k + 1, :] for k in range(K)]
    padded_s[pl.ds(0, 8), :] = earlier_ref[...].astype(FULL)
    padded_s[pl.ds(8, length), :] = conv_in_ref[...].astype(FULL)
    conv = table_ref[K : K + 1, :] + taps[0] * padded_s[pl.ds(9 - K, length), :]
    for k in range(1, K):
        conv = conv + taps[k] * padded_s[pl.ds(9 - K + k, length), :]
    sigma = jax.nn.sigmoid(conv)
    slope = sigma * (1.0 + conv * (1.0 - sigma))
    grad_values = value_grad_ref[...] + jnp.dot(
        proj_ref[...], xproj_ref[...], preferred_element_type=FULL
    )
    grad_conv = grad_values * slope
    grad_s[pl.ds(0, length), :] = grad_conv
    grad_s[pl.ds(length, 8), :] = jnp.zeros((8, grad_conv.shape[1]), FULL)
    for k in range(K):
        sums_ref[k : k + 1, :] = jnp.sum(
            grad_conv * padded_s[pl.ds(9 - K + k, length), :], axis=0, keepdims=True
        )
    sums_ref[K : K + 1, :] = jnp.sum(grad_conv, axis=0, keepdims=True)
    sums_ref[K + 1 :, :] = jnp.zeros((7 - K, grad_conv.shape[1]), FULL)
    total = taps[K - 1] * grad_conv
    for k in range(K - 1):
        total = total + taps[k] * grad_s[pl.ds(K - 1 - k, length), :]
    out_ref[...] = total.astype(LOW)
    last_ref[...] = total[length - 8 :]
    head_ref[...] = jnp.zeros_like(head_ref)
    for p in range(K - 1):
        row = taps[0] * grad_s[pl.ds(p, 1), :]
        for k in range(1, p + 1):
            row = row + taps[k] * grad_s[pl.ds(p - k, 1), :]
        head_ref[9 - K + p : 10 - K + p, :] = row


def conv_backward(value_grad, proj_grad, xproj_low, conv_in, earlier, table):
    length, channels = value_grad.shape
    width = min(256, channels)
    tall = pl.BlockSpec((length, width), lambda j: (0, j))
    short = pl.BlockSpec((8, width), lambda j: (0, j))
    few = jax.ShapeDtypeStruct((8, channels), FULL)
    return pl.pallas_call(
        conv_kernel,
        grid=(channels // width,),
        in_specs=[
            tall,
            pl.BlockSpec(proj_grad.shape, lambda j: (0, 0)),
            pl.BlockSpec((proj_grad.shape[1], width), lambda j: (0, j)),
            tall,
            short,
            pl.BlockSpec((8, width), lambda j: (0, j)),
        ],
        out_specs=[tall, short, short, short],
        out_shape=[jax.ShapeDtypeStruct((length, channels), LOW), few, few, few],
        scratch_shapes=[pltpu.VMEM((length + 8, width), FULL)] * 2,
        compiler_params=limits(),
        name="conv_backward",
    )(value_grad, proj_grad, xproj_low, conv_in, earlier, table)


def dot(a, b, dims, kind=FULL):
    return lax.dot_general(a, b, (dims, ((), ())), preferred_element_type=FULL).astype(kind)


def per_device(
    tokens,
    out_grad,
    norm_gain,
    in_weight,
    xproj_weight,
    step_weight,
    outproj_weight,
    channel_table,
    gain_second,
    in_rows,
    in_cols,
    xproj_rows,
    xproj_cols,
    step_rows,
    step_cols,
    out_rows,
    out_cols,
    table_second,
):
    micro = tokens.shape[0]
    length = tokens.shape[2]
    inner = in_weight.shape[2]
    n_tensor = lax.axis_size("tensor")
    n_owner = lax.axis_size("dp") * lax.axis_size("ctx")
    owned = in_weight.shape[0]
    order, inverse_order = relative_blocks()
    n_ctx = lax.axis_size("ctx")
    own_axes = ("ctx", "dp")
    me = lax.axis_index("tensor")

    n_x, n_s = xproj_weight.shape[0], step_weight.shape[0]
    every = range(micro)
    tokens_flat = tokens.reshape(micro * length, D)
    grad_flat = out_grad.reshape(micro * length, D)
    gain_rounded = after(norm_gain.astype(LOW), gain_second).astype(FULL)
    gain_row = jnp.stack([gain_rounded, gain_second])[None]
    for bit in bits("dp"):
        gain_row = jnp.concatenate([gain_row, swap(gain_row, "dp", bit)], axis=0)
    gain_low = gain_row
    for bit in bits("ctx"):
        gain_low = jnp.concatenate([gain_low, swap(gain_low, "ctx", bit)], axis=0)
    gain_low, second_low = gain_low[:, 0], gain_low[:, 1]
    normed, grad_rel = zip(
        *(normalize(order, m, length, tokens_flat, grad_flat, gain_low, n_ctx) for m in every)
    )
    normed, grad_rel = list(normed), list(grad_rel)
    in_own = in_weight.reshape(owned, 2 * inner).astype(LOW)
    first_own = [in_own[:, :inner], xproj_weight.astype(LOW), step_weight.astype(LOW)]
    pad_rows = -(owned + n_x + n_s) % 64
    if pad_rows:
        first_own.append(jnp.zeros((pad_rows, inner), LOW))
    blocks = fetch(after(jnp.concatenate(first_own, axis=0), gain_row), [normed[0][0]])
    conv_low = join([block[:owned] for block in blocks])
    small = jnp.concatenate(join([block[owned:] for block in blocks]), axis=0)
    small = pick_rows(small.reshape(n_owner, -1, inner), inverse_order)
    xproj_low = small[:, :n_x].reshape(n_owner * n_x, inner)
    step_low = small[:, n_x : n_x + n_s].reshape(n_owner * n_s, inner)
    gate_own = in_own[:, inner:]
    out_own = after(outproj_weight.astype(LOW), conv_low[-1])

    taps = channel_table[:K]
    conv_bias = channel_table[K]
    step_bias = channel_table[K + 1]
    skip = channel_table[K + 2][None]
    a_neg = -jnp.exp(channel_table[K + 3 :])
    rate = tiled(a_neg / LOG_2)

    def contract(parts, weights):
        total = dot(parts[0], weights[0], ((1,), (0,)))
        for part, weight in zip(parts[1:], weights[1:]):
            total = total + dot(part, weight, ((1,), (0,)))
        return total

    conv_in, earlier, values, part_proj, proj_steps = [], [], [], [], []
    for m in every:
        parts = normed[m] if m == 0 else after_all(normed[m], proj_steps[-1][-1])
        conv_in.append(contract(parts, conv_low).astype(LOW))
        earlier.append(shifted(conv_in[m][length - 8 :], "ctx", 1))
        padded = jnp.concatenate([earlier[m], conv_in[m]], axis=0).astype(FULL)
        conv = conv_bias + taps[0] * padded[9 - K : 9 - K + length]
        for k in range(1, K):
            conv = conv + taps[k] * padded[9 - K + k : 9 - K + k + length]
        values.append(jax.nn.silu(conv).astype(LOW))
        part_proj.append(dot(values[m], xproj_low, ((1,), (1,))))
        proj_steps.append(tensor_steps(part_proj[m]))
    gate_blocks, out_blocks = fetch_two(gate_own, out_own, conv_in[0], proj_steps[0][:1])
    gate_low, out_low = join(gate_blocks), join(out_blocks)
    weights = (in_weight, xproj_weight, step_weight, outproj_weight)
    all_weights = [norm_gain] + list(weights) + [channel_table]
    shares = jnp.array([1.0 / n_tensor, 1.0, 1.0, 1.0, 1.0, 1.0 / n_owner], FULL)
    gate_in, grad_gated, size, coef, rank_low, own_mixed, mixed = [], [], [], [], [], [], []
    gated, gate_grad, before, grad_c, grad_skip, tail, branch = [], [], [], [], [], [], []
    for m in every:
        proj = proj_steps[m][-2]
        rank_low.append(proj[:, :R].astype(LOW))
        coef.append(proj[:, R:])
        now_low, now_rel, now_normed = rank_low[m], grad_rel[m], normed[m]
        if m > 0:
            now_low = after(now_low, branch[-1])
            now_rel, now_normed = after_all(now_rel, branch[-1]), after_all(now_normed, branch[-1])
        pre = dot(now_low, step_low, ((1,), (0,))) + step_bias
        size.append(jax.nn.softplus(pre))
        gate_in.append(contract(now_normed, gate_low).astype(LOW))
        grad_gated.append(contract(now_rel, out_low))
        args = (size[m], values[m], grad_gated[m], gate_in[m], coef[m], rate)
        entering, leaving = edges(*args)
        tail.append(leaving)
        outs = scan_forward(*args, entering, skip)
        for held, out in zip((gated, gate_grad, before, grad_c, grad_skip), outs):
            held.append(out)
        branch.append(
            jnp.concatenate([dot(gated[m], w, ((1,), (1,)), LOW) for w in out_low], axis=1)
        )
        own_mixed.append(mix(order, m * n_tensor + me, tokens_flat, line_scatter(branch[m])))

    def over_micros(left, right):
        total = dot(left[0], right[0], ((0,), (0,)))
        for a, b in zip(left[1:], right[1:]):
            total = total + dot(a, b, ((0,), (0,)))
        return total

    def chunks_of(parts):
        return list(zip(*parts))

    backs, parts, first_of, gate_parts, part_out = [], [], [], [], []
    for m in every:
        leaving = after(tail[m], branch[-1], own_mixed[0])
        if m > 0:
            leaving = after(leaving, first_of[0], *part_out, *gate_parts[0], *own_mixed)
        pre_low, value_grad, grad_b, grad_rate, grad_bias = scan_backward(
            size[m], values[m], grad_gated[m], gate_in[m], coef[m], rate, leaving, skip, before[m]
        )
        backs.append((pre_low, value_grad, grad_rate, grad_bias))
        grad_rank = dot(pre_low, step_low, ((1,), (1,)))
        parts.append(jnp.concatenate([grad_rank, grad_b[:, :N], grad_c[m][:, :N]], axis=1))
        first_of.append(tensor_first(parts[m]))
        if m == 0:
            for side in chunks_of(grad_rel):
                part_out.append(over_micros(after_all(side, parts[0]), gated).astype(LOW))
            gate_grad_then = after(gate_grad[0], parts[0], *own_mixed)
            gate_parts.append([dot(gate_grad_then, g, ((1,), (1,))) for g in gate_low])
    mixed = [line_gather(own_mixed[0])]
    pre_lows = [back[0] for back in backs]
    conv_grads, proj_grads, gain_parts, tables, partial, tokens_out = [], [], [], [], [], []
    part_gate, totals = [], [tensor_rest(first_of[0])]
    for m in every:
        _, value_grad, grad_rate, grad_bias = backs[m]
        proj_grad = totals[m].astype(LOW)
        proj_grads.append(proj_grad)
        wait_for = [mixed[0], parts[-1]]
        if m > 0:
            started = [partial[0], first_of[m]]
            gate_grad_then = after(gate_grad[m], *started)
            gate_parts.append([dot(gate_grad_then, g, ((1,), (1,))) for g in gate_low])
            if m == micro - 1:
                for c, side in enumerate(chunks_of(normed)):
                    arrived = started + [totals[m]] if c else started
                    part_gate.append(over_micros(after_all(side, *arrived), gate_grad).astype(LOW))
            wait_for = wait_for + gate_parts[m] + part_gate
        conv_grad, last, head, sums = conv_backward(
            after(value_grad, *wait_for),
            proj_grad, xproj_low, conv_in[m], earlier[m], channel_table[:8],
        )
        last = last + shifted(head, "ctx", -1)
        conv_grad = lax.dynamic_update_slice(conv_grad, last.astype(LOW), (length - 8, 0))
        if m == 0:
            totals = totals + [tensor_rest(after(first, sums)) for first in first_of[1:]]
        conv_grads.append(conv_grad)
        partial.append(
            jnp.concatenate(
                [
                    (g + dot(conv_grad, c, ((1,), (1,)))).astype(LOW)
                    for g, c in zip(gate_parts[m], conv_low)
                ],
                axis=1,
            )
        )
        sent = after(partial[m], totals[-1])
        token, gain_part = token_rows(
            order, m * n_tensor + me, tokens_flat, grad_flat, gain_low, line_scatter(sent)
        )
        gain_parts.append(gain_part)
        tokens_out.append(token)
        rates = flat(grad_rate, inner) * a_neg
        tables.append(jnp.concatenate([sums[: K + 1], grad_bias, grad_skip[m], rates], axis=0))
    normed_then = [after_all(sides, partial[-1]) for sides in normed]
    part_conv = [over_micros(g, conv_grads).astype(LOW) for g in chunks_of(normed_then)]
    shard_conv, middle = scatter(part_conv)
    shard_out, _ = scatter(part_out, [middle])
    shard_gate, _ = scatter(part_gate, [middle])
    weight_sq = vector([jnp.sum(jnp.square(after(w, middle))) for w in all_weights]) * shares
    group = own_mixed[1:] + tokens_out[:-1]
    whole_mixed = fill(None, micro, 0, after(mixed[0], middle))
    token_grad = None
    if group:
        group_all, parts_all = line_gather(jnp.concatenate(group, axis=0)), len(group)
    for m in range(1, micro):
        whole_mixed = fill(whole_mixed, micro, m, group_all, parts_all, m - 1)
    for m in range(micro - 1):
        token_grad = fill(token_grad, micro, m, group_all, parts_all, micro - 1 + m)
    token_first = whole_mixed if token_grad is None else token_grad
    token_last = line_gather(tokens_out[-1])
    mixed = whole_mixed.reshape(tokens.shape)
    pre_lows = after_all(pre_lows, middle, tokens_out[0])
    proj_grads = after_all(proj_grads, middle, tokens_out[0])
    part_step = over_micros(rank_low, pre_lows)
    part_xproj = over_micros(proj_grads, values)
    part_small = jnp.concatenate(
        [part_xproj.reshape(n_owner, n_x, inner), part_step.reshape(n_owner, n_s, inner)], axis=1
    )
    pad_rows = -(n_x + n_s) % 16
    part_small = jnp.pad(part_small, ((0, 0), (0, pad_rows), (0, 0))).astype(LOW)
    shard_small, _ = scatter(list(pick_rows(part_small, order).reshape(n_ctx, -1, inner)))
    shard_xproj = shard_small[:n_x]
    shard_step = shard_small[n_x : n_x + n_s]
    grad_table = in_order(tables)

    shard_in = jnp.stack([shard_conv, shard_gate], axis=1)
    matrices = (shard_in, shard_xproj, shard_step, shard_out)
    old_rows = (in_rows, xproj_rows, step_rows, out_rows)
    old_cols = (in_cols, xproj_cols, step_cols, out_cols)
    width_cols = (2 * E, E, E, E)
    width_rows = (D, R + 2 * N, R, D)
    squares = [matrix * matrix + square_floor for matrix in matrices]
    row_parts = [jnp.sum(square.reshape(square.shape[0], -1), axis=1) for square in squares]
    col_parts = [jnp.sum(square, axis=0).reshape(-1, inner) for square in squares]
    row_sums = butterfly(
        jnp.concatenate(row_parts + [weight_sq, in_order(gain_parts).reshape(-1)]), ("tensor",)
    )
    heights = [part.shape[0] for part in row_parts]
    ends = np.cumsum([0] + heights)
    n_rows = int(ends[-1])
    per_row = np.repeat((1.0 - decay_rate) / np.array(width_cols), heights).astype(np.float32)
    row_all = decay_rate * jnp.concatenate(old_rows) + per_row * row_sums[:n_rows]
    row_news = [row_all[ends[i] : ends[i + 1]] for i in range(4)]
    segment = (np.arange(4)[:, None] == np.repeat(np.arange(4), heights)[None]).astype(np.float32)
    gain_sums = row_sums[n_rows + 6 :].reshape(-1, inner)
    n_gain = gain_sums.shape[0]
    summed = butterfly(jnp.concatenate(col_parts + [gain_sums, grad_table], axis=0), own_axes)
    gain_grad = summed[5 : 5 + n_gain].reshape(n_owner, owned)
    owner = lax.axis_index("dp") * n_ctx + lax.axis_index("ctx")
    shard_gain = lax.dynamic_index_in_dim(gain_grad, owner, 0, False)
    col_sums = [summed[0:2], summed[2], summed[3], summed[4]]
    table_grad = summed[5 + n_gain :]
    col_news = [
        decay_rate * old_cols[i] + (1.0 - decay_rate) * col_sums[i] / width_rows[i]
        for i in range(4)
    ]
    every_second = decay_rate * pick(second_low, inverse_order) + (
        1.0 - decay_rate
    ) * (gain_grad * gain_grad + square_floor)
    every_update = gain_grad * lax.rsqrt(every_second)
    new_gain_second = lax.dynamic_index_in_dim(every_second, owner, 0, False)
    gain_update = lax.dynamic_index_in_dim(every_update, owner, 0, False)
    new_table_second = decay_rate * table_second + (1.0 - decay_rate) * (
        table_grad * table_grad + square_floor
    )
    table_update = table_grad * lax.rsqrt(new_table_second)
    inverse_cols = lax.rsqrt(jnp.concatenate([col.reshape(-1, inner) for col in col_news], axis=0))
    inverse_rows = lax.rsqrt(row_all)
    scaled_sq = update_squares(
        [shard_conv, shard_gate, shard_xproj, shard_step, shard_out],
        [inverse_rows[ends[i] : ends[i + 1]][:, None] for i in (0, 0, 1, 2, 3)],
        inverse_cols,
        table_update,
    )
    sums = jnp.concatenate(
        [
            jnp.sum(scaled_sq, axis=1) * shares,
            jnp.sum(segment * row_all[None], axis=1) / n_tensor,
            row_sums[n_rows : n_rows + 6] / n_tensor,
        ]
    )
    sums = butterfly(after(sums, token_first), own_axes + ("tensor",))
    row_means = sums[6:10] / np.array(width_rows, np.float32)
    total_weight = sums[10:]
    gain_sq = jnp.sum(every_update * every_update)
    counts = jnp.array([D, 2 * D * E, (R + 2 * N) * E, R * E, D * E, (K + 3 + N) * E], FULL)
    ones = jnp.ones((1,), FULL)
    means = jnp.concatenate([ones, row_means, ones])
    total_update = jnp.where(jnp.arange(6) == 0, gain_sq, sums[:6] * means)
    update_rms = jnp.sqrt(total_update / counts)
    factor = jnp.maximum(1.0, update_rms / clip_limit)
    scale = jnp.sqrt(total_weight / counts)
    stride = step_rate * scale / factor * jnp.sqrt(means)
    new_weights = [norm_gain - stride[0] * gain_update]
    for i in range(4):
        shape = (-1,) + (1,) * (matrices[i].ndim - 1)
        second = inverse_rows[ends[i] : ends[i + 1]].reshape(shape) * lax.rsqrt(col_news[i])[None]
        new_weights.append(weights[i] - stride[i + 1] * matrices[i] * second)
    new_weights.append(channel_table - stride[5] * table_update)
    token_last = after(token_last, *new_weights)
    token_grad = fill(token_grad, micro, micro - 1, token_last).reshape(tokens.shape)
    return (
        mixed,
        token_grad,
        shard_gain,
        shard_in,
        shard_xproj,
        shard_step,
        shard_out,
        table_grad,
        new_weights[0],
        new_weights[1],
        new_weights[2],
        new_weights[3],
        new_weights[4],
        new_weights[5],
        new_gain_second,
        row_news[0],
        col_news[0],
        row_news[1],
        col_news[1],
        row_news[2],
        col_news[2],
        row_news[3],
        col_news[3],
        new_table_second,
        update_rms,
    )


def solution(mesh):
    rows = P(("dp", "ctx"))
    matrix = P(("dp", "ctx"), "tensor")
    cube = P(("dp", "ctx"), None, "tensor")
    table = P(None, "tensor")
    block = P(None, "dp", "ctx", None)
    cols = P("tensor")
    return jax.shard_map(
        per_device,
        mesh=mesh,
        in_specs=(block, block, rows, cube, matrix, matrix, matrix, table, rows)
        + (rows, table, rows, cols, rows, cols, rows, cols, table),
        out_specs=(block, block, rows, cube, matrix, matrix, matrix, table)
        + (rows, cube, matrix, matrix, matrix, table, rows)
        + (rows, table, rows, cols, rows, cols, rows, cols, table, P()),
        check_vma=False,
    )
```
